128 devices in a mesh: seq: 64 (over z, y, x_lo, core), batch: 2 (over x_hi).
Axes of the slice: x: 4 (x_hi: 2, x_lo: 2; x = x_hi * 2 + x_lo), y: 4, z: 4, core: 2. Of those that a mesh axis runs over, the one named last changes fastest.
Arguments:
- inputs: bfloat16 [4, 4096, 1536], P('batch', 'seq'), may hold values from -36 to 36
- conv_weight: bfloat16 [1536, 2304], P('seq'), may hold values from -0.09375 to 0.09375
- mix_weight: bfloat16 [768, 1536], P('seq'), may hold values from -0.21875 to 0.21875
- first_gain: float32 [1536], replicated, may hold values from 0.1 to 1.9
- first_bias: float32 [1536], replicated, may hold values from -3 to 3
- second_gain: float32 [768], replicated, may hold values from 0.1 to 1.9
- second_bias: float32 [768], replicated, may hold values from -3 to 3
- norm_gain: float32 [1536], replicated, may hold values from 0.1 to 1.9
- query_weight: bfloat16 [1536, 512], replicated, may hold values from -2.5 to 2.5
- key_weight: bfloat16 [1536, 512], replicated, may hold values from -2.5 to 2.5
- value_weight: bfloat16 [1536, 1536], replicated, may hold values from -0.4375 to 0.4375
- out_weight: bfloat16 [1536, 1536], replicated, may hold values from -0.15625 to 0.15625
- cotangent: bfloat16 [4, 4096, 1536], P('batch', 'seq'), may hold values from -12 to 12
Outputs:
- encoded: bfloat16 [4, 4096, 1536], P('batch', 'seq')
- grad_inputs: bfloat16 [4, 4096, 1536], P('batch', 'seq')
- grad_first_gain: float32 [1536], replicated
- grad_first_bias: float32 [1536], replicated
- grad_second_gain: float32 [768], replicated
- grad_second_bias: float32 [768], replicated
- grad_norm_gain: float32 [1536], replicated
The draws below stay inside these ranges and needn't reach their ends.
All inputs are finite; a program needn't handle non-finite values.
Results may differ from the reference program's by a relative error of at most 0.04.
Values may be sent and summed in bfloat16 or wider, within the bound.
A program may use at most 192 MiB of HBM per device.

```python
import math
import jax
import jax.numpy as jnp
from jax import lax

CHANNEL_COUNT = 1536
INNER_CHANNELS = 768
H = 8
KD = 64
VD = 192
DILATION_STEP = 16
WINDOW_BINS = 4096
WINDOWS = 4
QB = 8
QR = 8
N_SEQ = 64


def shared_common(key):
    return jnp.clip(jax.random.normal(key, (CHANNEL_COUNT, H * KD), jnp.float32), -4.0, 4.0)


def window_sign():
    return jnp.where(jnp.arange(WINDOWS) < WINDOWS // 2, 1.0, -1.0).astype(jnp.float32)[:, None, None]


def draw_query_weight(key, part):
    common = shared_common(key)
    key = jax.random.fold_in(key, 17)
    own_draw = jnp.clip(jax.random.normal(key, (CHANNEL_COUNT, H * KD), jnp.float32), -4.0, 4.0)
    blended = 0.6 * common + 0.8 * own_draw
    return (blended * CHANNEL_COUNT ** (-0.5)).astype(jnp.bfloat16)


def draw_key_weight(key, part):
    common = shared_common(key)
    blended = common
    return (blended * CHANNEL_COUNT ** (-0.5)).astype(jnp.bfloat16)


def draw_inputs(key, part):
    key = jax.random.fold_in(key, 11)
    noise_key = jax.random.fold_in(key, 0)
    row_key = jax.random.fold_in(key, 1)
    column_key = jax.random.fold_in(key, 2)
    half_key = jax.random.fold_in(key, 4)
    spread_key = jax.random.fold_in(key, 5)
    position = jnp.arange(WINDOW_BINS, dtype=jnp.float32) / (WINDOW_BINS - 1)
    rising = (1.0 + 2.0 * position)[None, :, None]
    row_factor = jnp.exp(jax.random.uniform(row_key, (WINDOWS, WINDOW_BINS, 1), jnp.float32, 0.0, math.log(2.0)))
    column_factor = jnp.exp(jax.random.uniform(column_key, (1, 1, CHANNEL_COUNT), jnp.float32, math.log(0.3), math.log(3.0)))
    sign = window_sign()
    half_offset = 0.8 * column_factor * jax.random.uniform(half_key, (1, 1, CHANNEL_COUNT), jnp.float32, -1.0, 1.0) * sign
    half_spread = jnp.exp(0.3 * jax.random.uniform(spread_key, (1, 1, CHANNEL_COUNT), jnp.float32, -1.0, 1.0) * sign)
    noise_draw = jnp.clip(jax.random.normal(noise_key, (WINDOWS, WINDOW_BINS, CHANNEL_COUNT), jnp.float32), -4.0, 4.0)
    return (0.33 * noise_draw * rising * row_factor * column_factor * half_spread + half_offset).astype(jnp.bfloat16)


def draw_cotangent(key, part):
    key = jax.random.fold_in(key, 13)
    noise_key = jax.random.fold_in(key, 0)
    row_key = jax.random.fold_in(key, 1)
    half_key = jax.random.fold_in(key, 3)
    position = jnp.arange(WINDOW_BINS, dtype=jnp.float32) / (WINDOW_BINS - 1)
    rising = (1.0 + 2.0 * position)[None, :, None]
    row_factor = jnp.exp(jax.random.uniform(row_key, (WINDOWS, WINDOW_BINS, 1), jnp.float32, 0.0, math.log(2.0)))
    half_offset = 0.4 * jax.random.uniform(half_key, (1, 1, CHANNEL_COUNT), jnp.float32, -1.0, 1.0) * window_sign()
    noise_draw = jnp.clip(jax.random.normal(noise_key, (WINDOWS, WINDOW_BINS, CHANNEL_COUNT), jnp.float32), -4.0, 4.0)
    return (0.42 * noise_draw * rising * row_factor + half_offset).astype(jnp.bfloat16)


def steps_of(own_key, extent, pieces, least, largest):
    def one(dim, parts):
        heights = jax.random.uniform(jax.random.fold_in(jax.random.fold_in(own_key, 6), dim), (parts,), jnp.float32, least / len(pieces), largest / len(pieces))
        return jnp.repeat(jnp.exp(heights), extent[dim] // parts).reshape((-1,) + (1,) * (len(extent) - dim - 1))

    level = one(*pieces[0])
    for cut in pieces[1:]:
        level = level * one(*cut)
    return level


def bell_draw(rng, shape, deviation, reach, shards=(), kind=jnp.bfloat16):
    array = jax.random.normal(rng, shape, jnp.float32) * deviation
    if len(shards) > 0:
        array = steps_of(rng, shape, shards, -0.22, 0.18) * array
    return jnp.clip(array, min=-reach, max=reach).astype(kind)


def setup_inputs(seed: int = 0) -> dict:
    splits = jax.random.split(jax.random.key(seed), 14)
    return {
        "inputs": draw_inputs(jax.random.fold_in(splits[13], 71), 0),
        "conv_weight": bell_draw(splits[1], (CHANNEL_COUNT, 3 * INNER_CHANNELS), (3 * CHANNEL_COUNT) ** -0.5, 0.09375, ((0, 64),)),
        "mix_weight": bell_draw(splits[2], (INNER_CHANNELS, CHANNEL_COUNT), INNER_CHANNELS ** -0.5, 0.21875, ((0, 64),)),
        "first_gain": jnp.clip(1.0 + 0.18 * jax.random.normal(splits[3], (CHANNEL_COUNT,), jnp.float32), 0.1, 1.9),
        "first_bias": bell_draw(splits[4], (CHANNEL_COUNT,), 0.5, 3.0, (), jnp.float32),
        "second_gain": jnp.clip(1.0 + 0.18 * jax.random.normal(splits[5], (INNER_CHANNELS,), jnp.float32), 0.1, 1.9),
        "second_bias": bell_draw(splits[6], (INNER_CHANNELS,), 0.5, 3.0, (), jnp.float32),
        "norm_gain": jnp.clip(1.0 + 0.18 * jax.random.normal(splits[7], (CHANNEL_COUNT,), jnp.float32), 0.1, 1.9),
        "query_weight": draw_query_weight(jax.random.fold_in(splits[13], 71), 0),
        "key_weight": draw_key_weight(jax.random.fold_in(splits[13], 71), 0),
        "value_weight": bell_draw(splits[10], (CHANNEL_COUNT, H * VD), (CHANNEL_COUNT // 8) ** -0.5, 0.4375),
        "out_weight": bell_draw(splits[11], (H * VD, CHANNEL_COUNT), (H * VD) ** -0.5, 0.15625),
        "cotangent": draw_cotangent(jax.random.fold_in(splits[13], 71), 0),
    }


EPS = 1e-05
GELU_C = 0.7978845608028654

def gelu_value(values):
    cubic = GELU_C * (values + 0.044715 * values * values * values)
    return 0.5 * values * (1.0 + jnp.tanh(cubic))

def gelu_slope(values):
    tangent = jnp.tanh(GELU_C * (values + 0.044715 * values * values * values))
    return 0.5 * (1.0 + tangent) + 0.5 * values * (1.0 - tangent * tangent) * GELU_C * (1.0 + 3.0 * 0.044715 * values * values)

def rounded(values):
    return lax.optimization_barrier(values.astype(jnp.bfloat16)).astype(jnp.float32)

def attend(items):
    queries, keys_head, values_head, grad_head = items
    key_scale = KD ** (-0.5)
    scores = jnp.dot(queries, keys_head.T, preferred_element_type=jnp.float32) * key_scale
    prob_rows = jax.nn.softmax(scores, axis=-1)
    prob_low = prob_rows.astype(jnp.bfloat16)
    attended = jnp.dot(prob_low, values_head, preferred_element_type=jnp.float32).astype(jnp.bfloat16)
    grad_probs = jnp.dot(grad_head, values_head.T, preferred_element_type=jnp.float32)
    center = lax.optimization_barrier(jnp.sum(prob_rows * grad_probs, axis=-1, keepdims=True))
    grad_scores = (prob_rows * (grad_probs - center) * key_scale).astype(jnp.bfloat16)
    grad_query = jnp.dot(grad_scores, keys_head, preferred_element_type=jnp.float32).astype(jnp.bfloat16)
    score_blocks = grad_scores.astype(jnp.float32).reshape(N_SEQ, QB, QR, WINDOW_BINS)
    query_blocks = queries.astype(jnp.float32).reshape(N_SEQ, QB, QR, KD)
    key_parts = jnp.einsum('sjrk,sjre->jke', score_blocks, query_blocks)
    grad_key = lax.optimization_barrier(jnp.sum(rounded(key_parts), axis=0)).astype(jnp.bfloat16)
    prob_blocks = prob_low.astype(jnp.float32).reshape(N_SEQ, QB, QR, WINDOW_BINS)
    out_blocks = grad_head.astype(jnp.float32).reshape(N_SEQ, QB, QR, VD)
    value_parts = jnp.einsum('sjrk,sjre->jke', prob_blocks, out_blocks)
    grad_value = lax.optimization_barrier(jnp.sum(rounded(value_parts), axis=0)).astype(jnp.bfloat16)
    return (attended, grad_query, grad_key, grad_value)

def to_heads(flat_rows, head_depth):
    return flat_rows.reshape(WINDOWS, WINDOW_BINS, H, head_depth).transpose(0, 2, 1, 3).reshape(WINDOWS * H, WINDOW_BINS, head_depth)

def from_heads(head_rows, head_depth):
    return head_rows.reshape(WINDOWS, H, WINDOW_BINS, head_depth).transpose(0, 2, 1, 3).reshape(WINDOWS * WINDOW_BINS, H * head_depth)

def reference(inputs, conv_weight, mix_weight, first_gain, first_bias, second_gain, second_bias, norm_gain, query_weight, key_weight, value_weight, out_weight, cotangent):
    total_rows = WINDOWS * WINDOW_BINS
    inputs_flat = inputs.astype(jnp.float32).reshape(total_rows, CHANNEL_COUNT)
    mean_one = lax.optimization_barrier(jnp.sum(inputs_flat, axis=0)) / total_rows
    scale_one = lax.rsqrt(lax.optimization_barrier(jnp.sum(inputs_flat * inputs_flat, axis=0)) / total_rows - mean_one * mean_one + EPS)
    hat_one = (inputs_flat - mean_one) * scale_one
    pre_one = hat_one * first_gain + first_bias
    first_activation = gelu_value(pre_one).astype(jnp.bfloat16).reshape(WINDOWS, WINDOW_BINS, CHANNEL_COUNT)
    padded_input = jnp.pad(first_activation, ((0, 0), (DILATION_STEP, DILATION_STEP), (0, 0)))
    hidden = jnp.zeros((total_rows, INNER_CHANNELS), jnp.float32)
    for kernel_tap_index in range(3):
        shifted_input = padded_input[:, kernel_tap_index * DILATION_STEP:kernel_tap_index * DILATION_STEP + WINDOW_BINS].reshape(total_rows, CHANNEL_COUNT)
        hidden = hidden + jnp.dot(shifted_input, conv_weight[:, kernel_tap_index * INNER_CHANNELS:(kernel_tap_index + 1) * INNER_CHANNELS], preferred_element_type=jnp.float32)
    mean_two = lax.optimization_barrier(jnp.sum(hidden, axis=0)) / total_rows
    scale_two = lax.rsqrt(lax.optimization_barrier(jnp.sum(hidden * hidden, axis=0)) / total_rows - mean_two * mean_two + EPS)
    hat_two = (hidden - mean_two) * scale_two
    pre_two = hat_two * second_gain + second_bias
    act_two = gelu_value(pre_two).astype(jnp.bfloat16)
    mixed_rows = inputs_flat + jnp.dot(act_two, mix_weight, preferred_element_type=jnp.float32)
    trunk_rows = rounded(mixed_rows)
    row_mean = lax.optimization_barrier(jnp.mean(trunk_rows, axis=-1, keepdims=True))
    centered = trunk_rows - row_mean
    row_scale = lax.rsqrt(lax.optimization_barrier(jnp.mean(centered * centered, axis=-1, keepdims=True)) + EPS)
    row_hat = centered * row_scale
    normed = (row_hat * norm_gain).astype(jnp.bfloat16)
    queries = jnp.dot(normed, query_weight, preferred_element_type=jnp.float32).astype(jnp.bfloat16)
    keys_flat = jnp.dot(normed, key_weight, preferred_element_type=jnp.float32).astype(jnp.bfloat16)
    values_flat = jnp.dot(normed, value_weight, preferred_element_type=jnp.float32).astype(jnp.bfloat16)
    cot_flat = cotangent.reshape(total_rows, CHANNEL_COUNT)
    grad_out = jnp.dot(cot_flat, out_weight.T, preferred_element_type=jnp.float32).astype(jnp.bfloat16)
    results = lax.map(attend, (to_heads(queries, KD), to_heads(keys_flat, KD), to_heads(values_flat, VD), to_heads(grad_out, VD)))
    attended = from_heads(results[0], VD)
    grad_query = from_heads(results[1], KD)
    grad_key = from_heads(results[2], KD)
    grad_value = from_heads(results[3], VD)
    encoded = (trunk_rows + jnp.dot(attended, out_weight, preferred_element_type=jnp.float32)).astype(jnp.bfloat16).reshape(WINDOWS, WINDOW_BINS, CHANNEL_COUNT)
    grad_normed = jnp.dot(grad_query, query_weight.T, preferred_element_type=jnp.float32)
    grad_normed = grad_normed + jnp.dot(grad_key, key_weight.T, preferred_element_type=jnp.float32)
    grad_normed = grad_normed + jnp.dot(grad_value, value_weight.T, preferred_element_type=jnp.float32)
    grad_norm_gain = lax.optimization_barrier(jnp.sum(grad_normed * row_hat, axis=0))
    grad_hat = grad_normed * norm_gain
    grad_trunk = row_scale * (grad_hat - lax.optimization_barrier(jnp.mean(grad_hat, axis=-1, keepdims=True)) - row_hat * lax.optimization_barrier(jnp.mean(grad_hat * row_hat, axis=-1, keepdims=True)))
    grad_mixed = cot_flat.astype(jnp.float32) + grad_trunk
    grad_low = grad_mixed.astype(jnp.bfloat16)
    grad_act_two = jnp.dot(grad_low, mix_weight.T, preferred_element_type=jnp.float32)
    grad_pre_two = grad_act_two * gelu_slope(pre_two)
    grad_second_bias = lax.optimization_barrier(jnp.sum(grad_pre_two, axis=0))
    grad_second_gain = lax.optimization_barrier(jnp.sum(grad_pre_two * hat_two, axis=0))
    hidden_gradient = (second_gain * scale_two * (grad_pre_two - grad_second_bias / total_rows - hat_two * grad_second_gain / total_rows)).astype(jnp.bfloat16).reshape(WINDOWS, WINDOW_BINS, INNER_CHANNELS)
    padded_gradient = jnp.pad(hidden_gradient, ((0, 0), (DILATION_STEP, DILATION_STEP), (0, 0)))
    grad_act_one = jnp.zeros((total_rows, CHANNEL_COUNT), jnp.float32)
    for kernel_tap_index in range(3):
        shifted_input = padded_gradient[:, (2 - kernel_tap_index) * DILATION_STEP:(2 - kernel_tap_index) * DILATION_STEP + WINDOW_BINS].reshape(total_rows, INNER_CHANNELS)
        grad_act_one = grad_act_one + jnp.dot(shifted_input, conv_weight[:, kernel_tap_index * INNER_CHANNELS:(kernel_tap_index + 1) * INNER_CHANNELS].T, preferred_element_type=jnp.float32)
    grad_pre_one = grad_act_one * gelu_slope(pre_one)
    grad_first_bias = lax.optimization_barrier(jnp.sum(grad_pre_one, axis=0))
    grad_first_gain = lax.optimization_barrier(jnp.sum(grad_pre_one * hat_one, axis=0))
    grad_rows = first_gain * scale_one * (grad_pre_one - grad_first_bias / total_rows - hat_one * grad_first_gain / total_rows)
    grad_inputs = (grad_mixed + grad_rows).astype(jnp.bfloat16).reshape(WINDOWS, WINDOW_BINS, CHANNEL_COUNT)
    return (encoded, grad_inputs, grad_first_gain, grad_first_bias, grad_second_gain, grad_second_bias, grad_norm_gain)
```

```python
import functools

import jax
import jax.numpy as jnp
from jax import lax
from jax.experimental import pallas as pl
from jax.experimental.pallas import tpu as pltpu
from jax.sharding import PartitionSpec as P

H = 8
KD = 64
VD = 192
DILATION_STEP = 16


EPS = 1e-05
GELU_C = 0.7978845608028654


MESH = pl.DeviceIdType.MESH


def seq_of(z, y, x, core):
    return ((z * 4 + y) * 2 + x) * 2 + core


def all_sum_kernel(x_ref, o_ref, line, plane, send_sem, recv_sem):
    seq = lax.axis_index("seq")
    batch = lax.axis_index("batch")
    mine = batch * 4 + lax.rem(seq, 4)
    spot = seq // 4

    def line_peer(step):
        other = lax.rem(mine + step, 8)
        return {"seq": spot * 4 + lax.rem(other, 4), "batch": other // 4}

    def plane_peer(step):
        return {"seq": lax.rem(spot + step, 16) * 4 + lax.rem(seq, 4), "batch": batch}

    barrier = pltpu.get_barrier_semaphore()
    for step in range(1, 8):
        pl.semaphore_signal(barrier, inc=1, device_id=line_peer(step), device_id_type=MESH)
    for step in range(1, 16):
        pl.semaphore_signal(barrier, inc=1, device_id=plane_peer(step), device_id_type=MESH)
    line[mine] = x_ref[...]
    pl.semaphore_wait(barrier, 22)

    copies = [
        pltpu.make_async_remote_copy(
            src_ref=x_ref,
            dst_ref=line.at[mine],
            send_sem=send_sem.at[step],
            recv_sem=recv_sem.at[step],
            device_id=line_peer(step),
            device_id_type=MESH,
        )
        for step in range(1, 8)
    ]
    for copy in copies:
        copy.start()
    for copy in copies:
        copy.wait()
    total = line[0]
    for i in range(1, 8):
        total = total + line[i]
    plane[spot] = total
    copies = [
        pltpu.make_async_remote_copy(
            src_ref=plane.at[spot],
            dst_ref=plane.at[spot],
            send_sem=send_sem.at[7 + step],
            recv_sem=recv_sem.at[7 + step],
            device_id=plane_peer(step),
            device_id_type=MESH,
        )
        for step in range(1, 16)
    ]
    for copy in copies:
        copy.start()
    for copy in copies:
        copy.wait()
    total = plane[0]
    for i in range(1, 16):
        total = total + plane[i]
    o_ref[...] = total


def all_sum(parts, number):
    width = parts[0].shape[0]
    joined = jnp.concatenate(parts).reshape(-1, 128)
    rows = joined.shape[0]
    full = -(-rows // 8) * 8
    if full != rows:
        joined = jnp.pad(joined, ((0, full - rows), (0, 0)))
    vmem = pl.BlockSpec(memory_space=pltpu.VMEM)
    summed = pl.pallas_call(
        all_sum_kernel,
        out_shape=jax.ShapeDtypeStruct((full, 128), jnp.float32),
        in_specs=[vmem],
        out_specs=vmem,
        scratch_shapes=[
            pltpu.VMEM((8, full, 128), jnp.float32),
            pltpu.VMEM((16, full, 128), jnp.float32),
            pltpu.SemaphoreType.DMA((23,)),
            pltpu.SemaphoreType.DMA((23,)),
        ],
        compiler_params=pltpu.CompilerParams(collective_id=number, has_side_effects=True),
        name=f"all_sum_{number}",
    )(joined)
    flat = summed.reshape(-1)
    return [flat[i * width : (i + 1) * width] for i in range(len(parts))]


def gather_kernel(conv_ref, mix_ref, conv_out, mix_out, send_sem, recv_sem, own_sem):
    seq = lax.axis_index("seq")
    core = lax.rem(seq, 2)
    x = lax.rem(seq // 2, 2)
    y = lax.rem(seq // 4, 4)
    z = seq // 16
    pairs = ((conv_ref, conv_out), (mix_ref, mix_out))

    def first_peer(step):
        return {"seq": seq_of(lax.rem(z + step * x, 4), lax.rem(y + step * (1 - x), 4), x, core)}

    def second_peer(step):
        return {"seq": seq_of(lax.rem(z + step * (1 - x), 4), lax.rem(y + step * x, 4), x, core)}

    def y_peer(step):
        return {"seq": seq_of(z, lax.rem(y + step, 4), x, core)}

    def z_peer(step):
        return {"seq": seq_of(lax.rem(z + step, 4), y, x, core)}

    x_peer = {"seq": seq_of(z, y, 1 - x, core)}
    sibling = {"seq": seq_of(z, y, x, 1 - core)}

    barrier = pltpu.get_barrier_semaphore()
    peers = [x_peer, sibling]
    for step in range(1, 4):
        peers += [y_peer(step), z_peer(step)]
    for peer in peers:
        pl.semaphore_signal(barrier, inc=1, device_id=peer, device_id_type=MESH)
    local = [
        pltpu.make_async_copy(source, out.at[z, y, x, core], own_sem.at[i])
        for i, (source, out) in enumerate(pairs)
    ]
    for copy in local:
        copy.start()
    pl.semaphore_wait(barrier, 8)

    def send(sources, targets, peer, slot):
        copies = [
            pltpu.make_async_remote_copy(
                src_ref=source,
                dst_ref=target,
                send_sem=send_sem.at[slot, i],
                recv_sem=recv_sem.at[slot, i],
                device_id=peer,
                device_id_type=MESH,
            )
            for i, (source, target) in enumerate(zip(sources, targets))
        ]
        for copy in copies:
            copy.start()
        return copies

    inputs = [conv_ref, mix_ref]
    outs = [conv_out, mix_out]
    own_place = [out.at[z, y, x, core] for out in outs]
    got_place = [out.at[z, y, 1 - x, core] for out in outs]
    started = []
    to_x = send(inputs, own_place, x_peer, 0)
    started += to_x
    spread = []
    for step in range(1, 4):
        spread += send(inputs, own_place, first_peer(step), step)
    for copy in to_x:
        copy.wait_recv()
    for step in range(1, 4):
        spread += send(got_place, got_place, second_peer(step), 3 + step)
    started += spread
    for copy in local:
        copy.wait()
    for copy in spread:
        copy.wait_recv()
    row_block = [out.at[z, :, 0, core] for out in outs]
    column_block = [out.at[:, y, 1, core] for out in outs]
    steps = []
    for step in (1, 3, 2):
        rows = send(row_block, row_block, z_peer(step), 6 + step)
        columns = send(column_block, column_block, y_peer(step), 9 + step)
        steps.append((step, rows, columns))
        started += rows + columns
    across = send(row_block, row_block, sibling, 13) + send(column_block, column_block, sibling, 14)
    for step, rows, columns in steps:
        for copy in rows:
            copy.wait_recv()
        block = [out.at[lax.rem(z + 4 - step, 4), :, 0, core] for out in outs]
        across += send(block, block, sibling, 14 + step)
        for copy in columns:
            copy.wait_recv()
        block = [out.at[:, lax.rem(y + 4 - step, 4), 1, core] for out in outs]
        across += send(block, block, sibling, 17 + step)
    for copy in across:
        copy.wait_recv()
    for copy in started + across:
        copy.wait_send()


def gather_weights(conv_weight, mix_weight):
    anywhere = pl.BlockSpec(memory_space=pl.ANY)
    conv_full, mix_full = pl.pallas_call(
        gather_kernel,
        out_shape=[
            jax.ShapeDtypeStruct((4, 4, 2, 2) + conv_weight.shape, conv_weight.dtype),
            jax.ShapeDtypeStruct((4, 4, 2, 2) + mix_weight.shape, mix_weight.dtype),
        ],
        in_specs=[anywhere, anywhere],
        out_specs=[anywhere, anywhere],
        scratch_shapes=[
            pltpu.SemaphoreType.DMA((21, 2)),
            pltpu.SemaphoreType.DMA((21, 2)),
            pltpu.SemaphoreType.DMA((2,)),
        ],
        compiler_params=pltpu.CompilerParams(collective_id=1, has_side_effects=True),
        name="gather_weights",
    )(conv_weight, mix_weight)
    return (
        conv_full.reshape(-1, conv_weight.shape[1]),
        mix_full.reshape(-1, mix_weight.shape[1]),
    )


def padded(block, sides, width):
    for axis, dim in sides:
        count = lax.axis_size(axis)
        forward = [(i, i + 1) for i in range(count - 1)]
        backward = [(target, source) for source, target in forward]
        low = lax.ppermute(
            lax.slice_in_dim(block, block.shape[dim] - width, None, axis=dim), axis, forward
        )
        high = lax.ppermute(lax.slice_in_dim(block, 0, width, axis=dim), axis, backward)
        block = jnp.concatenate([low, block, high], axis=dim)
    return block


def gelu_value(values):
    cubic = GELU_C * (values + 0.044715 * values * values * values)
    return 0.5 * values * (1.0 + jnp.tanh(cubic))


def gelu_slope(values):
    tangent = jnp.tanh(GELU_C * (values + 0.044715 * values * values * values))
    return 0.5 * (1.0 + tangent) + 0.5 * values * (1.0 - tangent * tangent) * GELU_C * (
        1.0 + 3.0 * 0.044715 * values * values
    )


def rounded(values):
    return lax.optimization_barrier(values.astype(jnp.bfloat16)).astype(jnp.float32)


def conv_taps(padded_input, weight, local_bins, mid_width):
    outputs = [
        jnp.einsum(
            "wbc,cm->wbm",
            padded_input[
                :, kernel_tap_index * DILATION_STEP : kernel_tap_index * DILATION_STEP + local_bins
            ],
            weight[:, kernel_tap_index * mid_width : (kernel_tap_index + 1) * mid_width],
            preferred_element_type=jnp.float32,
        )
        for kernel_tap_index in range(3)
    ]
    return outputs[0] + outputs[1] + outputs[2]


def conv_back(padded_gradient, weight, local_bins, mid_width):
    outputs = [
        jnp.einsum(
            "wbm,cm->wbc",
            padded_gradient[
                :,
                (2 - kernel_tap_index) * DILATION_STEP : (2 - kernel_tap_index) * DILATION_STEP
                + local_bins,
            ],
            weight[:, kernel_tap_index * mid_width : (kernel_tap_index + 1) * mid_width],
            preferred_element_type=jnp.float32,
        )
        for kernel_tap_index in range(3)
    ]
    return outputs[0] + outputs[1] + outputs[2]


def rows_to_heads(local_rows, blocks, head_depth):
    windows_here, local_bins = (local_rows.shape[0], local_rows.shape[1])
    per_block = local_bins // blocks
    split_view = local_rows.reshape(windows_here, blocks, per_block, H, head_depth)
    ordered = split_view.transpose(3, 1, 0, 2, 4)
    return ordered.reshape(blocks * H, windows_here, per_block * head_depth)


def heads_to_rows(received, blocks, head_depth):
    windows_here = received.shape[1]
    per_block = received.shape[2] // head_depth
    arranged = received.reshape(H, blocks, windows_here, per_block, head_depth).transpose(
        2, 1, 3, 0, 4
    )
    return arranged.reshape(windows_here * blocks * per_block, H * head_depth)


def keys_to_heads(local_rows, blocks, head_depth):
    windows_here, local_bins = (local_rows.shape[0], local_rows.shape[1])
    per_head = (
        local_rows.reshape(windows_here, local_bins, H, head_depth)
        .transpose(2, 0, 1, 3)
        .reshape(H, windows_here, local_bins * head_depth)
    )
    copies = jnp.broadcast_to(per_head[:, None], (H, blocks, windows_here, local_bins * head_depth))
    return copies.reshape(blocks * H, windows_here, local_bins * head_depth)


def sum_key_parts(received, blocks, head_depth):
    windows_here = received.shape[1]
    local_bins = received.shape[2] // head_depth
    widened = received.astype(jnp.float32)
    summed = jnp.sum(widened.reshape(H, blocks, windows_here, local_bins, head_depth), axis=1)
    return (
        summed.astype(jnp.bfloat16)
        .transpose(1, 2, 0, 3)
        .reshape(windows_here * local_bins, H * head_depth)
    )


def from_pieces(received, head_depth):
    devices = received.shape[0]
    windows_here = received.shape[1]
    return (
        received.reshape(devices, windows_here, -1, head_depth)
        .transpose(1, 0, 2, 3)
        .reshape(windows_here, -1, head_depth)
    )


def to_pieces(rows_mine, devices):
    windows_here = rows_mine.shape[0]
    return rows_mine.reshape(windows_here, devices, -1).transpose(1, 0, 2)


def on_device(
    inputs,
    conv_weight,
    mix_weight,
    first_gain,
    first_bias,
    second_gain,
    second_bias,
    norm_gain,
    query_weight,
    key_weight,
    value_weight,
    out_weight,
    cotangent,
):
    windows_here, local_bins, model_width = inputs.shape
    devices = lax.axis_size("seq")
    blocks = devices // H
    local_count = windows_here * local_bins
    total_rows = local_count * devices * lax.axis_size("batch")
    mid_width = mix_weight.shape[0] * devices
    key_scale = KD ** (-0.5)
    inputs_flat = inputs.astype(jnp.float32).reshape(local_count, model_width)
    conv_full, mix_full = gather_weights(conv_weight, mix_weight)
    sum_one, square_one = all_sum(
        (jnp.sum(inputs_flat, axis=0), jnp.sum(inputs_flat * inputs_flat, axis=0)), 2
    )
    mean_one = sum_one / total_rows
    scale_one = lax.rsqrt(square_one / total_rows - mean_one * mean_one + EPS)
    hat_one = (inputs_flat - mean_one) * scale_one
    pre_one = hat_one * first_gain + first_bias
    first_activation = (
        gelu_value(pre_one).astype(jnp.bfloat16).reshape(windows_here, local_bins, model_width)
    )
    padded_input = padded(first_activation, (("seq", 1),), DILATION_STEP)
    hidden = conv_taps(padded_input, conv_full, local_bins, mid_width)
    hidden = hidden.reshape(local_count, mid_width)
    sum_two, square_two = all_sum(
        (jnp.sum(hidden, axis=0), jnp.sum(hidden * hidden, axis=0)), 3
    )
    mean_two = sum_two / total_rows
    scale_two = lax.rsqrt(square_two / total_rows - mean_two * mean_two + EPS)
    hat_two = (hidden - mean_two) * scale_two
    pre_two = hat_two * second_gain + second_bias
    act_two = gelu_value(pre_two).astype(jnp.bfloat16)
    mixed_rows = inputs_flat + jnp.dot(act_two, mix_full, preferred_element_type=jnp.float32)
    trunk_rows = rounded(mixed_rows)
    row_mean = jnp.mean(trunk_rows, axis=-1, keepdims=True)
    centered = trunk_rows - row_mean
    row_scale = lax.rsqrt(jnp.mean(centered * centered, axis=-1, keepdims=True) + EPS)
    row_hat = centered * row_scale
    normed = (row_hat * norm_gain).astype(jnp.bfloat16)
    queries = jnp.dot(normed, query_weight, preferred_element_type=jnp.float32).astype(jnp.bfloat16)
    keys_local = jnp.dot(normed, key_weight, preferred_element_type=jnp.float32).astype(
        jnp.bfloat16
    )
    values_local = jnp.dot(normed, value_weight, preferred_element_type=jnp.float32).astype(
        jnp.bfloat16
    )
    cot_flat = cotangent.reshape(local_count, model_width)
    grad_out = jnp.dot(cot_flat, out_weight.T, preferred_element_type=jnp.float32).astype(
        jnp.bfloat16
    )
    query_pieces = rows_to_heads(queries.reshape(windows_here, local_bins, H * KD), blocks, KD)
    key_pieces = keys_to_heads(keys_local.reshape(windows_here, local_bins, H * KD), blocks, KD)
    value_pieces = keys_to_heads(values_local.reshape(windows_here, local_bins, H * VD), blocks, VD)
    grad_pieces = rows_to_heads(grad_out.reshape(windows_here, local_bins, H * VD), blocks, VD)
    query_got, key_got, value_got = (
        lax.all_to_all(query_pieces, "seq", split_axis=0, concat_axis=0, tiled=True),
        lax.all_to_all(key_pieces, "seq", split_axis=0, concat_axis=0, tiled=True),
        lax.all_to_all(value_pieces, "seq", split_axis=0, concat_axis=0, tiled=True),
    )
    queries_mine = from_pieces(query_got, KD)
    keys_mine = from_pieces(key_got, KD)
    values_mine = from_pieces(value_got, VD)
    score_rows = (
        jnp.einsum("wqe,wke->wqk", queries_mine, keys_mine, preferred_element_type=jnp.float32)
        * key_scale
    )
    prob_rows = jax.nn.softmax(score_rows, axis=-1)
    prob_low = prob_rows.astype(jnp.bfloat16)
    attended = jnp.einsum(
        "wqk,wke->wqe", prob_low, values_mine, preferred_element_type=jnp.float32
    ).astype(jnp.bfloat16)
    attended_got = lax.all_to_all(
        to_pieces(attended, devices), "seq", split_axis=0, concat_axis=0, tiled=True
    )
    attended_rows = heads_to_rows(attended_got, blocks, VD)
    encoded = (
        (trunk_rows + jnp.dot(attended_rows, out_weight, preferred_element_type=jnp.float32))
        .astype(jnp.bfloat16)
        .reshape(windows_here, local_bins, model_width)
    )
    grad_got = lax.all_to_all(grad_pieces, "seq", split_axis=0, concat_axis=0, tiled=True)
    grad_mine = from_pieces(grad_got, VD)
    grad_probs = jnp.einsum(
        "wqe,wke->wqk", grad_mine, values_mine, preferred_element_type=jnp.float32
    )
    center = jnp.sum(prob_rows * grad_probs, axis=-1, keepdims=True)
    grad_scores = (prob_rows * (grad_probs - center) * key_scale).astype(jnp.bfloat16)
    grad_query = jnp.einsum(
        "wqk,wke->wqe", grad_scores, keys_mine, preferred_element_type=jnp.float32
    ).astype(jnp.bfloat16)
    grad_key = jnp.einsum(
        "wqk,wqe->wke", grad_scores, queries_mine, preferred_element_type=jnp.float32
    ).astype(jnp.bfloat16)
    grad_value = jnp.einsum(
        "wqk,wqe->wke", prob_low, grad_mine, preferred_element_type=jnp.float32
    ).astype(jnp.bfloat16)
    query_back, key_back, value_back = (
        lax.all_to_all(
            to_pieces(grad_query, devices), "seq", split_axis=0, concat_axis=0, tiled=True
        ),
        lax.all_to_all(
            to_pieces(grad_key, devices), "seq", split_axis=0, concat_axis=0, tiled=True
        ),
        lax.all_to_all(
            to_pieces(grad_value, devices), "seq", split_axis=0, concat_axis=0, tiled=True
        ),
    )
    grad_query_rows = heads_to_rows(query_back, blocks, KD)
    grad_key_rows = sum_key_parts(key_back, blocks, KD)
    grad_value_rows = sum_key_parts(value_back, blocks, VD)
    grad_normed = jnp.dot(grad_query_rows, query_weight.T, preferred_element_type=jnp.float32)
    grad_normed = grad_normed + jnp.dot(
        grad_key_rows, key_weight.T, preferred_element_type=jnp.float32
    )
    grad_normed = grad_normed + jnp.dot(
        grad_value_rows, value_weight.T, preferred_element_type=jnp.float32
    )
    norm_gain_part = jnp.sum(grad_normed * row_hat, axis=0)
    grad_hat = grad_normed * norm_gain
    grad_trunk = row_scale * (
        grad_hat
        - jnp.mean(grad_hat, axis=-1, keepdims=True)
        - row_hat * jnp.mean(grad_hat * row_hat, axis=-1, keepdims=True)
    )
    grad_mixed = cot_flat.astype(jnp.float32) + grad_trunk
    grad_low = grad_mixed.astype(jnp.bfloat16)
    grad_act_two = jnp.dot(grad_low, mix_full.T, preferred_element_type=jnp.float32)
    grad_pre_two = grad_act_two * gelu_slope(pre_two)
    grad_second_bias, grad_second_gain = all_sum(
        (jnp.sum(grad_pre_two, axis=0), jnp.sum(grad_pre_two * hat_two, axis=0)), 4
    )
    hidden_gradient = (
        (
            second_gain
            * scale_two
            * (
                grad_pre_two
                - grad_second_bias / total_rows
                - hat_two * grad_second_gain / total_rows
            )
        )
        .astype(jnp.bfloat16)
        .reshape(windows_here, local_bins, mid_width)
    )
    padded_gradient = padded(hidden_gradient, (("seq", 1),), DILATION_STEP)
    grad_act_one = conv_back(padded_gradient, conv_full, local_bins, mid_width)
    grad_act_one = grad_act_one.reshape(local_count, model_width)
    grad_pre_one = grad_act_one * gelu_slope(pre_one)
    grad_first_bias, grad_first_gain, grad_norm_gain = all_sum(
        (jnp.sum(grad_pre_one, axis=0), jnp.sum(grad_pre_one * hat_one, axis=0), norm_gain_part), 5
    )
    grad_rows = (
        first_gain
        * scale_one
        * (grad_pre_one - grad_first_bias / total_rows - hat_one * grad_first_gain / total_rows)
    )
    grad_inputs = (
        (grad_mixed + grad_rows).astype(jnp.bfloat16).reshape(windows_here, local_bins, model_width)
    )
    return (
        encoded,
        grad_inputs,
        grad_first_gain,
        grad_first_bias,
        grad_second_gain,
        grad_second_bias,
        grad_norm_gain,
    )


def solution(mesh):
    in_specs = (
        P("batch", "seq", None),
        P("seq", None),
        P("seq", None),
        P(),
        P(),
        P(),
        P(),
        P(),
        P(),
        P(),
        P(),
        P(),
        P("batch", "seq", None),
    )
    out_specs = (P("batch", "seq", None), P("batch", "seq", None), P(), P(), P(), P(), P())
    return jax.shard_map(
        on_device, mesh=mesh, in_specs=in_specs, out_specs=out_specs, check_vma=False
    )
```

```python
import jax
import jax.numpy as jnp
from jax import lax
from jax.experimental import pallas as pl
from jax.experimental.pallas import tpu as pltpu
from jax.sharding import PartitionSpec as P

H = 8
KD = 64
VD = 192
DILATION_STEP = 16


EPS = 1e-05
GELU_C = 0.7978845608028654


MESH = pl.DeviceIdType.MESH


def seq_of(z, y, x, core):
    return ((z * 4 + y) * 2 + x) * 2 + core


def all_sum_kernel(x_ref, o_ref, line, plane, send_sem, recv_sem):
    seq = lax.axis_index("seq")
    batch = lax.axis_index("batch")
    mine = batch * 4 + lax.rem(seq, 4)
    spot = seq // 4

    def line_peer(step):
        other = lax.rem(mine + step, 8)
        return {"seq": spot * 4 + lax.rem(other, 4), "batch": other // 4}

    def plane_peer(step):
        return {"seq": lax.rem(spot + step, 16) * 4 + lax.rem(seq, 4), "batch": batch}

    barrier = pltpu.get_barrier_semaphore()
    for step in range(1, 8):
        pl.semaphore_signal(barrier, inc=1, device_id=line_peer(step), device_id_type=MESH)
    for step in range(1, 16):
        pl.semaphore_signal(barrier, inc=1, device_id=plane_peer(step), device_id_type=MESH)
    line[mine] = x_ref[...]
    pl.semaphore_wait(barrier, 22)

    copies = [
        pltpu.make_async_remote_copy(
            src_ref=x_ref,
            dst_ref=line.at[mine],
            send_sem=send_sem.at[step],
            recv_sem=recv_sem.at[step],
            device_id=line_peer(step),
            device_id_type=MESH,
        )
        for step in range(1, 8)
    ]
    for copy in copies:
        copy.start()
    for copy in copies:
        copy.wait()
    total = line[0]
    for i in range(1, 8):
        total = total + line[i]
    plane[spot] = total
    copies = [
        pltpu.make_async_remote_copy(
            src_ref=plane.at[spot],
            dst_ref=plane.at[spot],
            send_sem=send_sem.at[7 + step],
            recv_sem=recv_sem.at[7 + step],
            device_id=plane_peer(step),
            device_id_type=MESH,
        )
        for step in range(1, 16)
    ]
    for copy in copies:
        copy.start()
    for copy in copies:
        copy.wait()
    total = plane[0]
    for i in range(1, 16):
        total = total + plane[i]
    o_ref[...] = total


def all_sum(parts, number):
    width = parts[0].shape[0]
    joined = jnp.concatenate(parts).reshape(-1, 128)
    rows = joined.shape[0]
    full = -(-rows // 8) * 8
    if full != rows:
        joined = jnp.pad(joined, ((0, full - rows), (0, 0)))
    vmem = pl.BlockSpec(memory_space=pltpu.VMEM)
    summed = pl.pallas_call(
        all_sum_kernel,
        out_shape=jax.ShapeDtypeStruct((full, 128), jnp.float32),
        in_specs=[vmem],
        out_specs=vmem,
        scratch_shapes=[
            pltpu.VMEM((8, full, 128), jnp.float32),
            pltpu.VMEM((16, full, 128), jnp.float32),
            pltpu.SemaphoreType.DMA((23,)),
            pltpu.SemaphoreType.DMA((23,)),
        ],
        compiler_params=pltpu.CompilerParams(collective_id=number, has_side_effects=True),
        name=f"all_sum_{number}",
    )(joined)
    flat = summed.reshape(-1)
    return [flat[i * width : (i + 1) * width] for i in range(len(parts))]


def gather_kernel(conv_ref, mix_ref, conv_out, mix_out, send_sem, recv_sem, own_sem):
    seq = lax.axis_index("seq")
    core = lax.rem(seq, 2)
    x = lax.rem(seq // 2, 2)
    y = lax.rem(seq // 4, 4)
    z = seq // 16
    pairs = ((conv_ref, conv_out), (mix_ref, mix_out))

    def first_peer(step):
        return {"seq": seq_of(lax.rem(z + step * x, 4), lax.rem(y + step * (1 - x), 4), x, core)}

    def second_peer(step):
        return {"seq": seq_of(lax.rem(z + step * (1 - x), 4), lax.rem(y + step * x, 4), x, core)}

    def y_peer(step):
        return {"seq": seq_of(z, lax.rem(y + step, 4), x, core)}

    def z_peer(step):
        return {"seq": seq_of(lax.rem(z + step, 4), y, x, core)}

    x_peer = {"seq": seq_of(z, y, 1 - x, core)}
    sibling = {"seq": seq_of(z, y, x, 1 - core)}

    barrier = pltpu.get_barrier_semaphore()
    peers = [x_peer, sibling]
    for step in range(1, 4):
        peers += [y_peer(step), z_peer(step)]
    for peer in peers:
        pl.semaphore_signal(barrier, inc=1, device_id=peer, device_id_type=MESH)
    local = [
        pltpu.make_async_copy(source, out.at[z, y, x, core], own_sem.at[i])
        for i, (source, out) in enumerate(pairs)
    ]
    for copy in local:
        copy.start()
    pl.semaphore_wait(barrier, 8)

    def send(sources, targets, peer, slot):
        copies = [
            pltpu.make_async_remote_copy(
                src_ref=source,
                dst_ref=target,
                send_sem=send_sem.at[slot, i],
                recv_sem=recv_sem.at[slot, i],
                device_id=peer,
                device_id_type=MESH,
            )
            for i, (source, target) in enumerate(zip(sources, targets))
        ]
        for copy in copies:
            copy.start()
        return copies

    inputs = [conv_ref, mix_ref]
    outs = [conv_out, mix_out]
    own_place = [out.at[z, y, x, core] for out in outs]
    got_place = [out.at[z, y, 1 - x, core] for out in outs]
    started = []
    to_x = send(inputs, own_place, x_peer, 0)
    started += to_x
    spread = []
    for step in range(1, 4):
        spread += send(inputs, own_place, first_peer(step), step)
    for copy in to_x:
        copy.wait_recv()
    for step in range(1, 4):
        spread += send(got_place, got_place, second_peer(step), 3 + step)
    started += spread
    for copy in local:
        copy.wait()
    for copy in spread:
        copy.wait_recv()
    row_block = [out.at[z, :, 0, core] for out in outs]
    column_block = [out.at[:, y, 1, core] for out in outs]
    steps = []
    for step in (1, 3, 2):
        rows = send(row_block, row_block, z_peer(step), 6 + step)
        columns = send(column_block, column_block, y_peer(step), 9 + step)
        steps.append((step, rows, columns))
        started += rows + columns
    across = send(row_block, row_block, sibling, 13) + send(column_block, column_block, sibling, 14)
    for step, rows, columns in steps:
        for copy in rows:
            copy.wait_recv()
        block = [out.at[lax.rem(z + 4 - step, 4), :, 0, core] for out in outs]
        across += send(block, block, sibling, 14 + step)
        for copy in columns:
            copy.wait_recv()
        block = [out.at[:, lax.rem(y + 4 - step, 4), 1, core] for out in outs]
        across += send(block, block, sibling, 17 + step)
    for copy in across:
        copy.wait_recv()
    for copy in started + across:
        copy.wait_send()


def gather_weights(conv_weight, mix_weight):
    anywhere = pl.BlockSpec(memory_space=pl.ANY)
    conv_full, mix_full = pl.pallas_call(
        gather_kernel,
        out_shape=[
            jax.ShapeDtypeStruct((4, 4, 2, 2) + conv_weight.shape, conv_weight.dtype),
            jax.ShapeDtypeStruct((4, 4, 2, 2) + mix_weight.shape, mix_weight.dtype),
        ],
        in_specs=[anywhere, anywhere],
        out_specs=[anywhere, anywhere],
        scratch_shapes=[
            pltpu.SemaphoreType.DMA((21, 2)),
            pltpu.SemaphoreType.DMA((21, 2)),
            pltpu.SemaphoreType.DMA((2,)),
        ],
        compiler_params=pltpu.CompilerParams(collective_id=1, has_side_effects=True),
        name="gather_weights",
    )(conv_weight, mix_weight)
    return (
        conv_full.reshape(-1, conv_weight.shape[1]),
        mix_full.reshape(-1, mix_weight.shape[1]),
    )


LOW = VD
WIDE = VD + KD


def spots():
    seq = lax.axis_index("seq")
    core = lax.rem(seq, 2)
    z = seq // 16
    mine = (z // 2) * 8 + lax.rem(seq // 2, 8)
    return seq, core, lax.rem(z, 2), mine


def pair_ahead(mine, step):
    return lax.rem(mine // 4 + step // 4, 4) * 4 + lax.rem(lax.rem(mine, 4) + step % 4, 4)


def pair_behind(mine, step):
    return lax.rem(mine // 4 + 4 - step // 4, 4) * 4 + lax.rem(lax.rem(mine, 4) + 4 - step % 4, 4)


def holder(pair, z_low, core):
    return {"seq": ((pair // 8) * 2 + z_low) * 16 + lax.rem(pair, 8) * 2 + core}


def attention_peers(seq, core, z_low, mine):
    z_peer = {"seq": seq + 16 * (1 - 2 * z_low)}
    sibling = {"seq": seq + 1 - 2 * core}
    return z_peer, sibling


def greet(mine, z_low, core, z_peer, sibling):
    barrier = pltpu.get_barrier_semaphore()
    for step in range(1, 16):
        pl.semaphore_signal(
            barrier, inc=1, device_id=holder(pair_ahead(mine, step), z_low, core), device_id_type=MESH
        )
    pl.semaphore_signal(barrier, inc=1, device_id=z_peer, device_id_type=MESH)
    pl.semaphore_signal(barrier, inc=1, device_id=sibling, device_id_type=MESH)
    return barrier


def spread_kernel(q_ref, k_ref, v_ref, g_ref, x_out, y_out, x_part, y_part, send_sem, recv_sem):
    seq, core, z_low, mine = spots()
    z_peer, sibling = attention_peers(seq, core, z_low, mine)
    barrier = greet(mine, z_low, core, z_peer, sibling)
    for window in range(2):
        rows = slice(window * 64, window * 64 + 64)
        for head in range(H):
            pair = window * H + head
            y_part[pair, :, 0:LOW] = v_ref[rows, head * VD : head * VD + VD]
            y_part[pair, :, LOW:WIDE] = k_ref[rows, head * KD : head * KD + KD]
    pl.semaphore_wait(barrier, 17)

    def send(source, target, peer, slot):
        copy = pltpu.make_async_remote_copy(
            src_ref=source,
            dst_ref=target,
            send_sem=send_sem.at[slot],
            recv_sem=recv_sem.at[slot],
            device_id=peer,
            device_id_type=MESH,
        )
        copy.start()
        return copy

    y_sends = []
    for step in range(1, 16):
        pair = pair_ahead(mine, step)
        peer = holder(pair, z_low, core)
        y_sends.append(send(y_part.at[pair], y_out.at[z_low, core, mine], peer, step))
    for window in range(2):
        rows = slice(window * 64, window * 64 + 64)
        for head in range(H):
            pair = window * H + head
            x_part[pair, :, 0:LOW] = g_ref[rows, head * VD : head * VD + VD]
            x_part[pair, :, LOW:WIDE] = q_ref[rows, head * KD : head * KD + KD]
    x_sends = []
    for step in range(1, 16):
        pair = pair_ahead(mine, step)
        peer = holder(pair, z_low, core)
        x_sends.append(send(x_part.at[pair], x_out.at[mine], peer, 16 + step))
    y_out[z_low, core, mine] = y_part[mine]
    x_out[mine] = x_part[mine]
    along = []
    across = []
    for step in range(16):
        if step > 0:
            y_sends[step - 1].wait_recv()
        place = y_out.at[z_low, core, pair_behind(mine, step)]
        along.append(send(place, place, z_peer, 32 + step))
        across.append(send(place, place, sibling, 48 + step))
    for step in range(16):
        along[step].wait_recv()
        place = y_out.at[1 - z_low, core, pair_behind(mine, step)]
        across.append(send(place, place, sibling, 64 + step))
    for copy in x_sends + across:
        copy.wait_recv()
    for copy in y_sends + x_sends + along + across:
        copy.wait_send()


def spread(queries, keys, values, grad_out):
    vmem = pl.BlockSpec(memory_space=pltpu.VMEM)
    kind = queries.dtype
    return pl.pallas_call(
        spread_kernel,
        out_shape=[
            jax.ShapeDtypeStruct((16, 64, WIDE), kind),
            jax.ShapeDtypeStruct((2, 2, 16, 64, WIDE), kind),
        ],
        in_specs=[vmem] * 4,
        out_specs=[vmem] * 2,
        scratch_shapes=[
            pltpu.VMEM((16, 64, WIDE), kind),
            pltpu.VMEM((16, 64, WIDE), kind),
            pltpu.SemaphoreType.DMA((80,)),
            pltpu.SemaphoreType.DMA((80,)),
        ],
        compiler_params=pltpu.CompilerParams(
            collective_id=6, has_side_effects=True, vmem_limit_bytes=32 * 1024 * 1024
        ),
        name="spread",
    )(queries, keys, values, grad_out)


def collect_kernel(
    oq_ref, vk_ref, a_ref, gq_ref, gv_ref, gk_ref, oq_got, vk_got, from_core, to_z, from_z, total,
    send_sem, recv_sem
):
    seq, core, z_low, mine = spots()
    z_peer, sibling = attention_peers(seq, core, z_low, mine)
    barrier = greet(mine, z_low, core, z_peer, sibling)
    pl.semaphore_wait(barrier, 17)

    def send(source, target, peer, slot):
        copy = pltpu.make_async_remote_copy(
            src_ref=source,
            dst_ref=target,
            send_sem=send_sem.at[slot],
            recv_sem=recv_sem.at[slot],
            device_id=peer,
            device_id_type=MESH,
        )
        copy.start()
        return copy

    groups = [pl.ds(lax.rem(mine // 4 + k, 4) * 4, 4) for k in range(4)]
    across = []
    for far in range(2):
        z_part = 1 - z_low if far == 0 else z_low
        for k in range(4):
            across.append(
                send(
                    vk_ref.at[z_part, 1 - core, groups[k]],
                    from_core.at[far, groups[k]],
                    sibling,
                    4 * far + k,
                )
            )
    oq_sends = []
    for step in range(1, 16):
        pair = pair_ahead(mine, step)
        oq_sends.append(
            send(oq_ref.at[pair], oq_got.at[mine], holder(pair, z_low, core), 16 + step)
        )
    oq_got[mine] = oq_ref[mine]
    along = []
    for k in range(4):
        across[k].wait_recv()
        summed = vk_ref[1 - z_low, core, groups[k]].astype(jnp.float32) + from_core[
            0, groups[k]
        ].astype(jnp.float32)
        to_z[groups[k]] = summed.astype(to_z.dtype)
        along.append(send(to_z.at[groups[k]], from_z.at[groups[k]], z_peer, 8 + k))
    vk_sends = []
    for k in range(4):
        across[4 + k].wait_recv()
        along[k].wait_recv()
        summed = vk_ref[z_low, core, groups[k]].astype(jnp.float32) + from_core[
            1, groups[k]
        ].astype(jnp.float32)
        summed = summed + from_z[groups[k]].astype(jnp.float32)
        total[groups[k]] = summed.astype(total.dtype)
        for step in range(4 * k, 4 * k + 4):
            if step > 0:
                pair = pair_ahead(mine, step)
                vk_sends.append(
                    send(total.at[pair], vk_got.at[mine], holder(pair, z_low, core), 32 + step)
                )
    vk_got[mine] = total[mine]
    for copy in oq_sends:
        copy.wait_recv()
    for window in range(2):
        rows = slice(window * 64, window * 64 + 64)
        for head in range(H):
            pair = window * H + head
            a_ref[rows, head * VD : head * VD + VD] = oq_got[pair, :, 0:LOW]
            gq_ref[rows, head * KD : head * KD + KD] = oq_got[pair, :, LOW:WIDE]
    for copy in vk_sends:
        copy.wait_recv()
    for window in range(2):
        rows = slice(window * 64, window * 64 + 64)
        for head in range(H):
            pair = window * H + head
            gv_ref[rows, head * VD : head * VD + VD] = vk_got[pair, :, 0:LOW]
            gk_ref[rows, head * KD : head * KD + KD] = vk_got[pair, :, LOW:WIDE]
    for copy in across + oq_sends + along + vk_sends:
        copy.wait_send()


def collect(oq, vk):
    vmem = pl.BlockSpec(memory_space=pltpu.VMEM)
    kind = oq.dtype
    piece = (16, 64, WIDE)
    return pl.pallas_call(
        collect_kernel,
        out_shape=[
            jax.ShapeDtypeStruct((128, H * VD), kind),
            jax.ShapeDtypeStruct((128, H * KD), kind),
            jax.ShapeDtypeStruct((128, H * VD), kind),
            jax.ShapeDtypeStruct((128, H * KD), kind),
        ],
        in_specs=[vmem] * 2,
        out_specs=[vmem] * 4,
        scratch_shapes=[
            pltpu.VMEM(piece, kind),
            pltpu.VMEM(piece, kind),
            pltpu.VMEM((2,) + piece, kind),
            pltpu.VMEM(piece, kind),
            pltpu.VMEM(piece, kind),
            pltpu.VMEM(piece, kind),
            pltpu.SemaphoreType.DMA((48,)),
            pltpu.SemaphoreType.DMA((48,)),
        ],
        compiler_params=pltpu.CompilerParams(
            collective_id=7, has_side_effects=True, vmem_limit_bytes=32 * 1024 * 1024
        ),
        name="collect",
    )(oq, vk)


CHUNK = 1024
QUERY_BLOCK = 256
SIDE = (((1,), (1,)), ((), ()))


def attend_kernel(x_ref, y_ref, oq_ref, vk_ref, y_turned, score, slope, total):
    keys = y_ref.shape[0]
    chunks = [slice(start, start + CHUNK) for start in range(0, keys, CHUNK)]
    key_scale = KD ** (-0.5)
    for part in chunks:
        y_turned[:, part] = y_ref[part, :].T
    total[...] = jnp.zeros_like(total)

    def block(index, carry):
        rows = pl.ds(pl.multiple_of(index * QUERY_BLOCK, QUERY_BLOCK), QUERY_BLOCK)
        x_block = x_ref[rows, :]
        wide = x_block.astype(jnp.float32)
        low = lax.broadcasted_iota(jnp.int32, wide.shape, 1) < LOW
        query = jnp.where(low, 0.0, wide).astype(x_block.dtype)
        grad = jnp.where(low, wide, 0.0).astype(x_block.dtype)
        peak = None
        for part in chunks:
            scores = lax.dot_general(y_ref[part, :], query, SIDE, preferred_element_type=jnp.float32)
            score[part, :] = scores
            top = jnp.max(scores, axis=0, keepdims=True)
            peak = top if peak is None else jnp.maximum(peak, top)
        weight = jnp.zeros((1, QUERY_BLOCK), jnp.float32)
        center = jnp.zeros((1, QUERY_BLOCK), jnp.float32)
        for part in chunks:
            grads = lax.dot_general(y_ref[part, :], grad, SIDE, preferred_element_type=jnp.float32)
            slope[part, :] = grads
            terms = jnp.exp2((score[part, :] - peak) * (key_scale * 1.4426950408889634))
            score[part, :] = terms
            weight = weight + jnp.sum(terms, axis=0, keepdims=True)
            center = center + jnp.sum(terms * grads, axis=0, keepdims=True)
        share = 1.0 / weight
        center = center * share
        out = jnp.zeros((WIDE, QUERY_BLOCK), jnp.float32)
        back = jnp.zeros((WIDE, QUERY_BLOCK), jnp.float32)
        low_keys = lax.broadcasted_iota(jnp.int32, (CHUNK, WIDE), 1) < LOW
        for part in chunks:
            probs = score[part, :] * share
            prob_low = probs.astype(jnp.bfloat16)
            grads = (probs * (slope[part, :] - center) * key_scale).astype(jnp.bfloat16)
            out = out + jnp.dot(y_turned[:, part], prob_low, preferred_element_type=jnp.float32)
            back = back + jnp.dot(y_turned[:, part], grads, preferred_element_type=jnp.float32)
            for_values = jnp.dot(prob_low, x_block, preferred_element_type=jnp.float32)
            for_keys = jnp.dot(grads, x_block, preferred_element_type=jnp.float32)
            total[part, :] += jnp.where(low_keys, for_values, for_keys)
        low_rows = lax.broadcasted_iota(jnp.int32, out.shape, 0) < LOW
        oq_ref[rows, :] = jnp.where(low_rows, out, back).T.astype(oq_ref.dtype)
        return carry

    lax.fori_loop(0, x_ref.shape[0] // QUERY_BLOCK, block, 0)
    vk_ref[...] = total[...].astype(vk_ref.dtype)


def attend(x_rows, y_rows):
    vmem = pl.BlockSpec(memory_space=pltpu.VMEM)
    queries, keys = x_rows.shape[0], y_rows.shape[0]
    return pl.pallas_call(
        attend_kernel,
        out_shape=[
            jax.ShapeDtypeStruct(x_rows.shape, x_rows.dtype),
            jax.ShapeDtypeStruct(y_rows.shape, y_rows.dtype),
        ],
        in_specs=[vmem] * 2,
        out_specs=[vmem] * 2,
        scratch_shapes=[
            pltpu.VMEM((WIDE, keys), y_rows.dtype),
            pltpu.VMEM((keys, QUERY_BLOCK), jnp.float32),
            pltpu.VMEM((keys, QUERY_BLOCK), jnp.float32),
            pltpu.VMEM((keys, WIDE), jnp.float32),
        ],
        compiler_params=pltpu.CompilerParams(vmem_limit_bytes=52 * 1024 * 1024),
        name="attend",
        cost_estimate=pl.CostEstimate(
            flops=12 * queries * keys * WIDE, bytes_accessed=8 * keys * WIDE, transcendentals=queries * keys
        ),
    )(x_rows, y_rows)


def padded(block, sides, width):
    for axis, dim in sides:
        count = lax.axis_size(axis)
        forward = [(i, i + 1) for i in range(count - 1)]
        backward = [(target, source) for source, target in forward]
        low = lax.ppermute(
            lax.slice_in_dim(block, block.shape[dim] - width, None, axis=dim), axis, forward
        )
        high = lax.ppermute(lax.slice_in_dim(block, 0, width, axis=dim), axis, backward)
        block = jnp.concatenate([low, block, high], axis=dim)
    return block


def gelu_value(values):
    cubic = GELU_C * (values + 0.044715 * values * values * values)
    return 0.5 * values * (1.0 + jnp.tanh(cubic))


def gelu_slope(values):
    tangent = jnp.tanh(GELU_C * (values + 0.044715 * values * values * values))
    return 0.5 * (1.0 + tangent) + 0.5 * values * (1.0 - tangent * tangent) * GELU_C * (
        1.0 + 3.0 * 0.044715 * values * values
    )


def rounded(values):
    return lax.optimization_barrier(values.astype(jnp.bfloat16)).astype(jnp.float32)


def conv_taps(padded_input, weight, local_bins, mid_width):
    outputs = [
        jnp.einsum(
            "wbc,cm->wbm",
            padded_input[
                :, kernel_tap_index * DILATION_STEP : kernel_tap_index * DILATION_STEP + local_bins
            ],
            weight[:, kernel_tap_index * mid_width : (kernel_tap_index + 1) * mid_width],
            preferred_element_type=jnp.float32,
        )
        for kernel_tap_index in range(3)
    ]
    return outputs[0] + outputs[1] + outputs[2]


def conv_back(padded_gradient, weight, local_bins, mid_width):
    outputs = [
        jnp.einsum(
            "wbm,cm->wbc",
            padded_gradient[
                :,
                (2 - kernel_tap_index) * DILATION_STEP : (2 - kernel_tap_index) * DILATION_STEP
                + local_bins,
            ],
            weight[:, kernel_tap_index * mid_width : (kernel_tap_index + 1) * mid_width],
            preferred_element_type=jnp.float32,
        )
        for kernel_tap_index in range(3)
    ]
    return outputs[0] + outputs[1] + outputs[2]


def on_device(
    inputs,
    conv_weight,
    mix_weight,
    first_gain,
    first_bias,
    second_gain,
    second_bias,
    norm_gain,
    query_weight,
    key_weight,
    value_weight,
    out_weight,
    cotangent,
):
    windows_here, local_bins, model_width = inputs.shape
    devices = lax.axis_size("seq")
    local_count = windows_here * local_bins
    total_rows = local_count * devices * lax.axis_size("batch")
    mid_width = mix_weight.shape[0] * devices
    inputs_flat = inputs.astype(jnp.float32).reshape(local_count, model_width)
    conv_full, mix_full = gather_weights(conv_weight, mix_weight)
    sum_one, square_one = all_sum(
        (jnp.sum(inputs_flat, axis=0), jnp.sum(inputs_flat * inputs_flat, axis=0)), 2
    )
    mean_one = sum_one / total_rows
    scale_one = lax.rsqrt(square_one / total_rows - mean_one * mean_one + EPS)
    hat_one = (inputs_flat - mean_one) * scale_one
    pre_one = hat_one * first_gain + first_bias
    first_activation = (
        gelu_value(pre_one).astype(jnp.bfloat16).reshape(windows_here, local_bins, model_width)
    )
    padded_input = padded(first_activation, (("seq", 1),), DILATION_STEP)
    hidden = conv_taps(padded_input, conv_full, local_bins, mid_width)
    hidden = hidden.reshape(local_count, mid_width)
    sum_two, square_two = all_sum(
        (jnp.sum(hidden, axis=0), jnp.sum(hidden * hidden, axis=0)), 3
    )
    mean_two = sum_two / total_rows
    scale_two = lax.rsqrt(square_two / total_rows - mean_two * mean_two + EPS)
    hat_two = (hidden - mean_two) * scale_two
    pre_two = hat_two * second_gain + second_bias
    act_two = gelu_value(pre_two).astype(jnp.bfloat16)
    mixed_rows = inputs_flat + jnp.dot(act_two, mix_full, preferred_element_type=jnp.float32)
    trunk_rows = rounded(mixed_rows)
    row_mean = jnp.mean(trunk_rows, axis=-1, keepdims=True)
    centered = trunk_rows - row_mean
    row_scale = lax.rsqrt(jnp.mean(centered * centered, axis=-1, keepdims=True) + EPS)
    row_hat = centered * row_scale
    normed = (row_hat * norm_gain).astype(jnp.bfloat16)
    queries = jnp.dot(normed, query_weight, preferred_element_type=jnp.float32).astype(jnp.bfloat16)
    keys_local = jnp.dot(normed, key_weight, preferred_element_type=jnp.float32).astype(
        jnp.bfloat16
    )
    values_local = jnp.dot(normed, value_weight, preferred_element_type=jnp.float32).astype(
        jnp.bfloat16
    )
    cot_flat = cotangent.reshape(local_count, model_width)
    grad_out = jnp.dot(cot_flat, out_weight.T, preferred_element_type=jnp.float32).astype(
        jnp.bfloat16
    )
    x_got, y_got = spread(queries, keys_local, values_local, grad_out)
    oq, vk = attend(x_got.reshape(-1, WIDE), y_got.reshape(-1, WIDE))
    attended_rows, grad_query_rows, grad_value_rows, grad_key_rows = collect(
        oq.reshape(x_got.shape), vk.reshape(y_got.shape)
    )
    encoded = (
        (trunk_rows + jnp.dot(attended_rows, out_weight, preferred_element_type=jnp.float32))
        .astype(jnp.bfloat16)
        .reshape(windows_here, local_bins, model_width)
    )
    grad_normed = jnp.dot(grad_query_rows, query_weight.T, preferred_element_type=jnp.float32)
    grad_normed = grad_normed + jnp.dot(
        grad_key_rows, key_weight.T, preferred_element_type=jnp.float32
    )
    grad_normed = grad_normed + jnp.dot(
        grad_value_rows, value_weight.T, preferred_element_type=jnp.float32
    )
    norm_gain_part = jnp.sum(grad_normed * row_hat, axis=0)
    grad_hat = grad_normed * norm_gain
    grad_trunk = row_scale * (
        grad_hat
        - jnp.mean(grad_hat, axis=-1, keepdims=True)
        - row_hat * jnp.mean(grad_hat * row_hat, axis=-1, keepdims=True)
    )
    grad_mixed = cot_flat.astype(jnp.float32) + grad_trunk
    grad_low = grad_mixed.astype(jnp.bfloat16)
    grad_act_two = jnp.dot(grad_low, mix_full.T, preferred_element_type=jnp.float32)
    grad_pre_two = grad_act_two * gelu_slope(pre_two)
    grad_second_bias, grad_second_gain = all_sum(
        (jnp.sum(grad_pre_two, axis=0), jnp.sum(grad_pre_two * hat_two, axis=0)), 4
    )
    hidden_gradient = (
        (
            second_gain
            * scale_two
            * (
                grad_pre_two
                - grad_second_bias / total_rows
                - hat_two * grad_second_gain / total_rows
            )
        )
        .astype(jnp.bfloat16)
        .reshape(windows_here, local_bins, mid_width)
    )
    padded_gradient = padded(hidden_gradient, (("seq", 1),), DILATION_STEP)
    grad_act_one = conv_back(padded_gradient, conv_full, local_bins, mid_width)
    grad_act_one = grad_act_one.reshape(local_count, model_width)
    grad_pre_one = grad_act_one * gelu_slope(pre_one)
    grad_first_bias, grad_first_gain, grad_norm_gain = all_sum(
        (jnp.sum(grad_pre_one, axis=0), jnp.sum(grad_pre_one * hat_one, axis=0), norm_gain_part), 5
    )
    grad_rows = (
        first_gain
        * scale_one
        * (grad_pre_one - grad_first_bias / total_rows - hat_one * grad_first_gain / total_rows)
    )
    grad_inputs = (
        (grad_mixed + grad_rows).astype(jnp.bfloat16).reshape(windows_here, local_bins, model_width)
    )
    return (
        encoded,
        grad_inputs,
        grad_first_gain,
        grad_first_bias,
        grad_second_gain,
        grad_second_bias,
        grad_norm_gain,
    )


def solution(mesh):
    in_specs = (
        P("batch", "seq", None),
        P("seq", None),
        P("seq", None),
        P(),
        P(),
        P(),
        P(),
        P(),
        P(),
        P(),
        P(),
        P(),
        P("batch", "seq", None),
    )
    out_specs = (P("batch", "seq", None), P("batch", "seq", None), P(), P(), P(), P(), P())
    return jax.shard_map(
        on_device, mesh=mesh, in_specs=in_specs, out_specs=out_specs, check_vma=False
    )
```

```python
import jax
import jax.numpy as jnp
from jax import lax
from jax.experimental import pallas as pl
from jax.experimental.pallas import tpu as pltpu
from jax.sharding import PartitionSpec as P

H = 8
KD = 64
VD = 192
DILATION_STEP = 16


EPS = 1e-05
GELU_C = 0.7978845608028654


MESH = pl.DeviceIdType.MESH
ROWS = 128
LINE = 8
PLANE = 16
TAP_PARTS = ((0, 0, 0, 768), (1, 0, 768, 384), (1, 1, 0, 384), (2, 1, 384, 768))


def seq_of(z, y, x, core):
    return ((z * 4 + y) * 2 + x) * 2 + core


def remote(source, target, peer, sems, slot):
    copy = pltpu.make_async_remote_copy(
        src_ref=source,
        dst_ref=target,
        send_sem=sems[0].at[slot],
        recv_sem=sems[1].at[slot],
        device_id=peer,
        device_id_type=MESH,
    )
    copy.start()
    return copy


def line_place():
    return lax.axis_index("batch") * 4 + lax.rem(lax.axis_index("seq"), 4)


def line_peer(step):
    other = lax.rem(line_place() + step, LINE)
    spot = lax.axis_index("seq") // 4
    return {"seq": spot * 4 + lax.rem(other, 4), "batch": other // 4}


def plane_peer(step):
    seq = lax.axis_index("seq")
    return {"seq": lax.rem(seq // 4 + step, PLANE) * 4 + lax.rem(seq, 4)}


def ring_peer(step):
    count = 4 * PLANE
    return {"seq": lax.rem(lax.axis_index("seq") + step + count, count)}


def greet_all():
    barrier = pltpu.get_barrier_semaphore()
    peers = [line_peer(step) for step in range(1, LINE)]
    peers += [plane_peer(step) for step in range(1, PLANE)]
    peers += [ring_peer(1), ring_peer(-1)]
    for peer in peers:
        pl.semaphore_signal(barrier, inc=1, device_id=peer, device_id_type=MESH)
    return barrier, len(peers)


def line_send(line, sems, base):
    place = line.at[line_place()]
    return [remote(place, place, line_peer(step), sems, base + step) for step in range(1, LINE)]


def plane_send(line, plane, arrivals, sems, base):
    for copy in arrivals:
        copy.wait_recv()
    total = line[0]
    for i in range(1, LINE):
        total = total + line[i]
    spot = lax.axis_index("seq") // 4
    plane[spot] = total
    place = plane.at[spot]
    return [
        remote(place, place, plane_peer(step), sems, base + LINE + step) for step in range(1, PLANE)
    ]


def plane_sum(plane, arrivals):
    for copy in arrivals:
        copy.wait_recv()
    total = plane[0]
    for i in range(1, PLANE):
        total = total + plane[i]
    return total


def halo_send(middle, low, high, sems, base):
    return [
        remote(middle.at[:, 48:64, :], low, ring_peer(1), sems, (base, 0)),
        remote(middle.at[:, 0:16, :], high, ring_peer(-1), sems, (base, 1)),
    ]


def halo_fill(padded, low, high, copies):
    seq = lax.axis_index("seq")
    last = lax.axis_size("seq") - 1
    for copy in copies:
        copy.wait_recv()
    low_rows = low[...].astype(jnp.float32)
    high_rows = high[...].astype(jnp.float32)
    padded[:, 0:16, :] = jnp.where(seq == 0, 0.0, low_rows).astype(padded.dtype)
    padded[:, 80:96, :] = jnp.where(seq == last, 0.0, high_rows).astype(padded.dtype)


def tap_rows(padded, start):
    return jnp.concatenate([padded[0, start : start + 64, :], padded[1, start : start + 64, :]], axis=0)


def stacked(rows):
    return jnp.concatenate([jnp.sum(part, axis=0, keepdims=True) for part in rows], axis=0)


def gelu_value(values):
    cubic = GELU_C * (values + 0.044715 * values * values * values)
    return 0.5 * values * (1.0 + jnp.tanh(cubic))


def gelu_slope(values):
    tangent = jnp.tanh(GELU_C * (values + 0.044715 * values * values * values))
    return 0.5 * (1.0 + tangent) + 0.5 * values * (1.0 - tangent * tangent) * GELU_C * (
        1.0 + 3.0 * 0.044715 * values * values
    )


def rounded(values):
    return lax.optimization_barrier(values.astype(jnp.bfloat16)).astype(jnp.float32)


CHUNK = 1024
QUERY_BLOCK = 256
SIDE = (((1,), (1,)), ((), ()))
def front_kernel(
    x_ref, conv_ref, mix_ref, gain_ref, bias_ref, cot_ref, out_weight_ref,
    conv_out, mix_out, hidden_out, stats_one_out, stats_two_out, grad_out,
    line_one, plane_one, line_two, plane_two, conv_other, mix_other, mix_land, middle, padded,
    low, high, weight, sum_send, sum_recv, move_send, move_recv, own_sem
):
    seq = lax.axis_index("seq")
    core = lax.rem(seq, 2)
    x = lax.rem(seq // 2, 2)
    y = lax.rem(seq // 4, 4)
    z = seq // 16
    sums = (sum_send, sum_recv)
    moves = (move_send, move_recv)
    total_rows = ROWS * lax.axis_size("seq") * lax.axis_size("batch")
    barrier, count = greet_all()
    load = pltpu.make_async_copy(out_weight_ref, weight, own_sem)
    load.start()
    values = x_ref[...].astype(jnp.float32)
    line_one[line_place()] = stacked([values, values * values])
    pl.semaphore_wait(barrier, count)

    def first_peer(step):
        return {"seq": seq_of(lax.rem(z + step * x, 4), lax.rem(y + step * (1 - x), 4), x, core)}

    def second_peer(step):
        return {"seq": seq_of(lax.rem(z + step * (1 - x), 4), lax.rem(y + step * x, 4), x, core)}

    def y_peer(step):
        return {"seq": seq_of(z, lax.rem(y + step, 4), x, core)}

    def z_peer(step):
        return {"seq": seq_of(lax.rem(z + step, 4), y, x, core)}

    x_peer = {"seq": seq_of(z, y, 1 - x, core)}
    sibling = {"seq": seq_of(z, y, x, 1 - core)}
    outs = (conv_out, mix_land)
    widths = (conv_ref.shape[1] // 2, mix_ref.shape[1] // 2)
    halves = [pl.ds(pl.multiple_of(core * w, w), w) for w in widths]
    far_halves = [pl.ds(pl.multiple_of((1 - core) * w, w), w) for w in widths]

    def move(kind, where, peer, slot):
        place = outs[kind].at[(core, *where)]
        return remote(place, place, peer, moves, (slot, kind))

    started = line_send(line_one, sums, 0)
    line_started = started
    pair_up = [
        remote(conv_ref.at[:, far_halves[0]], conv_other, sibling, moves, (0, 0)),
        remote(mix_ref.at[:, far_halves[1]], mix_other, sibling, moves, (0, 1)),
    ]
    started = started + pair_up
    for kind, mine, other in ((0, conv_ref, conv_other), (1, mix_ref, mix_other)):
        pair_up[kind].wait_recv()
        out = outs[kind]
        here = mine[:, halves[kind]].astype(jnp.float32)
        there = other[...].astype(jnp.float32)
        upper = jnp.where(core == 0, here, there)
        lower = jnp.where(core == 0, there, here)
        out[core, z, y, x] = jnp.concatenate([upper, lower], axis=0).astype(out.dtype)
    to_x = [move(kind, (z, y, x), x_peer, 1) for kind in range(2)]
    spread_out = []
    for kind in range(2):
        for step in (1, 3):
            spread_out.append(move(kind, (z, y, x), first_peer(step), 1 + step))
    plane_started = plane_send(line_one, plane_one, line_started, sums, 0)
    for copy in to_x:
        copy.wait_recv()
    for kind in range(2):
        for step in (1, 3):
            spread_out.append(move(kind, (z, y, 1 - x), second_peer(step), 4 + step))
    first_block, second_block = spread_out[:4], spread_out[4:]
    for kind, step, back in ((0, 1, 3), (1, 3, 1)):
        first_block[2 * kind + step // 2].wait_recv()
        place = (lax.rem(z + back * x, 4), lax.rem(y + back * (1 - x), 4), x)
        spread_out.append(move(kind, place, first_peer(step), 3))
    total = plane_sum(plane_one, plane_started)
    mean = total[0:1, :] / total_rows
    scale = lax.rsqrt(total[1:2, :] / total_rows - mean * mean + EPS)
    stats_one_out[...] = jnp.concatenate([mean, scale], axis=0)
    pre = (values - mean) * scale * gain_ref[...] + bias_ref[...]
    active = gelu_value(pre).astype(middle.dtype)
    for window in range(2):
        middle[window] = active[window * 64 : window * 64 + 64, :]
        padded[window, 16:80, :] = active[window * 64 : window * 64 + 64, :]
    halos = halo_send(middle, low, high, moves, 19)
    for kind, step, back in ((0, 1, 3), (1, 3, 1)):
        second_block[2 * kind + step // 2].wait_recv()
        place = (lax.rem(z + back * (1 - x), 4), lax.rem(y + back * x, 4), 1 - x)
        spread_out.append(move(kind, place, second_peer(step), 6))
    waited = (first_block[0], first_block[3], second_block[0], second_block[3])
    for copy in spread_out:
        if all(copy is not other for other in waited):
            copy.wait_recv()
    whole = slice(None)
    blocks = [[], []]
    across = [[], []]

    def launch(kind):
        for step in (1, 3):
            blocks[kind].append(move(kind, (z, whole, 0), z_peer(step), 7 + step))
            blocks[kind].append(move(kind, (whole, y, 1), y_peer(step), 10 + step))
        across[kind].append(move(kind, (z, whole, 0), sibling, 14))
        across[kind].append(move(kind, (whole, y, 1), sibling, 15))

    def relay(kind):
        for i, (step, part) in enumerate(((1, slice(0, 2)), (3, slice(2, 4)))):
            from_z, from_y = lax.rem(z + 4 - step, 4), lax.rem(y + 4 - step, 4)
            blocks[kind][2 * i].wait_recv()
            blocks[kind].append(move(kind, (from_z, part, 0), z_peer(step), 9 if i == 0 else 24))
            blocks[kind][2 * i + 1].wait_recv()
            blocks[kind].append(move(kind, (part, from_y, 1), y_peer(step), 12 if i == 0 else 25))
            across[kind].append(move(kind, (from_z, whole, 0), sibling, 15 + step))
            across[kind].append(move(kind, (whole, from_y, 1), sibling, 20 + step))

    def finish(kind):
        blocks[kind][4].wait_recv()
        blocks[kind][6].wait_recv()
        across[kind].append(move(kind, (lax.rem(z + 2, 4), whole, 0), sibling, 17))
        blocks[kind][5].wait_recv()
        blocks[kind][7].wait_recv()
        across[kind].append(move(kind, (whole, lax.rem(y + 2, 4), 1), sibling, 22))

    launch(0)
    load.wait()
    grad_out[...] = lax.dot_general(
        cot_ref[...], weight[...], SIDE, preferred_element_type=jnp.float32
    ).astype(grad_out.dtype)
    halo_fill(padded, low, high, halos)

    relay(0)
    launch(1)
    finish(0)
    for copy in across[0]:
        copy.wait_recv()
    terms = {}
    for tap, half, start, size in TAP_PARTS:
        part = conv_out[half, :, :, :, :, start : start + size].reshape(-1, size)
        terms[tap, half] = jnp.dot(tap_rows(padded, 16 * tap), part, preferred_element_type=jnp.float32)
    middle_tap = jnp.concatenate([terms[1, 0], terms[1, 1]], axis=1)
    hidden = terms[0, 0] + middle_tap + terms[2, 1]
    hidden_out[...] = hidden
    line_two[line_place()] = stacked([hidden, hidden * hidden])
    line_again = line_send(line_two, sums, LINE + PLANE)
    relay(1)
    plane_again = plane_send(line_two, plane_two, line_again, sums, LINE + PLANE)
    finish(1)
    for copy in across[1]:
        copy.wait_recv()
    for i in range(4):
        for j in range(4):
            start = (i * 4 + j) * 48
            for half in range(2):
                pair = [mix_land[half, i, j, k].astype(jnp.float32) for k in range(2)]
                columns = slice(half * widths[1], half * widths[1] + widths[1])
                mix_out[start : start + 48, columns] = jnp.concatenate(pair, axis=0).astype(mix_out.dtype)
    stats_two_out[...] = plane_sum(plane_two, plane_again)
    ended = started + to_x + spread_out + halos + plane_started + line_again + plane_again
    for kind in range(2):
        ended += blocks[kind] + across[kind]
    for copy in ended:
        copy.wait_send()


def front(inputs, conv_weight, mix_weight, gain, bias, cot, out_weight):
    vmem = pl.BlockSpec(memory_space=pltpu.VMEM)
    anywhere = pl.BlockSpec(memory_space=pl.ANY)
    width = inputs.shape[1]
    mid_width = conv_weight.shape[1] // 3
    kind = inputs.dtype
    conv_rows, mix_rows = conv_weight.shape[0], mix_weight.shape[0]
    full, wide = jnp.float32, conv_weight.shape[1]
    sems = 2 * (LINE + PLANE)
    conv_full, *rest = pl.pallas_call(
        front_kernel,
        out_shape=[
            jax.ShapeDtypeStruct((2, 4, 4, 2, 2 * conv_rows, wide // 2), kind),
            jax.ShapeDtypeStruct((64 * mix_rows, width), kind),
            jax.ShapeDtypeStruct((ROWS, mid_width), full),
            jax.ShapeDtypeStruct((2, width), full),
            jax.ShapeDtypeStruct((2, mid_width), full),
            jax.ShapeDtypeStruct((ROWS, out_weight.shape[0]), kind),
        ],
        in_specs=[vmem] * 6 + [anywhere],
        out_specs=[vmem] * 6,
        scratch_shapes=[
            pltpu.VMEM((LINE, 2, width), full),
            pltpu.VMEM((PLANE, 2, width), full),
            pltpu.VMEM((LINE, 2, mid_width), full),
            pltpu.VMEM((PLANE, 2, mid_width), full),
            pltpu.VMEM((conv_rows, wide // 2), kind),
            pltpu.VMEM((mix_rows, width // 2), kind),
            pltpu.VMEM((2, 4, 4, 2, 2 * mix_rows, width // 2), kind),
            pltpu.VMEM((2, 64, width), kind),
            pltpu.VMEM((2, 96, width), kind),
            pltpu.VMEM((2, 16, width), kind),
            pltpu.VMEM((2, 16, width), kind),
            pltpu.VMEM(out_weight.shape, kind),
            pltpu.SemaphoreType.DMA((sems,)),
            pltpu.SemaphoreType.DMA((sems,)),
            pltpu.SemaphoreType.DMA((26, 2)),
            pltpu.SemaphoreType.DMA((26, 2)),
            pltpu.SemaphoreType.DMA,
        ],
        compiler_params=pltpu.CompilerParams(
            collective_id=1, has_side_effects=True, vmem_limit_bytes=48 * 1024 * 1024
        ),
        name="front",
    )(inputs, conv_weight, mix_weight, gain, bias, cot, out_weight)
    return [conv_full.reshape(2, -1, wide // 2)] + rest


def tail_kernel(
    grad_ref, hat_ref, factor_ref, norm_ref, x_ref, stats_ref, gain_ref, bias_ref, mixed_ref, conv_ref,
    out_ref, sums_two_out, sums_one_out,
    line_two, plane_two, line_one, plane_one, middle, padded, low, high, hat_one, slope_one, weight,
    sum_send, sum_recv, move_send, move_recv, own_sem
):
    sums = (sum_send, sum_recv)
    moves = (move_send, move_recv)
    total_rows = ROWS * lax.axis_size("seq") * lax.axis_size("batch")
    barrier, count = greet_all()
    load = pltpu.make_async_copy(conv_ref, weight, own_sem)
    load.start()
    grads = grad_ref[...]
    place = line_place()
    line_two[place, 0:2, :] = stacked([grads, grads * hat_ref[...]])
    line_two[place, 2:4, :] = norm_ref[...]
    pl.semaphore_wait(barrier, count)
    started = line_send(line_two, sums, 0)
    mean, scale = stats_ref[0:1, :], stats_ref[1:2, :]
    hat = (x_ref[...].astype(jnp.float32) - mean) * scale
    hat_one[...] = hat
    plane_started = plane_send(line_two, plane_two, started, sums, 0)
    slope_one[...] = gelu_slope(hat * gain_ref[...] + bias_ref[...])
    total = plane_sum(plane_two, plane_started)
    sums_two_out[...] = total
    hidden_grad = (
        factor_ref[...]
        * (grad_ref[...] - total[0:1, :] / total_rows - hat_ref[...] * total[1:2, :] / total_rows)
    ).astype(middle.dtype)
    for window in range(2):
        middle[window] = hidden_grad[window * 64 : window * 64 + 64, :]
        padded[window, 16:80, :] = hidden_grad[window * 64 : window * 64 + 64, :]
    halos = halo_send(middle, low, high, moves, 0)
    load.wait()
    grad_act = None
    for tap, half, start, size in (TAP_PARTS[1], TAP_PARTS[2], TAP_PARTS[0], TAP_PARTS[3]):
        if tap == 0:
            halo_fill(padded, low, high, halos)
        first = 0 if half == 0 or tap == 2 else 384
        term = lax.dot_general(
            tap_rows(padded, 16 * (2 - tap))[:, first : first + size],
            weight[half, :, start : start + size],
            SIDE,
            preferred_element_type=jnp.float32,
        )
        grad_act = term if grad_act is None else grad_act + term
    grad_pre = grad_act * slope_one[...]
    line_one[place] = stacked([grad_pre, grad_pre * hat_one[...]])
    line_again = line_send(line_one, sums, LINE + PLANE)
    plane_again = plane_send(line_one, plane_one, line_again, sums, LINE + PLANE)
    total = plane_sum(plane_one, plane_again)
    sums_one_out[...] = total
    grad_rows = (
        gain_ref[...]
        * scale
        * (grad_pre - total[0:1, :] / total_rows - hat_one[...] * total[1:2, :] / total_rows)
    )
    out_ref[...] = (mixed_ref[...] + grad_rows).astype(out_ref.dtype)
    for copy in started + plane_started + halos + line_again + plane_again:
        copy.wait_send()


def tail(grad_pre, hat_two, factor, norm_part, inputs, stats, gain, bias, mixed, conv_full):
    vmem = pl.BlockSpec(memory_space=pltpu.VMEM)
    anywhere = pl.BlockSpec(memory_space=pl.ANY)
    width, mid_width = inputs.shape[1], grad_pre.shape[1]
    kind, full = inputs.dtype, jnp.float32
    sems = 2 * (LINE + PLANE)
    return pl.pallas_call(
        tail_kernel,
        out_shape=[
            jax.ShapeDtypeStruct((ROWS, width), kind),
            jax.ShapeDtypeStruct((4, mid_width), full),
            jax.ShapeDtypeStruct((2, width), full),
        ],
        in_specs=[vmem] * 9 + [anywhere],
        out_specs=[vmem] * 3,
        scratch_shapes=[
            pltpu.VMEM((LINE, 4, mid_width), full),
            pltpu.VMEM((PLANE, 4, mid_width), full),
            pltpu.VMEM((LINE, 2, width), full),
            pltpu.VMEM((PLANE, 2, width), full),
            pltpu.VMEM((2, 64, mid_width), kind),
            pltpu.VMEM((2, 96, mid_width), kind),
            pltpu.VMEM((2, 16, mid_width), kind),
            pltpu.VMEM((2, 16, mid_width), kind),
            pltpu.VMEM((ROWS, width), full),
            pltpu.VMEM((ROWS, width), full),
            pltpu.VMEM(conv_full.shape, kind),
            pltpu.SemaphoreType.DMA((sems,)),
            pltpu.SemaphoreType.DMA((sems,)),
            pltpu.SemaphoreType.DMA((1, 2)),
            pltpu.SemaphoreType.DMA((1, 2)),
            pltpu.SemaphoreType.DMA,
        ],
        compiler_params=pltpu.CompilerParams(
            collective_id=2, has_side_effects=True, vmem_limit_bytes=40 * 1024 * 1024
        ),
        name="tail",
    )(grad_pre, hat_two, factor, norm_part, inputs, stats, gain, bias, mixed, conv_full)


LOW = VD
WIDE = VD + KD


def spots():
    seq = lax.axis_index("seq")
    core = lax.rem(seq, 2)
    z = seq // 16
    mine = (z // 2) * 8 + lax.rem(seq // 2, 8)
    return seq, core, lax.rem(z + z // 2, 2), mine


def pair_ahead(mine, step):
    return lax.rem(mine // 4 + step // 4, 4) * 4 + lax.rem(lax.rem(mine, 4) + step % 4, 4)


def pair_behind(mine, step):
    return lax.rem(mine // 4 + 4 - step // 4, 4) * 4 + lax.rem(lax.rem(mine, 4) + 4 - step % 4, 4)


def holder(pair, z_low, core):
    upper = pair // 8
    z = upper * 2 + lax.rem(z_low + upper, 2)
    return {"seq": z * 16 + lax.rem(pair, 8) * 2 + core}


def attention_peers(seq, core, z_low, mine):
    z_peer = holder(mine, 1 - z_low, core)
    sibling = {"seq": seq + 1 - 2 * core}
    return z_peer, sibling


def greet(mine, z_low, core, z_peer, sibling):
    barrier = pltpu.get_barrier_semaphore()
    for step in range(1, 16):
        pl.semaphore_signal(
            barrier, inc=1, device_id=holder(pair_ahead(mine, step), z_low, core), device_id_type=MESH
        )
    pl.semaphore_signal(barrier, inc=1, device_id=z_peer, device_id_type=MESH)
    pl.semaphore_signal(barrier, inc=1, device_id=sibling, device_id_type=MESH)
    return barrier


def spread_heads(q_ref, k_ref, v_ref, g_ref, x_out, y_out, x_part, y_part, sems):
    seq, core, z_low, mine = spots()
    z_peer, sibling = attention_peers(seq, core, z_low, mine)
    barrier = greet(mine, z_low, core, z_peer, sibling)
    for window in range(2):
        rows = slice(window * 64, window * 64 + 64)
        for head in range(H):
            pair = window * H + head
            y_part[pair, :, 0:LOW] = v_ref[rows, head * VD : head * VD + VD]
            y_part[pair, :, LOW:WIDE] = k_ref[rows, head * KD : head * KD + KD]
    pl.semaphore_wait(barrier, 17)

    def send(source, target, peer, slot):
        return remote(source, target, peer, sems, slot)

    y_sends = []
    for step in range(1, 16):
        pair = pair_ahead(mine, step)
        peer = holder(pair, z_low, core)
        y_sends.append(send(y_part.at[pair], y_out.at[z_low, core, mine], peer, step))
    for window in range(2):
        rows = slice(window * 64, window * 64 + 64)
        for head in range(H):
            pair = window * H + head
            x_part[pair, :, 0:LOW] = g_ref[rows, head * VD : head * VD + VD]
            x_part[pair, :, LOW:WIDE] = q_ref[rows, head * KD : head * KD + KD]
    x_sends = []
    for step in range(1, 16):
        pair = pair_ahead(mine, step)
        peer = holder(pair, z_low, core)
        x_sends.append(send(x_part.at[pair], x_out.at[mine], peer, 16 + step))
    y_out[z_low, core, mine] = y_part[mine]
    x_out[mine] = x_part[mine]
    along = []
    across = []
    for step in range(16):
        if step > 0:
            y_sends[step - 1].wait_recv()
        place = y_out.at[z_low, core, pair_behind(mine, step)]
        along.append(send(place, place, z_peer, 32 + step))
        across.append(send(place, place, sibling, 48 + step))
    for step in range(16):
        along[step].wait_recv()
        place = y_out.at[1 - z_low, core, pair_behind(mine, step)]
        across.append(send(place, place, sibling, 64 + step))
    for copy in x_sends + across:
        copy.wait_recv()
    for copy in y_sends + x_sends + along + across:
        copy.wait_send()


def collect_heads(
    oq_ref, vk_ref, a_ref, gq_ref, gv_ref, gk_ref, oq_got, vk_got, from_core, to_z, from_z, total, sems
):
    seq, core, z_low, mine = spots()
    z_peer, sibling = attention_peers(seq, core, z_low, mine)

    def send(source, target, peer, slot):
        return remote(source, target, peer, sems, 80 + slot)

    groups = [pl.ds(lax.rem(mine // 4 + k, 4) * 4, 4) for k in range(4)]
    across = []
    for far in range(2):
        z_part = 1 - z_low if far == 0 else z_low
        for k in range(4):
            across.append(
                send(
                    vk_ref.at[z_part, 1 - core, groups[k]],
                    from_core.at[far, groups[k]],
                    sibling,
                    4 * far + k,
                )
            )
    oq_sends = []
    for step in range(1, 16):
        pair = pair_ahead(mine, step)
        oq_sends.append(
            send(oq_ref.at[pair], oq_got.at[mine], holder(pair, z_low, core), 16 + step)
        )
    oq_got[mine] = oq_ref[mine]
    along = []
    for k in range(4):
        across[k].wait_recv()
        summed = vk_ref[1 - z_low, core, groups[k]].astype(jnp.float32) + from_core[
            0, groups[k]
        ].astype(jnp.float32)
        to_z[groups[k]] = summed.astype(to_z.dtype)
        along.append(send(to_z.at[groups[k]], from_z.at[groups[k]], z_peer, 8 + k))
    vk_sends = []
    for k in range(4):
        across[4 + k].wait_recv()
        along[k].wait_recv()
        summed = vk_ref[z_low, core, groups[k]].astype(jnp.float32) + from_core[
            1, groups[k]
        ].astype(jnp.float32)
        summed = summed + from_z[groups[k]].astype(jnp.float32)
        total[groups[k]] = summed.astype(total.dtype)
        for step in range(4 * k, 4 * k + 4):
            if step > 0:
                pair = pair_ahead(mine, step)
                vk_sends.append(
                    send(total.at[pair], vk_got.at[mine], holder(pair, z_low, core), 32 + step)
                )
    vk_got[mine] = total[mine]
    for copy in oq_sends:
        copy.wait_recv()
    for window in range(2):
        rows = slice(window * 64, window * 64 + 64)
        for head in range(H):
            pair = window * H + head
            a_ref[rows, head * VD : head * VD + VD] = oq_got[pair, :, 0:LOW]
            gq_ref[rows, head * KD : head * KD + KD] = oq_got[pair, :, LOW:WIDE]
    for copy in vk_sends:
        copy.wait_recv()
    for window in range(2):
        rows = slice(window * 64, window * 64 + 64)
        for head in range(H):
            pair = window * H + head
            gv_ref[rows, head * VD : head * VD + VD] = vk_got[pair, :, 0:LOW]
            gk_ref[rows, head * KD : head * KD + KD] = vk_got[pair, :, LOW:WIDE]
    for copy in across + oq_sends + along + vk_sends:
        copy.wait_send()


def attend_rows(x_ref, y_ref, oq_ref, vk_ref, y_turned, score, slope, total):
    keys = y_turned.shape[1]
    chunks = [slice(start, start + CHUNK) for start in range(0, keys, CHUNK)]

    def key_rows(part):
        quarter = part.start // CHUNK
        return y_ref[quarter // 2, quarter % 2].reshape(CHUNK, WIDE)

    key_scale = KD ** (-0.5)
    for part in chunks:
        y_turned[:, part] = key_rows(part).T
    total[...] = jnp.zeros_like(total)

    def block(index, carry):
        rows = pl.ds(index * 4, 4)
        x_block = x_ref[rows].reshape(QUERY_BLOCK, WIDE)
        wide = x_block.astype(jnp.float32)
        low = lax.broadcasted_iota(jnp.int32, wide.shape, 1) < LOW
        query = jnp.where(low, 0.0, wide).astype(x_block.dtype)
        grad = jnp.where(low, wide, 0.0).astype(x_block.dtype)
        peak = None
        for part in chunks:
            scores = lax.dot_general(key_rows(part), query, SIDE, preferred_element_type=jnp.float32)
            score[part, :] = scores
            top = jnp.max(scores, axis=0, keepdims=True)
            peak = top if peak is None else jnp.maximum(peak, top)
        weight = jnp.zeros((1, QUERY_BLOCK), jnp.float32)
        center = jnp.zeros((1, QUERY_BLOCK), jnp.float32)
        for part in chunks:
            grads = lax.dot_general(key_rows(part), grad, SIDE, preferred_element_type=jnp.float32)
            slope[part, :] = grads
            terms = jnp.exp2((score[part, :] - peak) * (key_scale * 1.4426950408889634))
            score[part, :] = terms
            weight = weight + jnp.sum(terms, axis=0, keepdims=True)
            center = center + jnp.sum(terms * grads, axis=0, keepdims=True)
        share = 1.0 / weight
        center = center * share
        out = jnp.zeros((WIDE, QUERY_BLOCK), jnp.float32)
        back = jnp.zeros((WIDE, QUERY_BLOCK), jnp.float32)
        low_keys = lax.broadcasted_iota(jnp.int32, (CHUNK, WIDE), 1) < LOW
        for part in chunks:
            probs = score[part, :] * share
            prob_low = probs.astype(jnp.bfloat16)
            grads = (probs * (slope[part, :] - center) * key_scale).astype(jnp.bfloat16)
            out = out + jnp.dot(y_turned[:, part], prob_low, preferred_element_type=jnp.float32)
            back = back + jnp.dot(y_turned[:, part], grads, preferred_element_type=jnp.float32)
            for_values = jnp.dot(prob_low, x_block, preferred_element_type=jnp.float32)
            for_keys = jnp.dot(grads, x_block, preferred_element_type=jnp.float32)
            total[part, :] += jnp.where(low_keys, for_values, for_keys)
        low_rows = lax.broadcasted_iota(jnp.int32, out.shape, 0) < LOW
        turned = jnp.where(low_rows, out, back).T
        oq_ref[rows] = turned.reshape(4, 64, WIDE).astype(oq_ref.dtype)
        return carry

    lax.fori_loop(0, x_ref.shape[0] // 4, block, 0)
    vk_ref[...] = total[...].reshape(vk_ref.shape).astype(vk_ref.dtype)


def attention_kernel(
    q_ref, k_ref, v_ref, g_ref, a_ref, gq_ref, gv_ref, gk_ref,
    x_part, y_part, x_got, y_got, y_turned, score, slope, total, oq, vk,
    oq_got, vk_got, from_core, to_z, from_z, summed, send_sem, recv_sem
):
    sems = (send_sem, recv_sem)
    spread_heads(q_ref, k_ref, v_ref, g_ref, x_got, y_got, x_part, y_part, sems)
    attend_rows(x_got, y_got, oq, vk, y_turned, score, slope, total)
    collect_heads(
        oq, vk, a_ref, gq_ref, gv_ref, gk_ref, oq_got, vk_got, from_core, to_z, from_z, summed, sems
    )


def attention(queries, keys, values, grad_out):
    vmem = pl.BlockSpec(memory_space=pltpu.VMEM)
    kind = queries.dtype
    piece = (16, 64, WIDE)
    count = 4 * 16 * 64
    return pl.pallas_call(
        attention_kernel,
        out_shape=[
            jax.ShapeDtypeStruct((ROWS, H * VD), kind),
            jax.ShapeDtypeStruct((ROWS, H * KD), kind),
            jax.ShapeDtypeStruct((ROWS, H * VD), kind),
            jax.ShapeDtypeStruct((ROWS, H * KD), kind),
        ],
        in_specs=[vmem] * 4,
        out_specs=[vmem] * 4,
        scratch_shapes=[
            pltpu.VMEM(piece, kind),
            pltpu.VMEM(piece, kind),
            pltpu.VMEM(piece, kind),
            pltpu.VMEM((2, 2) + piece, kind),
            pltpu.VMEM((WIDE, count), kind),
            pltpu.VMEM((count, QUERY_BLOCK), jnp.float32),
            pltpu.VMEM((count, QUERY_BLOCK), jnp.float32),
            pltpu.VMEM((count, WIDE), jnp.float32),
            pltpu.VMEM(piece, kind),
            pltpu.VMEM((2, 2) + piece, kind),
            pltpu.VMEM(piece, kind),
            pltpu.VMEM(piece, kind),
            pltpu.VMEM((2,) + piece, kind),
            pltpu.VMEM(piece, kind),
            pltpu.VMEM(piece, kind),
            pltpu.VMEM(piece, kind),
            pltpu.SemaphoreType.DMA((128,)),
            pltpu.SemaphoreType.DMA((128,)),
        ],
        compiler_params=pltpu.CompilerParams(
            collective_id=3, has_side_effects=True, vmem_limit_bytes=56 * 1024 * 1024
        ),
        name="attention",
    )(queries, keys, values, grad_out)


def on_device(
    inputs,
    conv_weight,
    mix_weight,
    first_gain,
    first_bias,
    second_gain,
    second_bias,
    norm_gain,
    query_weight,
    key_weight,
    value_weight,
    out_weight,
    cotangent,
):
    windows_here, local_bins, model_width = inputs.shape
    devices = lax.axis_size("seq")
    local_count = windows_here * local_bins
    total_rows = local_count * devices * lax.axis_size("batch")
    rows_in = inputs.reshape(local_count, model_width)
    inputs_flat = rows_in.astype(jnp.float32)
    cot_flat = cotangent.reshape(local_count, model_width)
    gain_one, bias_one = first_gain[None, :], first_bias[None, :]
    conv_full, mix_full, hidden, stats_one, stats_two, grad_out = front(
        rows_in, conv_weight, mix_weight, gain_one, bias_one, cot_flat, out_weight
    )
    sum_two, square_two = stats_two[0], stats_two[1]
    mean_two = sum_two / total_rows
    scale_two = lax.rsqrt(square_two / total_rows - mean_two * mean_two + EPS)
    hat_two = (hidden - mean_two) * scale_two
    pre_two = hat_two * second_gain + second_bias
    act_two = gelu_value(pre_two).astype(jnp.bfloat16)
    mixed_rows = inputs_flat + jnp.dot(act_two, mix_full, preferred_element_type=jnp.float32)
    trunk_rows = rounded(mixed_rows)
    row_mean = jnp.mean(trunk_rows, axis=-1, keepdims=True)
    centered = trunk_rows - row_mean
    row_scale = lax.rsqrt(jnp.mean(centered * centered, axis=-1, keepdims=True) + EPS)
    row_hat = centered * row_scale
    normed = (row_hat * norm_gain).astype(jnp.bfloat16)
    queries = jnp.dot(normed, query_weight, preferred_element_type=jnp.float32).astype(jnp.bfloat16)
    keys_local = jnp.dot(normed, key_weight, preferred_element_type=jnp.float32).astype(
        jnp.bfloat16
    )
    values_local = jnp.dot(normed, value_weight, preferred_element_type=jnp.float32).astype(
        jnp.bfloat16
    )
    attended_rows, grad_query_rows, grad_value_rows, grad_key_rows = attention(
        queries, keys_local, values_local, grad_out
    )
    encoded = (
        (trunk_rows + jnp.dot(attended_rows, out_weight, preferred_element_type=jnp.float32))
        .astype(jnp.bfloat16)
        .reshape(windows_here, local_bins, model_width)
    )
    grad_normed = jnp.dot(grad_query_rows, query_weight.T, preferred_element_type=jnp.float32)
    grad_normed = grad_normed + jnp.dot(
        grad_key_rows, key_weight.T, preferred_element_type=jnp.float32
    )
    grad_normed = grad_normed + jnp.dot(
        grad_value_rows, value_weight.T, preferred_element_type=jnp.float32
    )
    norm_gain_part = jnp.sum(grad_normed * row_hat, axis=0)
    grad_hat = grad_normed * norm_gain
    grad_trunk = row_scale * (
        grad_hat
        - jnp.mean(grad_hat, axis=-1, keepdims=True)
        - row_hat * jnp.mean(grad_hat * row_hat, axis=-1, keepdims=True)
    )
    grad_mixed = cot_flat.astype(jnp.float32) + grad_trunk
    grad_low = grad_mixed.astype(jnp.bfloat16)
    grad_act_two = jnp.dot(grad_low, mix_full.T, preferred_element_type=jnp.float32)
    grad_pre_two = grad_act_two * gelu_slope(pre_two)
    grad_rows, sums_two, sums_one = tail(
        grad_pre_two,
        hat_two,
        (second_gain * scale_two)[None, :],
        norm_gain_part.reshape(2, -1),
        rows_in,
        stats_one,
        gain_one,
        bias_one,
        grad_mixed,
        conv_full,
    )
    grad_inputs = grad_rows.reshape(windows_here, local_bins, model_width)
    grad_second_bias, grad_second_gain = sums_two[0], sums_two[1]
    grad_norm_gain = sums_two[2:4].reshape(-1)
    grad_first_bias, grad_first_gain = sums_one[0], sums_one[1]
    return (
        encoded,
        grad_inputs,
        grad_first_gain,
        grad_first_bias,
        grad_second_gain,
        grad_second_bias,
        grad_norm_gain,
    )


def solution(mesh):
    in_specs = (
        P("batch", "seq", None),
        P("seq", None),
        P("seq", None),
        P(),
        P(),
        P(),
        P(),
        P(),
        P(),
        P(),
        P(),
        P(),
        P("batch", "seq", None),
    )
    out_specs = (P("batch", "seq", None), P("batch", "seq", None), P(), P(), P(), P(), P())
    return jax.shard_map(
        on_device, mesh=mesh, in_specs=in_specs, out_specs=out_specs, check_vma=False
    )
```

```python
import jax
import jax.numpy as jnp
from jax import lax
from jax.experimental import pallas as pl
from jax.experimental.pallas import tpu as pltpu
from jax.sharding import PartitionSpec as P

H = 8
KD = 64
VD = 192
DILATION_STEP = 16


EPS = 1e-05
GELU_C = 0.7978845608028654


MESH = pl.DeviceIdType.MESH
ROWS = 128
LINE = 8
PLANE = 16
TAP_PARTS = ((0, 0, 0, 768), (1, 0, 768, 384), (1, 1, 0, 384), (2, 1, 384, 768))


def seq_of(z, y, x, core):
    return ((z * 4 + y) * 2 + x) * 2 + core


def remote(source, target, peer, sems, slot):
    copy = pltpu.make_async_remote_copy(
        src_ref=source,
        dst_ref=target,
        send_sem=sems[0].at[slot],
        recv_sem=sems[1].at[slot],
        device_id=peer,
        device_id_type=MESH,
    )
    copy.start()
    return copy


def line_place():
    return lax.axis_index("batch") * 4 + lax.rem(lax.axis_index("seq"), 4)


def line_peer(step):
    other = lax.rem(line_place() + step, LINE)
    spot = lax.axis_index("seq") // 4
    return {"seq": spot * 4 + lax.rem(other, 4), "batch": other // 4}


def plane_peer(step):
    seq = lax.axis_index("seq")
    return {"seq": lax.rem(seq // 4 + step, PLANE) * 4 + lax.rem(seq, 4)}


def ring_peer(step):
    count = 4 * PLANE
    return {"seq": lax.rem(lax.axis_index("seq") + step + count, count)}


def greet_all():
    barrier = pltpu.get_barrier_semaphore()
    peers = [line_peer(step) for step in range(1, LINE)]
    peers += [plane_peer(step) for step in range(1, PLANE)]
    peers += [ring_peer(1), ring_peer(-1)]
    for peer in peers:
        pl.semaphore_signal(barrier, inc=1, device_id=peer, device_id_type=MESH)
    return barrier, len(peers)


def line_send(line, sems, base):
    place = line.at[line_place()]
    return [remote(place, place, line_peer(step), sems, base + step) for step in range(1, LINE)]


def plane_send(line, plane, arrivals, sems, base):
    for copy in arrivals:
        copy.wait_recv()
    total = line[0]
    for i in range(1, LINE):
        total = total + line[i]
    spot = lax.axis_index("seq") // 4
    plane[spot] = total
    place = plane.at[spot]
    return [
        remote(place, place, plane_peer(step), sems, base + LINE + step) for step in range(1, PLANE)
    ]


def plane_sum(plane, arrivals):
    for copy in arrivals:
        copy.wait_recv()
    total = plane[0]
    for i in range(1, PLANE):
        total = total + plane[i]
    return total


def halo_send(middle, low, high, sems, base):
    return [
        remote(middle.at[:, 48:64, :], low, ring_peer(1), sems, (base, 0)),
        remote(middle.at[:, 0:16, :], high, ring_peer(-1), sems, (base, 1)),
    ]


def halo_fill(padded, low, high, copies):
    seq = lax.axis_index("seq")
    last = lax.axis_size("seq") - 1
    for copy in copies:
        copy.wait_recv()
    low_rows = low[...].astype(jnp.float32)
    high_rows = high[...].astype(jnp.float32)
    padded[:, 0:16, :] = jnp.where(seq == 0, 0.0, low_rows).astype(padded.dtype)
    padded[:, 80:96, :] = jnp.where(seq == last, 0.0, high_rows).astype(padded.dtype)


def tap_rows(padded, start):
    return jnp.concatenate([padded[0, start : start + 64, :], padded[1, start : start + 64, :]], axis=0)


def stacked(rows):
    return jnp.concatenate([jnp.sum(part, axis=0, keepdims=True) for part in rows], axis=0)


def gelu_value(values):
    cubic = GELU_C * (values + 0.044715 * values * values * values)
    return 0.5 * values * (1.0 + jnp.tanh(cubic))


def gelu_slope(values):
    tangent = jnp.tanh(GELU_C * (values + 0.044715 * values * values * values))
    return 0.5 * (1.0 + tangent) + 0.5 * values * (1.0 - tangent * tangent) * GELU_C * (
        1.0 + 3.0 * 0.044715 * values * values
    )


def rounded(values):
    return lax.optimization_barrier(values.astype(jnp.bfloat16)).astype(jnp.float32)


CHUNK = 1024
QUERY_BLOCK = 256
SIDE = (((1,), (1,)), ((), ()))
def front_kernel(
    x_from, conv_from, mix_from, gain_ref, bias_ref, cot_from, out_weight_ref,
    conv_out, mix_out, hidden_out, stats_one_out, stats_two_out, grad_out,
    line_one, plane_one, line_two, plane_two, conv_other, mix_other, mix_land, middle, padded,
    low, high, weight, x_ref, conv_ref, mix_ref, cot_ref, sum_send, sum_recv, move_send, move_recv, own_sem
):
    seq = lax.axis_index("seq")
    core = lax.rem(seq, 2)
    x = lax.rem(seq // 2, 2)
    y = lax.rem(seq // 4, 4)
    z = seq // 16
    sums = (sum_send, sum_recv)
    moves = (move_send, move_recv)
    total_rows = ROWS * lax.axis_size("seq") * lax.axis_size("batch")
    barrier, count = greet_all()
    loads = [
        pltpu.make_async_copy(source, target, own_sem.at[i])
        for i, (source, target) in enumerate(
            (
                (x_from, x_ref),
                (conv_from, conv_ref),
                (mix_from, mix_ref),
                (cot_from, cot_ref),
                (out_weight_ref, weight),
            )
        )
    ]
    for load in loads:
        load.start()
    loads[0].wait()
    values = x_ref[...].astype(jnp.float32)
    line_one[line_place()] = stacked([values, values * values])
    pl.semaphore_wait(barrier, count)

    def first_peer(step):
        return {"seq": seq_of(lax.rem(z + step * x, 4), lax.rem(y + step * (1 - x), 4), x, core)}

    def second_peer(step):
        return {"seq": seq_of(lax.rem(z + step * (1 - x), 4), lax.rem(y + step * x, 4), x, core)}

    def y_peer(step):
        return {"seq": seq_of(z, lax.rem(y + step, 4), x, core)}

    def z_peer(step):
        return {"seq": seq_of(lax.rem(z + step, 4), y, x, core)}

    x_peer = {"seq": seq_of(z, y, 1 - x, core)}
    sibling = {"seq": seq_of(z, y, x, 1 - core)}
    outs = (conv_out, mix_land)
    widths = (conv_ref.shape[1] // 2, mix_ref.shape[1] // 2)
    halves = [pl.ds(pl.multiple_of(core * w, w), w) for w in widths]
    far_halves = [pl.ds(pl.multiple_of((1 - core) * w, w), w) for w in widths]

    def move(kind, where, peer, slot):
        place = outs[kind].at[(core, *where)]
        return remote(place, place, peer, moves, (slot, kind))

    started = line_send(line_one, sums, 0)
    line_started = started
    pair_up = [
        remote(conv_from.at[:, far_halves[0]], conv_other, sibling, moves, (0, 0)),
        remote(mix_from.at[:, far_halves[1]], mix_other, sibling, moves, (0, 1)),
    ]
    started = started + pair_up
    for kind, mine, other in ((0, conv_ref, conv_other), (1, mix_ref, mix_other)):
        loads[1 + kind].wait()
        pair_up[kind].wait_recv()
        out = outs[kind]
        here = mine[:, halves[kind]].astype(jnp.float32)
        there = other[...].astype(jnp.float32)
        upper = jnp.where(core == 0, here, there)
        lower = jnp.where(core == 0, there, here)
        out[core, z, y, x] = jnp.concatenate([upper, lower], axis=0).astype(out.dtype)
    to_x = [move(kind, (z, y, x), x_peer, 1) for kind in range(2)]
    spread_out = []
    for kind in range(2):
        for step in (1, 3):
            spread_out.append(move(kind, (z, y, x), first_peer(step), 1 + step))
    plane_started = plane_send(line_one, plane_one, line_started, sums, 0)
    for copy in to_x:
        copy.wait_recv()
    for kind in range(2):
        for step in (1, 3):
            spread_out.append(move(kind, (z, y, 1 - x), second_peer(step), 4 + step))
    first_block, second_block = spread_out[:4], spread_out[4:]
    for kind, step, back in ((0, 1, 3), (1, 3, 1)):
        first_block[2 * kind + step // 2].wait_recv()
        place = (lax.rem(z + back * x, 4), lax.rem(y + back * (1 - x), 4), x)
        spread_out.append(move(kind, place, first_peer(step), 3))
    total = plane_sum(plane_one, plane_started)
    mean = total[0:1, :] / total_rows
    scale = lax.rsqrt(total[1:2, :] / total_rows - mean * mean + EPS)
    stats_one_out[...] = jnp.concatenate([mean, scale], axis=0)
    pre = (values - mean) * scale * gain_ref[...][None, :] + bias_ref[...][None, :]
    active = gelu_value(pre).astype(middle.dtype)
    for window in range(2):
        middle[window] = active[window * 64 : window * 64 + 64, :]
        padded[window, 16:80, :] = active[window * 64 : window * 64 + 64, :]
    halos = halo_send(middle, low, high, moves, 19)
    for kind, step, back in ((0, 1, 3), (1, 3, 1)):
        second_block[2 * kind + step // 2].wait_recv()
        place = (lax.rem(z + back * (1 - x), 4), lax.rem(y + back * x, 4), 1 - x)
        spread_out.append(move(kind, place, second_peer(step), 6))
    waited = (first_block[0], first_block[3], second_block[0], second_block[3])
    for copy in spread_out:
        if all(copy is not other for other in waited):
            copy.wait_recv()
    whole = slice(None)
    blocks = [[], []]
    across = [[], []]

    def launch(kind):
        for step in (1, 3):
            blocks[kind].append(move(kind, (z, whole, 0), z_peer(step), 7 + step))
            blocks[kind].append(move(kind, (whole, y, 1), y_peer(step), 10 + step))
        across[kind].append(move(kind, (z, whole, 0), sibling, 14))
        across[kind].append(move(kind, (whole, y, 1), sibling, 15))

    def relay(kind):
        for i, (step, part) in enumerate(((1, slice(0, 2)), (3, slice(2, 4)))):
            from_z, from_y = lax.rem(z + 4 - step, 4), lax.rem(y + 4 - step, 4)
            blocks[kind][2 * i].wait_recv()
            blocks[kind].append(move(kind, (from_z, part, 0), z_peer(step), 9 if i == 0 else 24))
            blocks[kind][2 * i + 1].wait_recv()
            blocks[kind].append(move(kind, (part, from_y, 1), y_peer(step), 12 if i == 0 else 25))
            across[kind].append(move(kind, (from_z, whole, 0), sibling, 15 + step))
            across[kind].append(move(kind, (whole, from_y, 1), sibling, 20 + step))

    def finish(kind):
        blocks[kind][4].wait_recv()
        blocks[kind][6].wait_recv()
        across[kind].append(move(kind, (lax.rem(z + 2, 4), whole, 0), sibling, 17))
        blocks[kind][5].wait_recv()
        blocks[kind][7].wait_recv()
        across[kind].append(move(kind, (whole, lax.rem(y + 2, 4), 1), sibling, 22))

    launch(0)
    loads[3].wait()
    loads[4].wait()
    grad_out[...] = lax.dot_general(
        cot_ref[...], weight[...], SIDE, preferred_element_type=jnp.float32
    ).astype(grad_out.dtype)
    halo_fill(padded, low, high, halos)

    relay(0)
    launch(1)
    finish(0)
    for copy in across[0]:
        copy.wait_recv()
    terms = {}
    for tap, half, start, size in TAP_PARTS:
        part = conv_out[half, :, :, :, :, start : start + size].reshape(-1, size)
        terms[tap, half] = jnp.dot(tap_rows(padded, 16 * tap), part, preferred_element_type=jnp.float32)
    middle_tap = jnp.concatenate([terms[1, 0], terms[1, 1]], axis=1)
    hidden = terms[0, 0] + middle_tap + terms[2, 1]
    hidden_out[...] = hidden
    line_two[line_place()] = stacked([hidden, hidden * hidden])
    line_again = line_send(line_two, sums, LINE + PLANE)
    relay(1)
    plane_again = plane_send(line_two, plane_two, line_again, sums, LINE + PLANE)
    finish(1)
    for copy in across[1]:
        copy.wait_recv()
    for i in range(4):
        for j in range(4):
            start = (i * 4 + j) * 48
            for half in range(2):
                pair = [mix_land[half, i, j, k].astype(jnp.float32) for k in range(2)]
                columns = slice(half * widths[1], half * widths[1] + widths[1])
                mix_out[start : start + 48, columns] = jnp.concatenate(pair, axis=0).astype(mix_out.dtype)
    stats_two_out[...] = plane_sum(plane_two, plane_again)
    ended = started + to_x + spread_out + halos + plane_started + line_again + plane_again
    for kind in range(2):
        ended += blocks[kind] + across[kind]
    for copy in ended:
        copy.wait_send()


def front(inputs, conv_weight, mix_weight, gain, bias, cot, out_weight):
    vmem = pl.BlockSpec(memory_space=pltpu.VMEM)
    anywhere = pl.BlockSpec(memory_space=pl.ANY)
    width = inputs.shape[1]
    mid_width = conv_weight.shape[1] // 3
    kind = inputs.dtype
    conv_rows, mix_rows = conv_weight.shape[0], mix_weight.shape[0]
    full, wide = jnp.float32, conv_weight.shape[1]
    sems = 2 * (LINE + PLANE)
    conv_full, *rest = pl.pallas_call(
        front_kernel,
        out_shape=[
            jax.ShapeDtypeStruct((2, 4, 4, 2, 2 * conv_rows, wide // 2), kind),
            jax.ShapeDtypeStruct((64 * mix_rows, width), kind),
            jax.ShapeDtypeStruct((ROWS, mid_width), full),
            jax.ShapeDtypeStruct((2, width), full),
            jax.ShapeDtypeStruct((2, mid_width), full),
            jax.ShapeDtypeStruct((ROWS, out_weight.shape[0]), kind),
        ],
        in_specs=[anywhere] * 3 + [vmem] * 2 + [anywhere] * 2,
        out_specs=[vmem] * 6,
        scratch_shapes=[
            pltpu.VMEM((LINE, 2, width), full),
            pltpu.VMEM((PLANE, 2, width), full),
            pltpu.VMEM((LINE, 2, mid_width), full),
            pltpu.VMEM((PLANE, 2, mid_width), full),
            pltpu.VMEM((conv_rows, wide // 2), kind),
            pltpu.VMEM((mix_rows, width // 2), kind),
            pltpu.VMEM((2, 4, 4, 2, 2 * mix_rows, width // 2), kind),
            pltpu.VMEM((2, 64, width), kind),
            pltpu.VMEM((2, 96, width), kind),
            pltpu.VMEM((2, 16, width), kind),
            pltpu.VMEM((2, 16, width), kind),
            pltpu.VMEM(out_weight.shape, kind),
            pltpu.VMEM(inputs.shape, kind),
            pltpu.VMEM(conv_weight.shape, kind),
            pltpu.VMEM(mix_weight.shape, kind),
            pltpu.VMEM(cot.shape, kind),
            pltpu.SemaphoreType.DMA((sems,)),
            pltpu.SemaphoreType.DMA((sems,)),
            pltpu.SemaphoreType.DMA((26, 2)),
            pltpu.SemaphoreType.DMA((26, 2)),
            pltpu.SemaphoreType.DMA((5,)),
        ],
        compiler_params=pltpu.CompilerParams(
            collective_id=1, has_side_effects=True, vmem_limit_bytes=48 * 1024 * 1024
        ),
        name="front",
    )(inputs, conv_weight, mix_weight, gain, bias, cot, out_weight)
    return [conv_full.reshape(2, -1, wide // 2)] + rest


LOW = VD
WIDE = VD + KD


def spots():
    seq = lax.axis_index("seq")
    core = lax.rem(seq, 2)
    z = seq // 16
    mine = (z // 2) * 8 + lax.rem(seq // 2, 8)
    return seq, core, lax.rem(z + z // 2, 2), mine


def pair_ahead(mine, step):
    return lax.rem(mine // 4 + step // 4, 4) * 4 + lax.rem(lax.rem(mine, 4) + step % 4, 4)


def pair_behind(mine, step):
    return lax.rem(mine // 4 + 4 - step // 4, 4) * 4 + lax.rem(lax.rem(mine, 4) + 4 - step % 4, 4)


def holder(pair, z_low, core):
    upper = pair // 8
    z = upper * 2 + lax.rem(z_low + upper, 2)
    return {"seq": z * 16 + lax.rem(pair, 8) * 2 + core}


def attention_peers(seq, core, z_low, mine):
    z_peer = holder(mine, 1 - z_low, core)
    sibling = {"seq": seq + 1 - 2 * core}
    return z_peer, sibling


def greet_attention(barrier):
    seq, core, z_low, mine = spots()
    peers = [holder(pair_ahead(mine, step), z_low, core) for step in range(1, 16)]
    peers += attention_peers(seq, core, z_low, mine)
    for peer in peers:
        pl.semaphore_signal(barrier, inc=1, device_id=peer, device_id_type=MESH)
    return len(peers)


def spread_heads(q_ref, k_ref, v_ref, g_ref, x_out, y_out, x_part, y_part, sems, meanwhile):
    seq, core, z_low, mine = spots()
    z_peer, sibling = attention_peers(seq, core, z_low, mine)
    for window in range(2):
        rows = slice(window * 64, window * 64 + 64)
        for head in range(H):
            pair = window * H + head
            y_part[pair, :, 0:LOW] = v_ref[rows, head * VD : head * VD + VD]
            y_part[pair, :, LOW:WIDE] = k_ref[rows, head * KD : head * KD + KD]

    def send(source, target, peer, slot):
        return remote(source, target, peer, sems, slot)

    y_sends = []
    for step in range(1, 16):
        pair = pair_ahead(mine, step)
        peer = holder(pair, z_low, core)
        y_sends.append(send(y_part.at[pair], y_out.at[z_low, core, mine], peer, step))
    for window in range(2):
        rows = slice(window * 64, window * 64 + 64)
        for head in range(H):
            pair = window * H + head
            x_part[pair, :, 0:LOW] = g_ref[rows, head * VD : head * VD + VD]
            x_part[pair, :, LOW:WIDE] = q_ref[rows, head * KD : head * KD + KD]
    x_sends = []
    for step in range(1, 16):
        pair = pair_ahead(mine, step)
        peer = holder(pair, z_low, core)
        x_sends.append(send(x_part.at[pair], x_out.at[mine], peer, 16 + step))
    y_out[z_low, core, mine] = y_part[mine]
    x_out[mine] = x_part[mine]
    along = []
    across = []
    for step in range(16):
        if step > 0:
            y_sends[step - 1].wait_recv()
        place = y_out.at[z_low, core, pair_behind(mine, step)]
        along.append(send(place, place, z_peer, 32 + step))
        across.append(send(place, place, sibling, 48 + step))
    meanwhile()
    for step in range(16):
        along[step].wait_recv()
        place = y_out.at[1 - z_low, core, pair_behind(mine, step)]
        across.append(send(place, place, sibling, 64 + step))
    for copy in x_sends + across:
        copy.wait_recv()
    for copy in y_sends + x_sends + along + across:
        copy.wait_send()


def collect_heads(
    oq_ref, vk_ref, a_ref, gq_ref, gv_ref, gk_ref, oq_got, vk_got, from_core, to_z, from_z, total, sems,
    meanwhile
):
    seq, core, z_low, mine = spots()
    z_peer, sibling = attention_peers(seq, core, z_low, mine)

    def send(source, target, peer, slot):
        return remote(source, target, peer, sems, 80 + slot)

    groups = [pl.ds(lax.rem(mine // 4 + k, 4) * 4, 4) for k in range(4)]
    across = []
    for far in range(2):
        z_part = 1 - z_low if far == 0 else z_low
        for k in range(4):
            across.append(
                send(
                    vk_ref.at[z_part, 1 - core, groups[k]],
                    from_core.at[far, groups[k]],
                    sibling,
                    4 * far + k,
                )
            )
    oq_sends = []
    for step in range(1, 16):
        pair = pair_ahead(mine, step)
        oq_sends.append(
            send(oq_ref.at[pair], oq_got.at[mine], holder(pair, z_low, core), 16 + step)
        )
    oq_got[mine] = oq_ref[mine]
    along = []
    for k in range(4):
        across[k].wait_recv()
        summed = vk_ref[1 - z_low, core, groups[k]].astype(jnp.float32) + from_core[
            0, groups[k]
        ].astype(jnp.float32)
        to_z[groups[k]] = summed.astype(to_z.dtype)
        along.append(send(to_z.at[groups[k]], from_z.at[groups[k]], z_peer, 8 + k))
    vk_sends = []
    for k in range(4):
        across[4 + k].wait_recv()
        along[k].wait_recv()
        summed = vk_ref[z_low, core, groups[k]].astype(jnp.float32) + from_core[
            1, groups[k]
        ].astype(jnp.float32)
        summed = summed + from_z[groups[k]].astype(jnp.float32)
        total[groups[k]] = summed.astype(total.dtype)
        for step in range(4 * k, 4 * k + 4):
            if step > 0:
                pair = pair_ahead(mine, step)
                vk_sends.append(
                    send(total.at[pair], vk_got.at[mine], holder(pair, z_low, core), 32 + step)
                )
    vk_got[mine] = total[mine]
    for copy in oq_sends:
        copy.wait_recv()
    for window in range(2):
        rows = slice(window * 64, window * 64 + 64)
        for head in range(H):
            pair = window * H + head
            a_ref[rows, head * VD : head * VD + VD] = oq_got[pair, :, 0:LOW]
            gq_ref[rows, head * KD : head * KD + KD] = oq_got[pair, :, LOW:WIDE]
    meanwhile()
    for copy in vk_sends:
        copy.wait_recv()
    for window in range(2):
        rows = slice(window * 64, window * 64 + 64)
        for head in range(H):
            pair = window * H + head
            gv_ref[rows, head * VD : head * VD + VD] = vk_got[pair, :, 0:LOW]
            gk_ref[rows, head * KD : head * KD + KD] = vk_got[pair, :, LOW:WIDE]
    for copy in across + oq_sends + along + vk_sends:
        copy.wait_send()


def attend_rows(x_ref, y_ref, oq_ref, vk_ref, y_turned, score, slope, total):
    keys = y_turned.shape[1]
    chunks = [slice(start, start + CHUNK) for start in range(0, keys, CHUNK)]

    def key_rows(part):
        quarter = part.start // CHUNK
        return y_ref[quarter // 2, quarter % 2].reshape(CHUNK, WIDE)

    key_scale = KD ** (-0.5)
    for part in chunks:
        y_turned[:, part] = key_rows(part).T
    total[...] = jnp.zeros_like(total)

    def block(index, carry):
        rows = pl.ds(index * 4, 4)
        x_block = x_ref[rows].reshape(QUERY_BLOCK, WIDE)
        wide = x_block.astype(jnp.float32)
        low = lax.broadcasted_iota(jnp.int32, wide.shape, 1) < LOW
        query = jnp.where(low, 0.0, wide).astype(x_block.dtype)
        grad = jnp.where(low, wide, 0.0).astype(x_block.dtype)
        peak = None
        for part in chunks:
            scores = lax.dot_general(key_rows(part), query, SIDE, preferred_element_type=jnp.float32)
            score[part, :] = scores
            top = jnp.max(scores, axis=0, keepdims=True)
            peak = top if peak is None else jnp.maximum(peak, top)
        weight = jnp.zeros((1, QUERY_BLOCK), jnp.float32)
        center = jnp.zeros((1, QUERY_BLOCK), jnp.float32)
        for part in chunks:
            grads = lax.dot_general(key_rows(part), grad, SIDE, preferred_element_type=jnp.float32)
            slope[part, :] = grads
            terms = jnp.exp2((score[part, :] - peak) * (key_scale * 1.4426950408889634))
            score[part, :] = terms
            weight = weight + jnp.sum(terms, axis=0, keepdims=True)
            center = center + jnp.sum(terms * grads, axis=0, keepdims=True)
        share = 1.0 / weight
        center = center * share
        out = jnp.zeros((WIDE, QUERY_BLOCK), jnp.float32)
        back = jnp.zeros((WIDE, QUERY_BLOCK), jnp.float32)
        low_keys = lax.broadcasted_iota(jnp.int32, (CHUNK, WIDE), 1) < LOW
        for part in chunks:
            probs = score[part, :] * share
            prob_low = probs.astype(jnp.bfloat16)
            grads = (probs * (slope[part, :] - center) * key_scale).astype(jnp.bfloat16)
            out = out + jnp.dot(y_turned[:, part], prob_low, preferred_element_type=jnp.float32)
            back = back + jnp.dot(y_turned[:, part], grads, preferred_element_type=jnp.float32)
            for_values = jnp.dot(prob_low, x_block, preferred_element_type=jnp.float32)
            for_keys = jnp.dot(grads, x_block, preferred_element_type=jnp.float32)
            total[part, :] += jnp.where(low_keys, for_values, for_keys)
        low_rows = lax.broadcasted_iota(jnp.int32, out.shape, 0) < LOW
        turned = jnp.where(low_rows, out, back).T
        oq_ref[rows] = turned.reshape(4, 64, WIDE).astype(oq_ref.dtype)
        return carry

    lax.fori_loop(0, x_ref.shape[0] // 4, block, 0)
    vk_ref[...] = total[...].reshape(vk_ref.shape).astype(vk_ref.dtype)


def back_kernel(
    x_ref, hidden_ref, stats_one_ref, stats_two_ref, gain_two_ref, bias_two_ref, norm_ref,
    gain_ref, bias_ref, g_ref, cot_ref, mix_from, q_from, k_from, v_from, o_from, conv_from,
    encoded_out, out_ref, sums_two_out, sums_one_out,
    mix, q_weight, k_weight, v_weight, o_weight, weight,
    hat_two, slope_two, trunk, row_hat, mixed, hat_one, slope_one, q_rows, k_rows, v_rows,
    a_rows, gq_rows, gv_rows, gk_rows,
    x_part, y_part, x_got, y_got, y_turned, score, slope, total_vk, oq, vk,
    oq_got, vk_got, from_core, to_z, from_z, summed,
    line_two, plane_two, line_one, plane_one, middle, padded, low, high,
    head_send, head_recv, sum_send, sum_recv, move_send, move_recv, own_sem
):
    heads = (head_send, head_recv)
    sums = (sum_send, sum_recv)
    moves = (move_send, move_recv)
    total_rows = ROWS * lax.axis_size("seq") * lax.axis_size("batch")
    kind = x_ref.dtype
    full = jnp.float32
    barrier, count = greet_all()
    count += greet_attention(barrier)
    loads = [
        pltpu.make_async_copy(source, target, own_sem.at[i])
        for i, (source, target) in enumerate(
            (
                (mix_from, mix),
                (q_from, q_weight),
                (k_from, k_weight),
                (v_from, v_weight),
                (o_from, o_weight),
                (conv_from, weight),
            )
        )
    ]
    for load in loads:
        load.start()
    mean_two = stats_two_ref[0:1, :] / total_rows
    scale_two = lax.rsqrt(stats_two_ref[1:2, :] / total_rows - mean_two * mean_two + EPS)
    hat = (hidden_ref[...] - mean_two) * scale_two
    pre = hat * gain_two_ref[...][None, :] + bias_two_ref[...][None, :]
    hat_two[...] = hat
    loads[0].wait()
    trunk[...] = (
        x_ref[...].astype(full)
        + jnp.dot(gelu_value(pre).astype(kind), mix[...], preferred_element_type=full)
    ).astype(kind)
    rows = trunk[...].astype(full)
    centered = rows - jnp.mean(rows, axis=-1, keepdims=True)
    row_scale = lax.rsqrt(jnp.mean(centered * centered, axis=-1, keepdims=True) + EPS)
    row_hat[...] = centered * row_scale
    norm_gain = norm_ref[...][None, :]
    normed = (row_hat[...] * norm_gain).astype(kind)
    for load, table, place in (
        (loads[3], v_weight, v_rows),
        (loads[2], k_weight, k_rows),
        (loads[1], q_weight, q_rows),
    ):
        load.wait()
        place[...] = jnp.dot(normed, table[...], preferred_element_type=full).astype(kind)
    pl.semaphore_wait(barrier, count)

    mean, scale = stats_one_ref[0:1, :], stats_one_ref[1:2, :]
    gain_one = gain_ref[...][None, :]

    def recall():
        slope_two[...] = gelu_slope(hat_two[...] * gain_two_ref[...][None, :] + bias_two_ref[...][None, :])
        hat_one[...] = (x_ref[...].astype(full) - mean) * scale
        slope_one[...] = gelu_slope(hat_one[...] * gain_one + bias_ref[...][None, :])

    def encode():
        loads[4].wait()
        encoded_out[...] = (
            trunk[...].astype(full) + jnp.dot(a_rows[...], o_weight[...], preferred_element_type=full)
        ).astype(kind)
        mixed[...] = lax.dot_general(gq_rows[...], q_weight[...], SIDE, preferred_element_type=full)

    spread_heads(q_rows, k_rows, v_rows, g_ref, x_got, y_got, x_part, y_part, heads, recall)
    attend_rows(x_got, y_got, oq, vk, y_turned, score, slope, total_vk)
    collect_heads(
        oq, vk, a_rows, gq_rows, gv_rows, gk_rows, oq_got, vk_got, from_core, to_z, from_z, summed,
        heads, encode
    )
    grad_normed = (
        mixed[...]
        + lax.dot_general(gk_rows[...], k_weight[...], SIDE, preferred_element_type=full)
        + lax.dot_general(gv_rows[...], v_weight[...], SIDE, preferred_element_type=full)
    )
    hats = row_hat[...]
    norm_part = jnp.sum(grad_normed * hats, axis=0, keepdims=True)
    grad_hat = grad_normed * norm_gain
    mixed[...] = cot_ref[...].astype(full) + row_scale * (
        grad_hat
        - jnp.mean(grad_hat, axis=-1, keepdims=True)
        - hats * jnp.mean(grad_hat * hats, axis=-1, keepdims=True)
    )
    grad_two = (
        lax.dot_general(mixed[...].astype(kind), mix[...], SIDE, preferred_element_type=full)
        * slope_two[...]
    )
    mid_width = grad_two.shape[1]
    place = line_place()
    line_two[place] = jnp.concatenate(
        [
            jnp.sum(grad_two, axis=0, keepdims=True),
            jnp.sum(grad_two * hat_two[...], axis=0, keepdims=True),
            norm_part[:, :mid_width],
            norm_part[:, mid_width:],
        ],
        axis=0,
    )
    started = line_send(line_two, sums, 0)
    plane_started = plane_send(line_two, plane_two, started, sums, 0)
    total = plane_sum(plane_two, plane_started)
    sums_two_out[...] = total
    hidden_grad = (
        gain_two_ref[...][None, :]
        * scale_two
        * (grad_two - total[0:1, :] / total_rows - hat_two[...] * total[1:2, :] / total_rows)
    ).astype(kind)
    for window in range(2):
        middle[window] = hidden_grad[window * 64 : window * 64 + 64, :]
        padded[window, 16:80, :] = hidden_grad[window * 64 : window * 64 + 64, :]
    halos = halo_send(middle, low, high, moves, 0)
    loads[5].wait()
    grad_act = None
    for tap, half, start, size in (TAP_PARTS[1], TAP_PARTS[2], TAP_PARTS[0], TAP_PARTS[3]):
        if tap == 0:
            halo_fill(padded, low, high, halos)
        first = 0 if half == 0 or tap == 2 else 384
        term = lax.dot_general(
            tap_rows(padded, 16 * (2 - tap))[:, first : first + size],
            weight[half, :, start : start + size],
            SIDE,
            preferred_element_type=jnp.float32,
        )
        grad_act = term if grad_act is None else grad_act + term
    grad_pre = grad_act * slope_one[...]
    line_one[place] = stacked([grad_pre, grad_pre * hat_one[...]])
    line_again = line_send(line_one, sums, LINE + PLANE)
    plane_again = plane_send(line_one, plane_one, line_again, sums, LINE + PLANE)
    total = plane_sum(plane_one, plane_again)
    sums_one_out[...] = total
    grad_rows = (
        gain_one
        * scale
        * (grad_pre - total[0:1, :] / total_rows - hat_one[...] * total[1:2, :] / total_rows)
    )
    out_ref[...] = (mixed[...] + grad_rows).astype(out_ref.dtype)
    for copy in started + plane_started + halos + line_again + plane_again:
        copy.wait_send()


def back(
    rows_in, hidden, stats_one, stats_two, gain_two, bias_two, norm_gain, gain_one, bias_one,
    grad_out, cot, mix_full, query_weight, key_weight, value_weight, out_weight, conv_full
):
    vmem = pl.BlockSpec(memory_space=pltpu.VMEM)
    anywhere = pl.BlockSpec(memory_space=pl.ANY)
    kind, full = rows_in.dtype, jnp.float32
    width, mid_width = rows_in.shape[1], hidden.shape[1]
    piece = (16, 64, WIDE)
    count = 4 * 16 * 64
    sems = 2 * (LINE + PLANE)
    weights = (mix_full, query_weight, key_weight, value_weight, out_weight, conv_full)
    scratch = [(table.shape, kind) for table in weights]
    scratch += [((ROWS, mid_width), full)] * 2 + [((ROWS, width), kind)] + [((ROWS, width), full)] * 4
    scratch += [((ROWS, H * KD), kind)] * 2 + [((ROWS, H * VD), kind)] * 2
    scratch += [((ROWS, H * KD), kind), ((ROWS, H * VD), kind), ((ROWS, H * KD), kind)]
    scratch += [(piece, kind)] * 3 + [((2, 2) + piece, kind), ((WIDE, count), kind)]
    scratch += [((count, QUERY_BLOCK), full)] * 2 + [((count, WIDE), full)]
    scratch += [(piece, kind), ((2, 2) + piece, kind), (piece, kind), (piece, kind)]
    scratch += [((2,) + piece, kind)] + [(piece, kind)] * 3
    scratch += [((LINE, 4, mid_width), full), ((PLANE, 4, mid_width), full)]
    scratch += [((LINE, 2, width), full), ((PLANE, 2, width), full)]
    scratch += [((2, 64, mid_width), kind), ((2, 96, mid_width), kind)] + [((2, 16, mid_width), kind)] * 2
    dma = pltpu.SemaphoreType.DMA
    return pl.pallas_call(
        back_kernel,
        out_shape=[
            jax.ShapeDtypeStruct((ROWS, width), kind),
            jax.ShapeDtypeStruct((ROWS, width), kind),
            jax.ShapeDtypeStruct((4, mid_width), full),
            jax.ShapeDtypeStruct((2, width), full),
        ],
        in_specs=[vmem] * 11 + [anywhere] * 6,
        out_specs=[vmem] * 4,
        scratch_shapes=[pltpu.VMEM(shape, held) for shape, held in scratch]
        + [dma((128,)), dma((128,)), dma((sems,)), dma((sems,)), dma((1, 2)), dma((1, 2)), dma((6,))],
        compiler_params=pltpu.CompilerParams(
            collective_id=2, has_side_effects=True, vmem_limit_bytes=62 * 1024 * 1024
        ),
        name="back",
    )(
        rows_in, hidden, stats_one, stats_two, gain_two, bias_two, norm_gain, gain_one, bias_one,
        grad_out, cot, *weights
    )


def on_device(
    inputs,
    conv_weight,
    mix_weight,
    first_gain,
    first_bias,
    second_gain,
    second_bias,
    norm_gain,
    query_weight,
    key_weight,
    value_weight,
    out_weight,
    cotangent,
):
    windows_here, local_bins, model_width = inputs.shape
    local_count = windows_here * local_bins
    rows_in = inputs.reshape(local_count, model_width)
    cot_flat = cotangent.reshape(local_count, model_width)
    conv_full, mix_full, hidden, stats_one, stats_two, grad_out = front(
        rows_in, conv_weight, mix_weight, first_gain, first_bias, cot_flat, out_weight
    )
    encoded_rows, grad_rows, sums_two, sums_one = back(
        rows_in,
        hidden,
        stats_one,
        stats_two,
        second_gain,
        second_bias,
        norm_gain,
        first_gain,
        first_bias,
        grad_out,
        cot_flat,
        mix_full,
        query_weight,
        key_weight,
        value_weight,
        out_weight,
        conv_full,
    )
    encoded = encoded_rows.reshape(windows_here, local_bins, model_width)
    grad_inputs = grad_rows.reshape(windows_here, local_bins, model_width)
    grad_second_bias, grad_second_gain = sums_two[0], sums_two[1]
    grad_norm_gain = sums_two[2:4].reshape(-1)
    grad_first_bias, grad_first_gain = sums_one[0], sums_one[1]
    return (
        encoded,
        grad_inputs,
        grad_first_gain,
        grad_first_bias,
        grad_second_gain,
        grad_second_bias,
        grad_norm_gain,
    )


def solution(mesh):
    in_specs = (
        P("batch", "seq", None),
        P("seq", None),
        P("seq", None),
        P(),
        P(),
        P(),
        P(),
        P(),
        P(),
        P(),
        P(),
        P(),
        P("batch", "seq", None),
    )
    out_specs = (P("batch", "seq", None), P("batch", "seq", None), P(), P(), P(), P(), P())
    return jax.shard_map(
        on_device, mesh=mesh, in_specs=in_specs, out_specs=out_specs, check_vma=False
    )
```

```python
import jax
import jax.numpy as jnp
from jax import lax
from jax.experimental import pallas as pl
from jax.experimental.pallas import tpu as pltpu
from jax.sharding import PartitionSpec as P

H = 8
KD = 64
VD = 192
DILATION_STEP = 16


EPS = 1e-05
GELU_C = 0.7978845608028654


MESH = pl.DeviceIdType.MESH
ROWS = 128
LINE = 8
PLANE = 16
TAP_PARTS = ((0, 0, 0, 768), (1, 0, 768, 384), (1, 1, 0, 384), (2, 1, 384, 768))


def seq_of(z, y, x, core):
    return ((z * 4 + y) * 2 + x) * 2 + core


def remote(source, target, peer, sems, slot):
    copy = pltpu.make_async_remote_copy(
        src_ref=source,
        dst_ref=target,
        send_sem=sems[0].at[slot],
        recv_sem=sems[1].at[slot],
        device_id=peer,
        device_id_type=MESH,
    )
    copy.start()
    return copy


def line_place():
    return lax.axis_index("batch") * 4 + lax.rem(lax.axis_index("seq"), 4)


def line_peer(step):
    other = lax.rem(line_place() + step, LINE)
    spot = lax.axis_index("seq") // 4
    return {"seq": spot * 4 + lax.rem(other, 4), "batch": other // 4}


def plane_peer(step):
    seq = lax.axis_index("seq")
    return {"seq": lax.rem(seq // 4 + step, PLANE) * 4 + lax.rem(seq, 4)}


def ring_peer(step):
    count = 4 * PLANE
    return {"seq": lax.rem(lax.axis_index("seq") + step + count, count)}


def greet_all():
    barrier = pltpu.get_barrier_semaphore()
    peers = [line_peer(step) for step in range(1, LINE)]
    peers += [plane_peer(step) for step in range(1, PLANE)]
    peers += [ring_peer(1), ring_peer(-1)]
    for peer in peers:
        pl.semaphore_signal(barrier, inc=1, device_id=peer, device_id_type=MESH)
    return barrier, len(peers)


def line_send(line, sems, base):
    place = line.at[line_place()]
    return [remote(place, place, line_peer(step), sems, base + step) for step in range(1, LINE)]


def plane_send(line, plane, arrivals, sems, base):
    for copy in arrivals:
        copy.wait_recv()
    total = line[0]
    for i in range(1, LINE):
        total = total + line[i]
    spot = lax.axis_index("seq") // 4
    plane[spot] = total
    place = plane.at[spot]
    return [
        remote(place, place, plane_peer(step), sems, base + LINE + step) for step in range(1, PLANE)
    ]


def plane_sum(plane, arrivals):
    for copy in arrivals:
        copy.wait_recv()
    total = plane[0]
    for i in range(1, PLANE):
        total = total + plane[i]
    return total


def halo_send(middle, low, high, sems, base):
    return [
        remote(middle.at[:, 48:64, :], low, ring_peer(1), sems, (base, 0)),
        remote(middle.at[:, 0:16, :], high, ring_peer(-1), sems, (base, 1)),
    ]


def halo_fill(padded, low, high, copies):
    seq = lax.axis_index("seq")
    last = lax.axis_size("seq") - 1
    for copy in copies:
        copy.wait_recv()
    low_rows = low[...].astype(jnp.float32)
    high_rows = high[...].astype(jnp.float32)
    padded[:, 0:16, :] = jnp.where(seq == 0, 0.0, low_rows).astype(padded.dtype)
    padded[:, 80:96, :] = jnp.where(seq == last, 0.0, high_rows).astype(padded.dtype)


def tap_rows(padded, start):
    return jnp.concatenate([padded[0, start : start + 64, :], padded[1, start : start + 64, :]], axis=0)


def stacked(rows):
    return jnp.concatenate([jnp.sum(part, axis=0, keepdims=True) for part in rows], axis=0)


def gelu_value(values):
    cubic = GELU_C * (values + 0.044715 * values * values * values)
    return 0.5 * values * (1.0 + jnp.tanh(cubic))


def gelu_slope(values):
    tangent = jnp.tanh(GELU_C * (values + 0.044715 * values * values * values))
    return 0.5 * (1.0 + tangent) + 0.5 * values * (1.0 - tangent * tangent) * GELU_C * (
        1.0 + 3.0 * 0.044715 * values * values
    )


def rounded(values):
    return lax.optimization_barrier(values.astype(jnp.bfloat16)).astype(jnp.float32)


CHUNK = 1024
QUERY_BLOCK = 256
SIDE = (((1,), (1,)), ((), ()))
def front_kernel(
    x_from, conv_from, mix_from, gain_ref, bias_ref, cot_from, out_weight_ref,
    conv_to, mix_to, hidden_out, stats_one_out, stats_two_out, grad_out,
    conv_out, mix_out, line_one, plane_one, line_two, plane_two, conv_other, mix_other, mix_land, middle, padded,
    low, high, weight, x_ref, conv_ref, mix_ref, cot_ref, sum_send, sum_recv, move_send, move_recv, own_sem
):
    seq = lax.axis_index("seq")
    core = lax.rem(seq, 2)
    x = lax.rem(seq // 2, 2)
    y = lax.rem(seq // 4, 4)
    z = seq // 16
    sums = (sum_send, sum_recv)
    moves = (move_send, move_recv)
    total_rows = ROWS * lax.axis_size("seq") * lax.axis_size("batch")
    barrier, count = greet_all()
    loads = [
        pltpu.make_async_copy(source, target, own_sem.at[i])
        for i, (source, target) in enumerate(
            (
                (x_from, x_ref),
                (conv_from, conv_ref),
                (mix_from, mix_ref),
                (cot_from, cot_ref),
                (out_weight_ref, weight),
            )
        )
    ]
    for load in loads:
        load.start()
    loads[0].wait()
    values = x_ref[...].astype(jnp.float32)
    line_one[line_place()] = stacked([values, values * values])
    pl.semaphore_wait(barrier, count)

    def first_peer(step):
        return {"seq": seq_of(lax.rem(z + step * x, 4), lax.rem(y + step * (1 - x), 4), x, core)}

    def second_peer(step):
        return {"seq": seq_of(lax.rem(z + step * (1 - x), 4), lax.rem(y + step * x, 4), x, core)}

    def y_peer(step):
        return {"seq": seq_of(z, lax.rem(y + step, 4), x, core)}

    def z_peer(step):
        return {"seq": seq_of(lax.rem(z + step, 4), y, x, core)}

    x_peer = {"seq": seq_of(z, y, 1 - x, core)}
    sibling = {"seq": seq_of(z, y, x, 1 - core)}
    outs = (conv_out, mix_land)
    widths = (conv_ref.shape[1] // 2, mix_ref.shape[1] // 2)
    halves = [pl.ds(pl.multiple_of(core * w, w), w) for w in widths]
    far_halves = [pl.ds(pl.multiple_of((1 - core) * w, w), w) for w in widths]

    def move(kind, where, peer, slot):
        place = outs[kind].at[(core, *where)]
        return remote(place, place, peer, moves, (slot, kind))

    started = line_send(line_one, sums, 0)
    line_started = started
    pair_up = [
        remote(conv_from.at[:, far_halves[0]], conv_other, sibling, moves, (0, 0)),
        remote(mix_from.at[:, far_halves[1]], mix_other, sibling, moves, (0, 1)),
    ]
    started = started + pair_up
    for kind, mine, other in ((0, conv_ref, conv_other), (1, mix_ref, mix_other)):
        loads[1 + kind].wait()
        pair_up[kind].wait_recv()
        out = outs[kind]
        here = mine[:, halves[kind]].astype(jnp.float32)
        there = other[...].astype(jnp.float32)
        upper = jnp.where(core == 0, here, there)
        lower = jnp.where(core == 0, there, here)
        out[core, z, y, x] = jnp.concatenate([upper, lower], axis=0).astype(out.dtype)
    to_x = [move(kind, (z, y, x), x_peer, 1) for kind in range(2)]
    spread_out = []
    for kind in range(2):
        for step in (1, 3):
            spread_out.append(move(kind, (z, y, x), first_peer(step), 1 + step))
    plane_started = plane_send(line_one, plane_one, line_started, sums, 0)
    for copy in to_x:
        copy.wait_recv()
    for kind in range(2):
        for step in (1, 3):
            spread_out.append(move(kind, (z, y, 1 - x), second_peer(step), 4 + step))
    first_block, second_block = spread_out[:4], spread_out[4:]
    for kind, step, back in ((0, 1, 3), (1, 3, 1)):
        first_block[2 * kind + step // 2].wait_recv()
        place = (lax.rem(z + back * x, 4), lax.rem(y + back * (1 - x), 4), x)
        spread_out.append(move(kind, place, first_peer(step), 3))
    total = plane_sum(plane_one, plane_started)
    mean = total[0:1, :] / total_rows
    scale = lax.rsqrt(total[1:2, :] / total_rows - mean * mean + EPS)
    stats_one_out[...] = jnp.concatenate([mean, scale], axis=0)
    pre = (values - mean) * scale * gain_ref[...][None, :] + bias_ref[...][None, :]
    active = gelu_value(pre).astype(middle.dtype)
    for window in range(2):
        middle[window] = active[window * 64 : window * 64 + 64, :]
        padded[window, 16:80, :] = active[window * 64 : window * 64 + 64, :]
    halos = halo_send(middle, low, high, moves, 19)
    for kind, step, back in ((0, 1, 3), (1, 3, 1)):
        second_block[2 * kind + step // 2].wait_recv()
        place = (lax.rem(z + back * (1 - x), 4), lax.rem(y + back * x, 4), 1 - x)
        spread_out.append(move(kind, place, second_peer(step), 6))
    waited = (first_block[0], first_block[3], second_block[0], second_block[3])
    for copy in spread_out:
        if all(copy is not other for other in waited):
            copy.wait_recv()
    whole = slice(None)
    blocks = [[], []]
    across = [[], []]

    def launch(kind):
        for step in (1, 3):
            blocks[kind].append(move(kind, (z, whole, 0), z_peer(step), 7 + step))
            blocks[kind].append(move(kind, (whole, y, 1), y_peer(step), 10 + step))
        across[kind].append(move(kind, (z, whole, 0), sibling, 14))
        across[kind].append(move(kind, (whole, y, 1), sibling, 15))

    def relay(kind):
        for i, (step, part) in enumerate(((1, slice(0, 2)), (3, slice(2, 4)))):
            from_z, from_y = lax.rem(z + 4 - step, 4), lax.rem(y + 4 - step, 4)
            blocks[kind][2 * i].wait_recv()
            blocks[kind].append(move(kind, (from_z, part, 0), z_peer(step), 9 if i == 0 else 24))
            blocks[kind][2 * i + 1].wait_recv()
            blocks[kind].append(move(kind, (part, from_y, 1), y_peer(step), 12 if i == 0 else 25))
            across[kind].append(move(kind, (from_z, whole, 0), sibling, 15 + step))
            across[kind].append(move(kind, (whole, from_y, 1), sibling, 20 + step))

    def finish(kind):
        blocks[kind][4].wait_recv()
        blocks[kind][6].wait_recv()
        across[kind].append(move(kind, (lax.rem(z + 2, 4), whole, 0), sibling, 17))
        blocks[kind][5].wait_recv()
        blocks[kind][7].wait_recv()
        across[kind].append(move(kind, (whole, lax.rem(y + 2, 4), 1), sibling, 22))

    launch(0)
    loads[3].wait()
    loads[4].wait()
    grad_out[...] = lax.dot_general(
        cot_ref[...], weight[...], SIDE, preferred_element_type=jnp.float32
    ).astype(grad_out.dtype)
    halo_fill(padded, low, high, halos)

    relay(0)
    launch(1)
    finish(0)
    for copy in across[0]:
        copy.wait_recv()
    stores = [pltpu.make_async_copy(conv_out, conv_to, own_sem.at[5])]
    stores[0].start()
    terms = {}
    for tap, half, start, size in TAP_PARTS:
        part = conv_out[half, :, :, :, :, start : start + size].reshape(-1, size)
        terms[tap, half] = jnp.dot(tap_rows(padded, 16 * tap), part, preferred_element_type=jnp.float32)
    middle_tap = jnp.concatenate([terms[1, 0], terms[1, 1]], axis=1)
    hidden = terms[0, 0] + middle_tap + terms[2, 1]
    hidden_out[...] = hidden
    line_two[line_place()] = stacked([hidden, hidden * hidden])
    line_again = line_send(line_two, sums, LINE + PLANE)
    relay(1)
    plane_again = plane_send(line_two, plane_two, line_again, sums, LINE + PLANE)
    finish(1)
    for copy in across[1]:
        copy.wait_recv()
    for i in range(4):
        for j in range(4):
            start = (i * 4 + j) * 48
            for half in range(2):
                pair = [mix_land[half, i, j, k].astype(jnp.float32) for k in range(2)]
                columns = slice(half * widths[1], half * widths[1] + widths[1])
                mix_out[start : start + 48, columns] = jnp.concatenate(pair, axis=0).astype(mix_out.dtype)
    stores.append(pltpu.make_async_copy(mix_out, mix_to, own_sem.at[6]))
    stores[1].start()
    stats_two_out[...] = plane_sum(plane_two, plane_again)
    ended = started + to_x + spread_out + halos + plane_started + line_again + plane_again
    for kind in range(2):
        ended += blocks[kind] + across[kind]
    for copy in ended:
        copy.wait_send()
    for copy in stores:
        copy.wait()


def front(inputs, conv_weight, mix_weight, gain, bias, cot, out_weight):
    vmem = pl.BlockSpec(memory_space=pltpu.VMEM)
    anywhere = pl.BlockSpec(memory_space=pl.ANY)
    width = inputs.shape[1]
    mid_width = conv_weight.shape[1] // 3
    kind = inputs.dtype
    conv_rows, mix_rows = conv_weight.shape[0], mix_weight.shape[0]
    full, wide = jnp.float32, conv_weight.shape[1]
    sems = 2 * (LINE + PLANE)
    conv_full, *rest = pl.pallas_call(
        front_kernel,
        out_shape=[
            jax.ShapeDtypeStruct((2, 4, 4, 2, 2 * conv_rows, wide // 2), kind),
            jax.ShapeDtypeStruct((64 * mix_rows, width), kind),
            jax.ShapeDtypeStruct((ROWS, mid_width), full),
            jax.ShapeDtypeStruct((2, width), full),
            jax.ShapeDtypeStruct((2, mid_width), full),
            jax.ShapeDtypeStruct((ROWS, out_weight.shape[0]), kind),
        ],
        in_specs=[anywhere] * 3 + [vmem] * 2 + [anywhere] * 2,
        out_specs=[anywhere] * 2 + [vmem] * 4,
        scratch_shapes=[
            pltpu.VMEM((2, 4, 4, 2, 2 * conv_rows, wide // 2), kind),
            pltpu.VMEM((64 * mix_rows, width), kind),
            pltpu.VMEM((LINE, 2, width), full),
            pltpu.VMEM((PLANE, 2, width), full),
            pltpu.VMEM((LINE, 2, mid_width), full),
            pltpu.VMEM((PLANE, 2, mid_width), full),
            pltpu.VMEM((conv_rows, wide // 2), kind),
            pltpu.VMEM((mix_rows, width // 2), kind),
            pltpu.VMEM((2, 4, 4, 2, 2 * mix_rows, width // 2), kind),
            pltpu.VMEM((2, 64, width), kind),
            pltpu.VMEM((2, 96, width), kind),
            pltpu.VMEM((2, 16, width), kind),
            pltpu.VMEM((2, 16, width), kind),
            pltpu.VMEM(out_weight.shape, kind),
            pltpu.VMEM(inputs.shape, kind),
            pltpu.VMEM(conv_weight.shape, kind),
            pltpu.VMEM(mix_weight.shape, kind),
            pltpu.VMEM(cot.shape, kind),
            pltpu.SemaphoreType.DMA((sems,)),
            pltpu.SemaphoreType.DMA((sems,)),
            pltpu.SemaphoreType.DMA((26, 2)),
            pltpu.SemaphoreType.DMA((26, 2)),
            pltpu.SemaphoreType.DMA((7,)),
        ],
        compiler_params=pltpu.CompilerParams(
            collective_id=1, has_side_effects=True, vmem_limit_bytes=62 * 1024 * 1024
        ),
        name="front",
    )(inputs, conv_weight, mix_weight, gain, bias, cot, out_weight)
    return [conv_full.reshape(2, -1, wide // 2)] + rest


LOW = VD
WIDE = VD + KD


def spots():
    seq = lax.axis_index("seq")
    core = lax.rem(seq, 2)
    z = seq // 16
    mine = (z // 2) * 8 + lax.rem(seq // 2, 8)
    return seq, core, lax.rem(z + z // 2, 2), mine


def pair_ahead(mine, step):
    return lax.rem(mine // 4 + step // 4, 4) * 4 + lax.rem(lax.rem(mine, 4) + step % 4, 4)


def pair_behind(mine, step):
    return lax.rem(mine // 4 + 4 - step // 4, 4) * 4 + lax.rem(lax.rem(mine, 4) + 4 - step % 4, 4)


def holder(pair, z_low, core):
    upper = pair // 8
    z = upper * 2 + lax.rem(z_low + upper, 2)
    return {"seq": z * 16 + lax.rem(pair, 8) * 2 + core}


def attention_peers(seq, core, z_low, mine):
    z_peer = holder(mine, 1 - z_low, core)
    sibling = {"seq": seq + 1 - 2 * core}
    return z_peer, sibling


def greet_attention(barrier):
    seq, core, z_low, mine = spots()
    peers = [holder(pair_ahead(mine, step), z_low, core) for step in range(1, 16)]
    peers += attention_peers(seq, core, z_low, mine)
    for peer in peers:
        pl.semaphore_signal(barrier, inc=1, device_id=peer, device_id_type=MESH)
    return len(peers)


def spread_heads(q_ref, k_ref, v_ref, g_ref, x_out, y_out, x_part, y_part, sems, meanwhile):
    seq, core, z_low, mine = spots()
    z_peer, sibling = attention_peers(seq, core, z_low, mine)
    for window in range(2):
        rows = slice(window * 64, window * 64 + 64)
        for head in range(H):
            pair = window * H + head
            y_part[pair, :, 0:LOW] = v_ref[rows, head * VD : head * VD + VD]
            y_part[pair, :, LOW:WIDE] = k_ref[rows, head * KD : head * KD + KD]

    def send(source, target, peer, slot):
        return remote(source, target, peer, sems, slot)

    y_sends = []
    for step in range(1, 16):
        pair = pair_ahead(mine, step)
        peer = holder(pair, z_low, core)
        y_sends.append(send(y_part.at[pair], y_out.at[z_low, core, mine], peer, step))
    for window in range(2):
        rows = slice(window * 64, window * 64 + 64)
        for head in range(H):
            pair = window * H + head
            x_part[pair, :, 0:LOW] = g_ref[rows, head * VD : head * VD + VD]
            x_part[pair, :, LOW:WIDE] = q_ref[rows, head * KD : head * KD + KD]
    x_sends = []
    for step in range(1, 16):
        pair = pair_ahead(mine, step)
        peer = holder(pair, z_low, core)
        x_sends.append(send(x_part.at[pair], x_out.at[mine], peer, 16 + step))
    y_out[z_low, core, mine] = y_part[mine]
    x_out[mine] = x_part[mine]
    along = []
    across = []
    for step in range(16):
        if step > 0:
            y_sends[step - 1].wait_recv()
        place = y_out.at[z_low, core, pair_behind(mine, step)]
        along.append(send(place, place, z_peer, 32 + step))
        across.append(send(place, place, sibling, 48 + step))
    meanwhile()
    for step in range(16):
        along[step].wait_recv()
        place = y_out.at[1 - z_low, core, pair_behind(mine, step)]
        across.append(send(place, place, sibling, 64 + step))
    for copy in x_sends + across:
        copy.wait_recv()
    for copy in y_sends + x_sends + along + across:
        copy.wait_send()


def collect_heads(
    oq_ref, vk_ref, a_ref, gq_ref, gv_ref, gk_ref, oq_got, vk_got, from_core, to_z, from_z, total, sems,
    meanwhile
):
    seq, core, z_low, mine = spots()
    z_peer, sibling = attention_peers(seq, core, z_low, mine)

    def send(source, target, peer, slot):
        return remote(source, target, peer, sems, 80 + slot)

    groups = [pl.ds(lax.rem(mine // 4 + k, 4) * 4, 4) for k in range(4)]
    across = []
    for far in range(2):
        z_part = 1 - z_low if far == 0 else z_low
        for k in range(4):
            across.append(
                send(
                    vk_ref.at[z_part, 1 - core, groups[k]],
                    from_core.at[far, groups[k]],
                    sibling,
                    4 * far + k,
                )
            )
    oq_sends = []
    for step in range(1, 16):
        pair = pair_ahead(mine, step)
        oq_sends.append(
            send(oq_ref.at[pair], oq_got.at[mine], holder(pair, z_low, core), 16 + step)
        )
    oq_got[mine] = oq_ref[mine]
    along = []
    for k in range(4):
        across[k].wait_recv()
        summed = vk_ref[1 - z_low, core, groups[k]].astype(jnp.float32) + from_core[
            0, groups[k]
        ].astype(jnp.float32)
        to_z[groups[k]] = summed.astype(to_z.dtype)
        along.append(send(to_z.at[groups[k]], from_z.at[groups[k]], z_peer, 8 + k))
    vk_sends = []
    for k in range(4):
        across[4 + k].wait_recv()
        along[k].wait_recv()
        summed = vk_ref[z_low, core, groups[k]].astype(jnp.float32) + from_core[
            1, groups[k]
        ].astype(jnp.float32)
        summed = summed + from_z[groups[k]].astype(jnp.float32)
        total[groups[k]] = summed.astype(total.dtype)
        for step in range(4 * k, 4 * k + 4):
            if step > 0:
                pair = pair_ahead(mine, step)
                vk_sends.append(
                    send(total.at[pair], vk_got.at[mine], holder(pair, z_low, core), 32 + step)
                )
    vk_got[mine] = total[mine]
    for copy in oq_sends:
        copy.wait_recv()
    for window in range(2):
        rows = slice(window * 64, window * 64 + 64)
        for head in range(H):
            pair = window * H + head
            a_ref[rows, head * VD : head * VD + VD] = oq_got[pair, :, 0:LOW]
            gq_ref[rows, head * KD : head * KD + KD] = oq_got[pair, :, LOW:WIDE]
    meanwhile()
    for copy in vk_sends:
        copy.wait_recv()
    for window in range(2):
        rows = slice(window * 64, window * 64 + 64)
        for head in range(H):
            pair = window * H + head
            gv_ref[rows, head * VD : head * VD + VD] = vk_got[pair, :, 0:LOW]
            gk_ref[rows, head * KD : head * KD + KD] = vk_got[pair, :, LOW:WIDE]
    for copy in across + oq_sends + along + vk_sends:
        copy.wait_send()


def attend_rows(x_ref, y_ref, oq_ref, vk_ref, y_turned, score, slope, total):
    keys = y_turned.shape[1]
    chunks = [slice(start, start + CHUNK) for start in range(0, keys, CHUNK)]

    def key_rows(part):
        quarter = part.start // CHUNK
        return y_ref[quarter // 2, quarter % 2].reshape(CHUNK, WIDE)

    key_scale = KD ** (-0.5)
    for part in chunks:
        y_turned[:, part] = key_rows(part).T
    total[...] = jnp.zeros_like(total)

    def block(index, carry):
        rows = pl.ds(index * 4, 4)
        x_block = x_ref[rows].reshape(QUERY_BLOCK, WIDE)
        wide = x_block.astype(jnp.float32)
        low = lax.broadcasted_iota(jnp.int32, wide.shape, 1) < LOW
        query = jnp.where(low, 0.0, wide).astype(x_block.dtype)
        grad = jnp.where(low, wide, 0.0).astype(x_block.dtype)
        peak = None
        for part in chunks:
            scores = lax.dot_general(key_rows(part), query, SIDE, preferred_element_type=jnp.float32)
            score[part, :] = scores
            top = jnp.max(scores, axis=0, keepdims=True)
            peak = top if peak is None else jnp.maximum(peak, top)
        weight = jnp.zeros((1, QUERY_BLOCK), jnp.float32)
        center = jnp.zeros((1, QUERY_BLOCK), jnp.float32)
        for part in chunks:
            grads = lax.dot_general(key_rows(part), grad, SIDE, preferred_element_type=jnp.float32)
            slope[part, :] = grads
            terms = jnp.exp2((score[part, :] - peak) * (key_scale * 1.4426950408889634))
            score[part, :] = terms
            weight = weight + jnp.sum(terms, axis=0, keepdims=True)
            center = center + jnp.sum(terms * grads, axis=0, keepdims=True)
        share = 1.0 / weight
        center = center * share
        out = jnp.zeros((WIDE, QUERY_BLOCK), jnp.float32)
        back = jnp.zeros((WIDE, QUERY_BLOCK), jnp.float32)
        low_keys = lax.broadcasted_iota(jnp.int32, (CHUNK, WIDE), 1) < LOW
        for part in chunks:
            probs = score[part, :] * share
            prob_low = probs.astype(jnp.bfloat16)
            grads = (probs * (slope[part, :] - center)).astype(jnp.bfloat16)
            out = out + jnp.dot(y_turned[:, part], prob_low, preferred_element_type=jnp.float32)
            back = back + jnp.dot(y_turned[:, part], grads, preferred_element_type=jnp.float32)
            for_values = jnp.dot(prob_low, x_block, preferred_element_type=jnp.float32)
            for_keys = jnp.dot(grads, x_block, preferred_element_type=jnp.float32)
            total[part, :] += jnp.where(low_keys, for_values, for_keys)
        low_rows = lax.broadcasted_iota(jnp.int32, out.shape, 0) < LOW
        turned = jnp.where(low_rows, out, back * key_scale).T
        oq_ref[rows] = turned.reshape(4, 64, WIDE).astype(oq_ref.dtype)
        return carry

    lax.fori_loop(0, x_ref.shape[0] // 4, block, 0)
    low_keys = lax.broadcasted_iota(jnp.int32, (CHUNK, WIDE), 1) < LOW
    for part in chunks:
        quarter = part.start // CHUNK
        grads = total[part, :]
        grads = jnp.where(low_keys, grads, grads * key_scale).astype(vk_ref.dtype)
        vk_ref[quarter // 2, quarter % 2] = grads.reshape(vk_ref.shape[2:])


def back_kernel(
    x_ref, hidden_ref, stats_one_ref, stats_two_ref, gain_two_ref, bias_two_ref, norm_ref,
    gain_ref, bias_ref, g_ref, cot_ref, mix_from, q_from, k_from, v_from, o_from, conv_from,
    encoded_out, out_ref, sums_two_out, sums_one_out,
    mix, q_weight, k_weight, v_weight, o_weight, weight,
    hat_two, slope_two, trunk, row_hat, mixed, hat_one, slope_one, q_rows, k_rows, v_rows,
    a_rows, gq_rows, gv_rows, gk_rows,
    x_part, y_part, x_got, y_got, y_turned, score, slope, total_vk, oq, vk,
    oq_got, vk_got, from_core, to_z, from_z, summed,
    line_two, plane_two, line_one, plane_one, middle, padded, low, high,
    head_send, head_recv, sum_send, sum_recv, move_send, move_recv, own_sem
):
    heads = (head_send, head_recv)
    sums = (sum_send, sum_recv)
    moves = (move_send, move_recv)
    total_rows = ROWS * lax.axis_size("seq") * lax.axis_size("batch")
    kind = x_ref.dtype
    full = jnp.float32
    barrier, count = greet_all()
    count += greet_attention(barrier)
    loads = [
        pltpu.make_async_copy(source, target, own_sem.at[i])
        for i, (source, target) in enumerate(
            (
                (mix_from, mix),
                (q_from, q_weight),
                (k_from, k_weight),
                (v_from, v_weight),
                (o_from, o_weight),
                (conv_from, weight),
            )
        )
    ]
    for load in loads:
        load.start()
    mean_two = stats_two_ref[0:1, :] / total_rows
    scale_two = lax.rsqrt(stats_two_ref[1:2, :] / total_rows - mean_two * mean_two + EPS)
    hat = (hidden_ref[...] - mean_two) * scale_two
    pre = hat * gain_two_ref[...][None, :] + bias_two_ref[...][None, :]
    hat_two[...] = hat
    loads[0].wait()
    trunk[...] = (
        x_ref[...].astype(full)
        + jnp.dot(gelu_value(pre).astype(kind), mix[...], preferred_element_type=full)
    ).astype(kind)
    rows = trunk[...].astype(full)
    centered = rows - jnp.mean(rows, axis=-1, keepdims=True)
    row_scale = lax.rsqrt(jnp.mean(centered * centered, axis=-1, keepdims=True) + EPS)
    row_hat[...] = centered * row_scale
    norm_gain = norm_ref[...][None, :]
    normed = (row_hat[...] * norm_gain).astype(kind)
    for load, table, place in (
        (loads[3], v_weight, v_rows),
        (loads[2], k_weight, k_rows),
        (loads[1], q_weight, q_rows),
    ):
        load.wait()
        place[...] = jnp.dot(normed, table[...], preferred_element_type=full).astype(kind)
    pl.semaphore_wait(barrier, count)

    mean, scale = stats_one_ref[0:1, :], stats_one_ref[1:2, :]
    gain_one = gain_ref[...][None, :]

    def recall():
        slope_two[...] = gelu_slope(hat_two[...] * gain_two_ref[...][None, :] + bias_two_ref[...][None, :])
        hat_one[...] = (x_ref[...].astype(full) - mean) * scale
        slope_one[...] = gelu_slope(hat_one[...] * gain_one + bias_ref[...][None, :])

    def encode():
        loads[4].wait()
        encoded_out[...] = (
            trunk[...].astype(full) + jnp.dot(a_rows[...], o_weight[...], preferred_element_type=full)
        ).astype(kind)
        mixed[...] = lax.dot_general(gq_rows[...], q_weight[...], SIDE, preferred_element_type=full)

    spread_heads(q_rows, k_rows, v_rows, g_ref, x_got, y_got, x_part, y_part, heads, recall)
    attend_rows(x_got, y_got, oq, vk, y_turned, score, slope, total_vk)
    collect_heads(
        oq, vk, a_rows, gq_rows, gv_rows, gk_rows, oq_got, vk_got, from_core, to_z, from_z, summed,
        heads, encode
    )
    grad_normed = (
        mixed[...]
        + lax.dot_general(gk_rows[...], k_weight[...], SIDE, preferred_element_type=full)
        + lax.dot_general(gv_rows[...], v_weight[...], SIDE, preferred_element_type=full)
    )
    hats = row_hat[...]
    norm_part = jnp.sum(grad_normed * hats, axis=0, keepdims=True)
    grad_hat = grad_normed * norm_gain
    mixed[...] = cot_ref[...].astype(full) + row_scale * (
        grad_hat
        - jnp.mean(grad_hat, axis=-1, keepdims=True)
        - hats * jnp.mean(grad_hat * hats, axis=-1, keepdims=True)
    )
    grad_two = (
        lax.dot_general(mixed[...].astype(kind), mix[...], SIDE, preferred_element_type=full)
        * slope_two[...]
    )
    mid_width = grad_two.shape[1]
    place = line_place()
    line_two[place] = jnp.concatenate(
        [
            jnp.sum(grad_two, axis=0, keepdims=True),
            jnp.sum(grad_two * hat_two[...], axis=0, keepdims=True),
            norm_part[:, :mid_width],
            norm_part[:, mid_width:],
        ],
        axis=0,
    )
    started = line_send(line_two, sums, 0)
    plane_started = plane_send(line_two, plane_two, started, sums, 0)
    total = plane_sum(plane_two, plane_started)
    sums_two_out[...] = total
    hidden_grad = (
        gain_two_ref[...][None, :]
        * scale_two
        * (grad_two - total[0:1, :] / total_rows - hat_two[...] * total[1:2, :] / total_rows)
    ).astype(kind)
    for window in range(2):
        middle[window] = hidden_grad[window * 64 : window * 64 + 64, :]
        padded[window, 16:80, :] = hidden_grad[window * 64 : window * 64 + 64, :]
    halos = halo_send(middle, low, high, moves, 0)
    loads[5].wait()
    grad_act = None
    for tap, half, start, size in (TAP_PARTS[1], TAP_PARTS[2], TAP_PARTS[0], TAP_PARTS[3]):
        if tap == 0:
            halo_fill(padded, low, high, halos)
        first = 0 if half == 0 or tap == 2 else 384
        term = lax.dot_general(
            tap_rows(padded, 16 * (2 - tap))[:, first : first + size],
            weight[half, :, start : start + size],
            SIDE,
            preferred_element_type=jnp.float32,
        )
        grad_act = term if grad_act is None else grad_act + term
    grad_pre = grad_act * slope_one[...]
    line_one[place] = stacked([grad_pre, grad_pre * hat_one[...]])
    line_again = line_send(line_one, sums, LINE + PLANE)
    plane_again = plane_send(line_one, plane_one, line_again, sums, LINE + PLANE)
    total = plane_sum(plane_one, plane_again)
    sums_one_out[...] = total
    grad_rows = (
        gain_one
        * scale
        * (grad_pre - total[0:1, :] / total_rows - hat_one[...] * total[1:2, :] / total_rows)
    )
    out_ref[...] = (mixed[...] + grad_rows).astype(out_ref.dtype)
    for copy in started + plane_started + halos + line_again + plane_again:
        copy.wait_send()


def back(
    rows_in, hidden, stats_one, stats_two, gain_two, bias_two, norm_gain, gain_one, bias_one,
    grad_out, cot, mix_full, query_weight, key_weight, value_weight, out_weight, conv_full
):
    vmem = pl.BlockSpec(memory_space=pltpu.VMEM)
    anywhere = pl.BlockSpec(memory_space=pl.ANY)
    kind, full = rows_in.dtype, jnp.float32
    width, mid_width = rows_in.shape[1], hidden.shape[1]
    piece = (16, 64, WIDE)
    count = 4 * 16 * 64
    sems = 2 * (LINE + PLANE)
    weights = (mix_full, query_weight, key_weight, value_weight, out_weight, conv_full)
    scratch = [(table.shape, kind) for table in weights]
    scratch += [((ROWS, mid_width), full)] * 2 + [((ROWS, width), kind)] + [((ROWS, width), full)] * 4
    scratch += [((ROWS, H * KD), kind)] * 2 + [((ROWS, H * VD), kind)] * 2
    scratch += [((ROWS, H * KD), kind), ((ROWS, H * VD), kind), ((ROWS, H * KD), kind)]
    scratch += [(piece, kind)] * 3 + [((2, 2) + piece, kind), ((WIDE, count), kind)]
    scratch += [((count, QUERY_BLOCK), full)] * 2 + [((count, WIDE), full)]
    scratch += [(piece, kind), ((2, 2) + piece, kind), (piece, kind), (piece, kind)]
    scratch += [((2,) + piece, kind)] + [(piece, kind)] * 3
    scratch += [((LINE, 4, mid_width), full), ((PLANE, 4, mid_width), full)]
    scratch += [((LINE, 2, width), full), ((PLANE, 2, width), full)]
    scratch += [((2, 64, mid_width), kind), ((2, 96, mid_width), kind)] + [((2, 16, mid_width), kind)] * 2
    dma = pltpu.SemaphoreType.DMA
    return pl.pallas_call(
        back_kernel,
        out_shape=[
            jax.ShapeDtypeStruct((ROWS, width), kind),
            jax.ShapeDtypeStruct((ROWS, width), kind),
            jax.ShapeDtypeStruct((4, mid_width), full),
            jax.ShapeDtypeStruct((2, width), full),
        ],
        in_specs=[vmem] * 11 + [anywhere] * 6,
        out_specs=[vmem] * 4,
        scratch_shapes=[pltpu.VMEM(shape, held) for shape, held in scratch]
        + [dma((128,)), dma((128,)), dma((sems,)), dma((sems,)), dma((1, 2)), dma((1, 2)), dma((6,))],
        compiler_params=pltpu.CompilerParams(
            collective_id=2, has_side_effects=True, vmem_limit_bytes=62 * 1024 * 1024
        ),
        name="back",
    )(
        rows_in, hidden, stats_one, stats_two, gain_two, bias_two, norm_gain, gain_one, bias_one,
        grad_out, cot, *weights
    )


def on_device(
    inputs,
    conv_weight,
    mix_weight,
    first_gain,
    first_bias,
    second_gain,
    second_bias,
    norm_gain,
    query_weight,
    key_weight,
    value_weight,
    out_weight,
    cotangent,
):
    windows_here, local_bins, model_width = inputs.shape
    local_count = windows_here * local_bins
    rows_in = inputs.reshape(local_count, model_width)
    cot_flat = cotangent.reshape(local_count, model_width)
    conv_full, mix_full, hidden, stats_one, stats_two, grad_out = front(
        rows_in, conv_weight, mix_weight, first_gain, first_bias, cot_flat, out_weight
    )
    encoded_rows, grad_rows, sums_two, sums_one = back(
        rows_in,
        hidden,
        stats_one,
        stats_two,
        second_gain,
        second_bias,
        norm_gain,
        first_gain,
        first_bias,
        grad_out,
        cot_flat,
        mix_full,
        query_weight,
        key_weight,
        value_weight,
        out_weight,
        conv_full,
    )
    encoded = encoded_rows.reshape(windows_here, local_bins, model_width)
    grad_inputs = grad_rows.reshape(windows_here, local_bins, model_width)
    grad_second_bias, grad_second_gain = sums_two[0], sums_two[1]
    grad_norm_gain = sums_two[2:4].reshape(-1)
    grad_first_bias, grad_first_gain = sums_one[0], sums_one[1]
    return (
        encoded,
        grad_inputs,
        grad_first_gain,
        grad_first_bias,
        grad_second_gain,
        grad_second_bias,
        grad_norm_gain,
    )


def solution(mesh):
    in_specs = (
        P("batch", "seq", None),
        P("seq", None),
        P("seq", None),
        P(),
        P(),
        P(),
        P(),
        P(),
        P(),
        P(),
        P(),
        P(),
        P("batch", "seq", None),
    )
    out_specs = (P("batch", "seq", None), P("batch", "seq", None), P(), P(), P(), P(), P())
    return jax.shard_map(
        on_device, mesh=mesh, in_specs=in_specs, out_specs=out_specs, check_vma=False
    )
```

```python
import jax
import jax.numpy as jnp
from jax import lax
from jax.experimental import pallas as pl
from jax.experimental.pallas import tpu as pltpu
from jax.sharding import PartitionSpec as P

H = 8
KD = 64
VD = 192
DILATION_STEP = 16


EPS = 1e-05
GELU_C = 0.7978845608028654


MESH = pl.DeviceIdType.MESH
ROWS = 128
LINE = 8
PLANE = 16
TAP_PARTS = ((0, 0, 0, 768), (1, 0, 768, 384), (1, 1, 0, 384), (2, 1, 384, 768))


def seq_of(z, y, x, core):
    return ((z * 4 + y) * 2 + x) * 2 + core


def remote(source, target, peer, sems, slot):
    copy = pltpu.make_async_remote_copy(
        src_ref=source,
        dst_ref=target,
        send_sem=sems[0].at[slot],
        recv_sem=sems[1].at[slot],
        device_id=peer,
        device_id_type=MESH,
    )
    copy.start()
    return copy


def line_place():
    return lax.axis_index("batch") * 4 + lax.rem(lax.axis_index("seq"), 4)


def line_peer(step):
    other = lax.rem(line_place() + step, LINE)
    spot = lax.axis_index("seq") // 4
    return {"seq": spot * 4 + lax.rem(other, 4), "batch": other // 4}


def plane_peer(step):
    seq = lax.axis_index("seq")
    return {"seq": lax.rem(seq // 4 + step, PLANE) * 4 + lax.rem(seq, 4)}


def ring_peer(step):
    count = 4 * PLANE
    return {"seq": lax.rem(lax.axis_index("seq") + step + count, count)}


def greet_all():
    barrier = pltpu.get_barrier_semaphore()
    peers = [line_peer(step) for step in range(1, LINE)]
    peers += [plane_peer(step) for step in range(1, PLANE)]
    peers += [ring_peer(1), ring_peer(-1)]
    for peer in peers:
        pl.semaphore_signal(barrier, inc=1, device_id=peer, device_id_type=MESH)
    return barrier, len(peers)


def line_send(line, sems, base):
    place = line.at[line_place()]
    return [remote(place, place, line_peer(step), sems, base + step) for step in range(1, LINE)]


def plane_send(line, plane, arrivals, sems, base):
    for copy in arrivals:
        copy.wait_recv()
    total = line[0]
    for i in range(1, LINE):
        total = total + line[i]
    spot = lax.axis_index("seq") // 4
    plane[spot] = total
    place = plane.at[spot]
    return [
        remote(place, place, plane_peer(step), sems, base + LINE + step) for step in range(1, PLANE)
    ]


def plane_sum(plane, arrivals):
    for copy in arrivals:
        copy.wait_recv()
    total = plane[0]
    for i in range(1, PLANE):
        total = total + plane[i]
    return total


def halo_send(middle, low, high, sems, base):
    return [
        remote(middle.at[:, 48:64, :], low, ring_peer(1), sems, (base, 0)),
        remote(middle.at[:, 0:16, :], high, ring_peer(-1), sems, (base, 1)),
    ]


def halo_fill(padded, low, high, copies):
    seq = lax.axis_index("seq")
    last = lax.axis_size("seq") - 1
    for copy in copies:
        copy.wait_recv()
    low_rows = low[...].astype(jnp.float32)
    high_rows = high[...].astype(jnp.float32)
    padded[:, 0:16, :] = jnp.where(seq == 0, 0.0, low_rows).astype(padded.dtype)
    padded[:, 80:96, :] = jnp.where(seq == last, 0.0, high_rows).astype(padded.dtype)


def tap_rows(padded, start):
    return jnp.concatenate([padded[0, start : start + 64, :], padded[1, start : start + 64, :]], axis=0)


def stacked(rows):
    return jnp.concatenate([jnp.sum(part, axis=0, keepdims=True) for part in rows], axis=0)


def gelu_value(values):
    cubic = GELU_C * (values + 0.044715 * values * values * values)
    return 0.5 * values * (1.0 + jnp.tanh(cubic))


def gelu_slope(values):
    tangent = jnp.tanh(GELU_C * (values + 0.044715 * values * values * values))
    return 0.5 * (1.0 + tangent) + 0.5 * values * (1.0 - tangent * tangent) * GELU_C * (
        1.0 + 3.0 * 0.044715 * values * values
    )


def rounded(values):
    return lax.optimization_barrier(values.astype(jnp.bfloat16)).astype(jnp.float32)


CHUNK = 256
QUERY_BLOCK = 256
SIDE = (((1,), (1,)), ((), ()))
def front_kernel(
    x_from, conv_from, mix_from, gain_ref, bias_ref, cot_from, out_weight_ref,
    conv_to, mix_to, hidden_out, stats_one_out, stats_two_out, grad_out,
    conv_out, mix_out, line_one, plane_one, line_two, plane_two, conv_other, mix_other, mix_land, middle, padded,
    low, high, weight, x_ref, conv_ref, mix_ref, cot_ref, sum_send, sum_recv, move_send, move_recv, own_sem
):
    seq = lax.axis_index("seq")
    core = lax.rem(seq, 2)
    x = lax.rem(seq // 2, 2)
    y = lax.rem(seq // 4, 4)
    z = seq // 16
    sums = (sum_send, sum_recv)
    moves = (move_send, move_recv)
    total_rows = ROWS * lax.axis_size("seq") * lax.axis_size("batch")
    barrier, count = greet_all()
    loads = [
        pltpu.make_async_copy(source, target, own_sem.at[i])
        for i, (source, target) in enumerate(
            (
                (x_from, x_ref),
                (conv_from, conv_ref),
                (mix_from, mix_ref),
                (cot_from, cot_ref),
                (out_weight_ref, weight),
            )
        )
    ]
    for load in loads:
        load.start()
    loads[0].wait()
    values = x_ref[...].astype(jnp.float32)
    line_one[line_place()] = stacked([values, values * values])
    pl.semaphore_wait(barrier, count)

    def first_peer(step):
        return {"seq": seq_of(lax.rem(z + step * x, 4), lax.rem(y + step * (1 - x), 4), x, core)}

    def second_peer(step):
        return {"seq": seq_of(lax.rem(z + step * (1 - x), 4), lax.rem(y + step * x, 4), x, core)}

    def y_peer(step):
        return {"seq": seq_of(z, lax.rem(y + step, 4), x, core)}

    def z_peer(step):
        return {"seq": seq_of(lax.rem(z + step, 4), y, x, core)}

    x_peer = {"seq": seq_of(z, y, 1 - x, core)}
    sibling = {"seq": seq_of(z, y, x, 1 - core)}
    outs = (conv_out, mix_land)
    widths = (conv_ref.shape[1] // 2, mix_ref.shape[1] // 2)
    halves = [pl.ds(pl.multiple_of(core * w, w), w) for w in widths]
    far_halves = [pl.ds(pl.multiple_of((1 - core) * w, w), w) for w in widths]

    def move(kind, where, peer, slot):
        place = outs[kind].at[(core, *where)]
        return remote(place, place, peer, moves, (slot, kind))

    started = line_send(line_one, sums, 0)
    line_started = started
    pair_up = [
        remote(conv_from.at[:, far_halves[0]], conv_other, sibling, moves, (0, 0)),
        remote(mix_from.at[:, far_halves[1]], mix_other, sibling, moves, (0, 1)),
    ]
    started = started + pair_up
    for kind, mine, other in ((0, conv_ref, conv_other), (1, mix_ref, mix_other)):
        loads[1 + kind].wait()
        pair_up[kind].wait_recv()
        out = outs[kind]
        here = mine[:, halves[kind]].astype(jnp.float32)
        there = other[...].astype(jnp.float32)
        upper = jnp.where(core == 0, here, there)
        lower = jnp.where(core == 0, there, here)
        out[core, z, y, x] = jnp.concatenate([upper, lower], axis=0).astype(out.dtype)
    to_x = [move(kind, (z, y, x), x_peer, 1) for kind in range(2)]
    spread_out = []
    for kind in range(2):
        for step in (1, 3):
            spread_out.append(move(kind, (z, y, x), first_peer(step), 1 + step))
    plane_started = plane_send(line_one, plane_one, line_started, sums, 0)
    for copy in to_x:
        copy.wait_recv()
    for kind in range(2):
        for step in (1, 3):
            spread_out.append(move(kind, (z, y, 1 - x), second_peer(step), 4 + step))
    first_block, second_block = spread_out[:4], spread_out[4:]
    for kind, step, back in ((0, 1, 3), (1, 3, 1)):
        first_block[2 * kind + step // 2].wait_recv()
        place = (lax.rem(z + back * x, 4), lax.rem(y + back * (1 - x), 4), x)
        spread_out.append(move(kind, place, first_peer(step), 3))
    total = plane_sum(plane_one, plane_started)
    mean = total[0:1, :] / total_rows
    scale = lax.rsqrt(total[1:2, :] / total_rows - mean * mean + EPS)
    stats_one_out[...] = jnp.concatenate([mean, scale], axis=0)
    pre = (values - mean) * scale * gain_ref[...][None, :] + bias_ref[...][None, :]
    active = gelu_value(pre).astype(middle.dtype)
    for window in range(2):
        middle[window] = active[window * 64 : window * 64 + 64, :]
        padded[window, 16:80, :] = active[window * 64 : window * 64 + 64, :]
    halos = halo_send(middle, low, high, moves, 19)
    for kind, step, back in ((0, 1, 3), (1, 3, 1)):
        second_block[2 * kind + step // 2].wait_recv()
        place = (lax.rem(z + back * (1 - x), 4), lax.rem(y + back * x, 4), 1 - x)
        spread_out.append(move(kind, place, second_peer(step), 6))
    waited = (first_block[0], first_block[3], second_block[0], second_block[3])
    for copy in spread_out:
        if all(copy is not other for other in waited):
            copy.wait_recv()
    whole = slice(None)
    blocks = [[], []]
    across = [[], []]

    def launch(kind):
        for step in (1, 3):
            blocks[kind].append(move(kind, (z, whole, 0), z_peer(step), 7 + step))
            blocks[kind].append(move(kind, (whole, y, 1), y_peer(step), 10 + step))
        across[kind].append(move(kind, (z, whole, 0), sibling, 14))
        across[kind].append(move(kind, (whole, y, 1), sibling, 15))

    def relay(kind):
        for i, (step, part) in enumerate(((1, slice(0, 2)), (3, slice(2, 4)))):
            from_z, from_y = lax.rem(z + 4 - step, 4), lax.rem(y + 4 - step, 4)
            blocks[kind][2 * i].wait_recv()
            blocks[kind].append(move(kind, (from_z, part, 0), z_peer(step), 9 if i == 0 else 24))
            blocks[kind][2 * i + 1].wait_recv()
            blocks[kind].append(move(kind, (part, from_y, 1), y_peer(step), 12 if i == 0 else 25))
            across[kind].append(move(kind, (from_z, whole, 0), sibling, 15 + step))
            across[kind].append(move(kind, (whole, from_y, 1), sibling, 20 + step))

    def finish(kind):
        blocks[kind][4].wait_recv()
        blocks[kind][6].wait_recv()
        across[kind].append(move(kind, (lax.rem(z + 2, 4), whole, 0), sibling, 17))
        blocks[kind][5].wait_recv()
        blocks[kind][7].wait_recv()
        across[kind].append(move(kind, (whole, lax.rem(y + 2, 4), 1), sibling, 22))

    launch(0)
    loads[3].wait()
    loads[4].wait()
    grad_out[...] = lax.dot_general(
        cot_ref[...], weight[...], SIDE, preferred_element_type=jnp.float32
    ).astype(grad_out.dtype)
    halo_fill(padded, low, high, halos)

    relay(0)
    launch(1)
    finish(0)
    for copy in across[0]:
        copy.wait_recv()
    stores = [pltpu.make_async_copy(conv_out, conv_to, own_sem.at[5])]
    stores[0].start()
    terms = {}
    for tap, half, start, size in TAP_PARTS:
        part = conv_out[half, :, :, :, :, start : start + size].reshape(-1, size)
        terms[tap, half] = jnp.dot(tap_rows(padded, 16 * tap), part, preferred_element_type=jnp.float32)
    middle_tap = jnp.concatenate([terms[1, 0], terms[1, 1]], axis=1)
    hidden = terms[0, 0] + middle_tap + terms[2, 1]
    hidden_out[...] = hidden
    line_two[line_place()] = stacked([hidden, hidden * hidden])
    line_again = line_send(line_two, sums, LINE + PLANE)
    relay(1)
    plane_again = plane_send(line_two, plane_two, line_again, sums, LINE + PLANE)
    finish(1)
    for copy in across[1]:
        copy.wait_recv()
    for i in range(4):
        for j in range(4):
            start = (i * 4 + j) * 48
            for half in range(2):
                pair = [mix_land[half, i, j, k].astype(jnp.float32) for k in range(2)]
                columns = slice(half * widths[1], half * widths[1] + widths[1])
                mix_out[start : start + 48, columns] = jnp.concatenate(pair, axis=0).astype(mix_out.dtype)
    stores.append(pltpu.make_async_copy(mix_out, mix_to, own_sem.at[6]))
    stores[1].start()
    stats_two_out[...] = plane_sum(plane_two, plane_again)
    ended = started + to_x + spread_out + halos + plane_started + line_again + plane_again
    for kind in range(2):
        ended += blocks[kind] + across[kind]
    for copy in ended:
        copy.wait_send()
    for copy in stores:
        copy.wait()


def front(inputs, conv_weight, mix_weight, gain, bias, cot, out_weight):
    vmem = pl.BlockSpec(memory_space=pltpu.VMEM)
    anywhere = pl.BlockSpec(memory_space=pl.ANY)
    width = inputs.shape[1]
    mid_width = conv_weight.shape[1] // 3
    kind = inputs.dtype
    conv_rows, mix_rows = conv_weight.shape[0], mix_weight.shape[0]
    full, wide = jnp.float32, conv_weight.shape[1]
    sems = 2 * (LINE + PLANE)
    conv_full, *rest = pl.pallas_call(
        front_kernel,
        out_shape=[
            jax.ShapeDtypeStruct((2, 4, 4, 2, 2 * conv_rows, wide // 2), kind),
            jax.ShapeDtypeStruct((64 * mix_rows, width), kind),
            jax.ShapeDtypeStruct((ROWS, mid_width), full),
            jax.ShapeDtypeStruct((2, width), full),
            jax.ShapeDtypeStruct((2, mid_width), full),
            jax.ShapeDtypeStruct((ROWS, out_weight.shape[0]), kind),
        ],
        in_specs=[anywhere] * 3 + [vmem] * 2 + [anywhere] * 2,
        out_specs=[anywhere] * 2 + [vmem] * 4,
        scratch_shapes=[
            pltpu.VMEM((2, 4, 4, 2, 2 * conv_rows, wide // 2), kind),
            pltpu.VMEM((64 * mix_rows, width), kind),
            pltpu.VMEM((LINE, 2, width), full),
            pltpu.VMEM((PLANE, 2, width), full),
            pltpu.VMEM((LINE, 2, mid_width), full),
            pltpu.VMEM((PLANE, 2, mid_width), full),
            pltpu.VMEM((conv_rows, wide // 2), kind),
            pltpu.VMEM((mix_rows, width // 2), kind),
            pltpu.VMEM((2, 4, 4, 2, 2 * mix_rows, width // 2), kind),
            pltpu.VMEM((2, 64, width), kind),
            pltpu.VMEM((2, 96, width), kind),
            pltpu.VMEM((2, 16, width), kind),
            pltpu.VMEM((2, 16, width), kind),
            pltpu.VMEM(out_weight.shape, kind),
            pltpu.VMEM(inputs.shape, kind),
            pltpu.VMEM(conv_weight.shape, kind),
            pltpu.VMEM(mix_weight.shape, kind),
            pltpu.VMEM(cot.shape, kind),
            pltpu.SemaphoreType.DMA((sems,)),
            pltpu.SemaphoreType.DMA((sems,)),
            pltpu.SemaphoreType.DMA((26, 2)),
            pltpu.SemaphoreType.DMA((26, 2)),
            pltpu.SemaphoreType.DMA((7,)),
        ],
        compiler_params=pltpu.CompilerParams(
            collective_id=1, has_side_effects=True, vmem_limit_bytes=62 * 1024 * 1024
        ),
        name="front",
    )(inputs, conv_weight, mix_weight, gain, bias, cot, out_weight)
    return [conv_full.reshape(2, -1, wide // 2)] + rest


LOW = VD
WIDE = VD + KD


def spots():
    seq = lax.axis_index("seq")
    core = lax.rem(seq, 2)
    z = seq // 16
    mine = (z // 2) * 8 + lax.rem(seq // 2, 8)
    return seq, core, lax.rem(z + z // 2, 2), mine


def pair_ahead(mine, step):
    return lax.rem(mine // 4 + step // 4, 4) * 4 + lax.rem(lax.rem(mine, 4) + step % 4, 4)


def pair_behind(mine, step):
    return lax.rem(mine // 4 + 4 - step // 4, 4) * 4 + lax.rem(lax.rem(mine, 4) + 4 - step % 4, 4)


def holder(pair, z_low, core):
    upper = pair // 8
    z = upper * 2 + lax.rem(z_low + upper, 2)
    return {"seq": z * 16 + lax.rem(pair, 8) * 2 + core}


def attention_peers(seq, core, z_low, mine):
    z_peer = holder(mine, 1 - z_low, core)
    sibling = {"seq": seq + 1 - 2 * core}
    return z_peer, sibling


def greet_attention(barrier):
    seq, core, z_low, mine = spots()
    peers = [holder(pair_ahead(mine, step), z_low, core) for step in range(1, 16)]
    peers += attention_peers(seq, core, z_low, mine)
    for peer in peers:
        pl.semaphore_signal(barrier, inc=1, device_id=peer, device_id_type=MESH)
    return len(peers)


def spread_heads(q_ref, k_ref, v_ref, g_ref, x_out, y_out, x_part, y_part, sems, meanwhile):
    seq, core, z_low, mine = spots()
    z_peer, sibling = attention_peers(seq, core, z_low, mine)
    for window in range(2):
        rows = slice(window * 64, window * 64 + 64)
        for head in range(H):
            pair = window * H + head
            y_part[pair, :, 0:LOW] = v_ref[rows, head * VD : head * VD + VD]
            y_part[pair, :, LOW:WIDE] = k_ref[rows, head * KD : head * KD + KD]

    def send(source, target, peer, slot):
        return remote(source, target, peer, sems, slot)

    y_sends = []
    for step in range(1, 16):
        pair = pair_ahead(mine, step)
        peer = holder(pair, z_low, core)
        y_sends.append(send(y_part.at[pair], y_out.at[z_low, core, mine], peer, step))
    for window in range(2):
        rows = slice(window * 64, window * 64 + 64)
        for head in range(H):
            pair = window * H + head
            x_part[pair, :, 0:LOW] = g_ref[rows, head * VD : head * VD + VD]
            x_part[pair, :, LOW:WIDE] = q_ref[rows, head * KD : head * KD + KD]
    x_sends = []
    for step in range(1, 16):
        pair = pair_ahead(mine, step)
        peer = holder(pair, z_low, core)
        x_sends.append(send(x_part.at[pair], x_out.at[mine], peer, 16 + step))
    y_out[z_low, core, mine] = y_part[mine]
    x_out[mine] = x_part[mine]
    along = []
    across = []
    for step in range(16):
        if step > 0:
            y_sends[step - 1].wait_recv()
        place = y_out.at[z_low, core, pair_behind(mine, step)]
        along.append(send(place, place, z_peer, 32 + step))
        across.append(send(place, place, sibling, 48 + step))
    meanwhile()
    for step in range(16):
        along[step].wait_recv()
        place = y_out.at[1 - z_low, core, pair_behind(mine, step)]
        across.append(send(place, place, sibling, 64 + step))
    for copy in x_sends + across:
        copy.wait_recv()
    for copy in y_sends + x_sends + along + across:
        copy.wait_send()


def collect_heads(
    oq_ref, vk_ref, a_ref, gq_ref, gv_ref, gk_ref, oq_got, vk_got, from_core, to_z, from_z, total, sems,
    meanwhile
):
    seq, core, z_low, mine = spots()
    z_peer, sibling = attention_peers(seq, core, z_low, mine)

    def send(source, target, peer, slot):
        return remote(source, target, peer, sems, 80 + slot)

    groups = [pl.ds(lax.rem(mine // 4 + k, 4) * 4, 4) for k in range(4)]
    across = []
    for far in range(2):
        z_part = 1 - z_low if far == 0 else z_low
        for k in range(4):
            across.append(
                send(
                    vk_ref.at[z_part, 1 - core, groups[k]],
                    from_core.at[far, groups[k]],
                    sibling,
                    4 * far + k,
                )
            )
    oq_sends = []
    for step in range(1, 16):
        pair = pair_ahead(mine, step)
        oq_sends.append(
            send(oq_ref.at[pair], oq_got.at[mine], holder(pair, z_low, core), 16 + step)
        )
    oq_got[mine] = oq_ref[mine]
    along = []
    for k in range(4):
        across[k].wait_recv()
        summed = vk_ref[1 - z_low, core, groups[k]].astype(jnp.float32) + from_core[
            0, groups[k]
        ].astype(jnp.float32)
        to_z[groups[k]] = summed.astype(to_z.dtype)
        along.append(send(to_z.at[groups[k]], from_z.at[groups[k]], z_peer, 8 + k))
    vk_sends = []
    for k in range(4):
        across[4 + k].wait_recv()
        along[k].wait_recv()
        summed = vk_ref[z_low, core, groups[k]].astype(jnp.float32) + from_core[
            1, groups[k]
        ].astype(jnp.float32)
        summed = summed + from_z[groups[k]].astype(jnp.float32)
        total[groups[k]] = summed.astype(total.dtype)
        for step in range(4 * k, 4 * k + 4):
            if step > 0:
                pair = pair_ahead(mine, step)
                vk_sends.append(
                    send(total.at[pair], vk_got.at[mine], holder(pair, z_low, core), 32 + step)
                )
    vk_got[mine] = total[mine]
    for copy in oq_sends:
        copy.wait_recv()
    for window in range(2):
        rows = slice(window * 64, window * 64 + 64)
        for head in range(H):
            pair = window * H + head
            a_ref[rows, head * VD : head * VD + VD] = oq_got[pair, :, 0:LOW]
            gq_ref[rows, head * KD : head * KD + KD] = oq_got[pair, :, LOW:WIDE]
    meanwhile()
    for copy in vk_sends:
        copy.wait_recv()
    for window in range(2):
        rows = slice(window * 64, window * 64 + 64)
        for head in range(H):
            pair = window * H + head
            gv_ref[rows, head * VD : head * VD + VD] = vk_got[pair, :, 0:LOW]
            gk_ref[rows, head * KD : head * KD + KD] = vk_got[pair, :, LOW:WIDE]
    for copy in across + oq_sends + along + vk_sends:
        copy.wait_send()


def attend_rows(x_ref, y_ref, oq_ref, vk_ref, y_turned, score, slope, total):
    keys = y_turned.shape[1]
    chunks = [slice(start, start + CHUNK) for start in range(0, keys, CHUNK)]

    def key_rows(part):
        quarter, first = part.start // 1024, part.start % 1024 // 64
        return y_ref[quarter // 2, quarter % 2, first : first + CHUNK // 64].reshape(CHUNK, WIDE)

    key_scale = KD ** (-0.5)
    for part in chunks:
        y_turned[:, part] = key_rows(part).T
    total[...] = jnp.zeros_like(total)

    def block(index, carry):
        rows = pl.ds(index * 4, 4)
        x_block = x_ref[rows].reshape(QUERY_BLOCK, WIDE)
        wide = x_block.astype(jnp.float32)
        low = lax.broadcasted_iota(jnp.int32, wide.shape, 1) < LOW
        query = jnp.where(low, 0.0, wide).astype(x_block.dtype)
        grad = jnp.where(low, wide, 0.0).astype(x_block.dtype)
        peak = None
        for part in chunks:
            scores = lax.dot_general(key_rows(part), query, SIDE, preferred_element_type=jnp.float32)
            score[part, :] = scores
            top = jnp.max(scores, axis=0, keepdims=True)
            peak = top if peak is None else jnp.maximum(peak, top)
        weight = jnp.zeros((1, QUERY_BLOCK), jnp.float32)
        center = jnp.zeros((1, QUERY_BLOCK), jnp.float32)
        for part in chunks:
            grads = lax.dot_general(key_rows(part), grad, SIDE, preferred_element_type=jnp.float32)
            slope[part, :] = grads
            terms = jnp.exp2((score[part, :] - peak) * (key_scale * 1.4426950408889634))
            score[part, :] = terms
            weight = weight + jnp.sum(terms, axis=0, keepdims=True)
            center = center + jnp.sum(terms * grads, axis=0, keepdims=True)
        share = 1.0 / weight
        center = center * share
        out = jnp.zeros((WIDE, QUERY_BLOCK), jnp.float32)
        back = jnp.zeros((WIDE, QUERY_BLOCK), jnp.float32)
        low_keys = lax.broadcasted_iota(jnp.int32, (CHUNK, WIDE), 1) < LOW
        for part in chunks:
            probs = score[part, :] * share
            prob_low = probs.astype(jnp.bfloat16)
            grads = (probs * (slope[part, :] - center)).astype(jnp.bfloat16)
            out = out + jnp.dot(y_turned[:, part], prob_low, preferred_element_type=jnp.float32)
            back = back + jnp.dot(y_turned[:, part], grads, preferred_element_type=jnp.float32)
            for_values = jnp.dot(prob_low, x_block, preferred_element_type=jnp.float32)
            for_keys = jnp.dot(grads, x_block, preferred_element_type=jnp.float32)
            total[part, :] += jnp.where(low_keys, for_values, for_keys)
        low_rows = lax.broadcasted_iota(jnp.int32, out.shape, 0) < LOW
        turned = jnp.where(low_rows, out, back * key_scale).T
        oq_ref[rows] = turned.reshape(4, 64, WIDE).astype(oq_ref.dtype)
        return carry

    lax.fori_loop(0, x_ref.shape[0] // 4, block, 0)
    low_keys = lax.broadcasted_iota(jnp.int32, (CHUNK, WIDE), 1) < LOW
    for part in chunks:
        quarter, first = part.start // 1024, part.start % 1024 // 64
        grads = total[part, :]
        grads = jnp.where(low_keys, grads, grads * key_scale).astype(vk_ref.dtype)
        pieces = slice(first, first + CHUNK // 64)
        vk_ref[quarter // 2, quarter % 2, pieces] = grads.reshape(CHUNK // 64, 64, WIDE)


def back_kernel(
    x_ref, hidden_ref, stats_one_ref, stats_two_ref, gain_two_ref, bias_two_ref, norm_ref,
    gain_ref, bias_ref, g_ref, cot_ref, mix_from, q_from, k_from, v_from, o_from, conv_from,
    encoded_out, out_ref, sums_two_out, sums_one_out,
    mix, q_weight, k_weight, v_weight, o_weight, weight,
    hat_two, slope_two, trunk, row_hat, mixed, hat_one, slope_one, q_rows, k_rows, v_rows,
    a_rows, gq_rows, gv_rows, gk_rows,
    x_part, y_part, x_got, y_got, y_turned, score, slope, total_vk, oq, vk,
    oq_got, vk_got, from_core, to_z, from_z, summed,
    line_two, plane_two, line_one, plane_one, middle, padded, low, high,
    head_send, head_recv, sum_send, sum_recv, move_send, move_recv, own_sem
):
    heads = (head_send, head_recv)
    sums = (sum_send, sum_recv)
    moves = (move_send, move_recv)
    total_rows = ROWS * lax.axis_size("seq") * lax.axis_size("batch")
    kind = x_ref.dtype
    full = jnp.float32
    barrier, count = greet_all()
    count += greet_attention(barrier)
    loads = [
        pltpu.make_async_copy(source, target, own_sem.at[i])
        for i, (source, target) in enumerate(
            (
                (mix_from, mix),
                (q_from, q_weight),
                (k_from, k_weight),
                (v_from, v_weight),
                (o_from, o_weight),
                (conv_from, weight),
            )
        )
    ]
    for load in loads:
        load.start()
    mean_two = stats_two_ref[0:1, :] / total_rows
    scale_two = lax.rsqrt(stats_two_ref[1:2, :] / total_rows - mean_two * mean_two + EPS)
    hat = (hidden_ref[...] - mean_two) * scale_two
    pre = hat * gain_two_ref[...][None, :] + bias_two_ref[...][None, :]
    hat_two[...] = hat
    loads[0].wait()
    trunk[...] = (
        x_ref[...].astype(full)
        + jnp.dot(gelu_value(pre).astype(kind), mix[...], preferred_element_type=full)
    ).astype(kind)
    rows = trunk[...].astype(full)
    centered = rows - jnp.mean(rows, axis=-1, keepdims=True)
    row_scale = lax.rsqrt(jnp.mean(centered * centered, axis=-1, keepdims=True) + EPS)
    row_hat[...] = centered * row_scale
    norm_gain = norm_ref[...][None, :]
    normed = (row_hat[...] * norm_gain).astype(kind)
    for load, table, place in (
        (loads[3], v_weight, v_rows),
        (loads[2], k_weight, k_rows),
        (loads[1], q_weight, q_rows),
    ):
        load.wait()
        place[...] = jnp.dot(normed, table[...], preferred_element_type=full).astype(kind)
    pl.semaphore_wait(barrier, count)

    mean, scale = stats_one_ref[0:1, :], stats_one_ref[1:2, :]
    gain_one = gain_ref[...][None, :]

    def recall():
        slope_two[...] = gelu_slope(hat_two[...] * gain_two_ref[...][None, :] + bias_two_ref[...][None, :])
        hat_one[...] = (x_ref[...].astype(full) - mean) * scale
        slope_one[...] = gelu_slope(hat_one[...] * gain_one + bias_ref[...][None, :])

    def encode():
        loads[4].wait()
        encoded_out[...] = (
            trunk[...].astype(full) + jnp.dot(a_rows[...], o_weight[...], preferred_element_type=full)
        ).astype(kind)
        mixed[...] = lax.dot_general(gq_rows[...], q_weight[...], SIDE, preferred_element_type=full)

    spread_heads(q_rows, k_rows, v_rows, g_ref, x_got, y_got, x_part, y_part, heads, recall)
    attend_rows(x_got, y_got, oq, vk, y_turned, score, slope, total_vk)
    collect_heads(
        oq, vk, a_rows, gq_rows, gv_rows, gk_rows, oq_got, vk_got, from_core, to_z, from_z, summed,
        heads, encode
    )
    grad_normed = (
        mixed[...]
        + lax.dot_general(gk_rows[...], k_weight[...], SIDE, preferred_element_type=full)
        + lax.dot_general(gv_rows[...], v_weight[...], SIDE, preferred_element_type=full)
    )
    hats = row_hat[...]
    norm_part = jnp.sum(grad_normed * hats, axis=0, keepdims=True)
    grad_hat = grad_normed * norm_gain
    mixed[...] = cot_ref[...].astype(full) + row_scale * (
        grad_hat
        - jnp.mean(grad_hat, axis=-1, keepdims=True)
        - hats * jnp.mean(grad_hat * hats, axis=-1, keepdims=True)
    )
    grad_two = (
        lax.dot_general(mixed[...].astype(kind), mix[...], SIDE, preferred_element_type=full)
        * slope_two[...]
    )
    mid_width = grad_two.shape[1]
    place = line_place()
    line_two[place] = jnp.concatenate(
        [
            jnp.sum(grad_two, axis=0, keepdims=True),
            jnp.sum(grad_two * hat_two[...], axis=0, keepdims=True),
            norm_part[:, :mid_width],
            norm_part[:, mid_width:],
        ],
        axis=0,
    )
    started = line_send(line_two, sums, 0)
    plane_started = plane_send(line_two, plane_two, started, sums, 0)
    total = plane_sum(plane_two, plane_started)
    sums_two_out[...] = total
    hidden_grad = (
        gain_two_ref[...][None, :]
        * scale_two
        * (grad_two - total[0:1, :] / total_rows - hat_two[...] * total[1:2, :] / total_rows)
    ).astype(kind)
    for window in range(2):
        middle[window] = hidden_grad[window * 64 : window * 64 + 64, :]
        padded[window, 16:80, :] = hidden_grad[window * 64 : window * 64 + 64, :]
    halos = halo_send(middle, low, high, moves, 0)
    loads[5].wait()
    grad_act = None
    for tap, half, start, size in (TAP_PARTS[1], TAP_PARTS[2], TAP_PARTS[0], TAP_PARTS[3]):
        if tap == 0:
            halo_fill(padded, low, high, halos)
        first = 0 if half == 0 or tap == 2 else 384
        term = lax.dot_general(
            tap_rows(padded, 16 * (2 - tap))[:, first : first + size],
            weight[half, :, start : start + size],
            SIDE,
            preferred_element_type=jnp.float32,
        )
        grad_act = term if grad_act is None else grad_act + term
    grad_pre = grad_act * slope_one[...]
    line_one[place] = stacked([grad_pre, grad_pre * hat_one[...]])
    line_again = line_send(line_one, sums, LINE + PLANE)
    plane_again = plane_send(line_one, plane_one, line_again, sums, LINE + PLANE)
    total = plane_sum(plane_one, plane_again)
    sums_one_out[...] = total
    grad_rows = (
        gain_one
        * scale
        * (grad_pre - total[0:1, :] / total_rows - hat_one[...] * total[1:2, :] / total_rows)
    )
    out_ref[...] = (mixed[...] + grad_rows).astype(out_ref.dtype)
    for copy in started + plane_started + halos + line_again + plane_again:
        copy.wait_send()


def back(
    rows_in, hidden, stats_one, stats_two, gain_two, bias_two, norm_gain, gain_one, bias_one,
    grad_out, cot, mix_full, query_weight, key_weight, value_weight, out_weight, conv_full
):
    vmem = pl.BlockSpec(memory_space=pltpu.VMEM)
    anywhere = pl.BlockSpec(memory_space=pl.ANY)
    kind, full = rows_in.dtype, jnp.float32
    width, mid_width = rows_in.shape[1], hidden.shape[1]
    piece = (16, 64, WIDE)
    count = 4 * 16 * 64
    sems = 2 * (LINE + PLANE)
    weights = (mix_full, query_weight, key_weight, value_weight, out_weight, conv_full)
    scratch = [(table.shape, kind) for table in weights]
    scratch += [((ROWS, mid_width), full)] * 2 + [((ROWS, width), kind)] + [((ROWS, width), full)] * 4
    scratch += [((ROWS, H * KD), kind)] * 2 + [((ROWS, H * VD), kind)] * 2
    scratch += [((ROWS, H * KD), kind), ((ROWS, H * VD), kind), ((ROWS, H * KD), kind)]
    scratch += [(piece, kind)] * 3 + [((2, 2) + piece, kind), ((WIDE, count), kind)]
    scratch += [((count, QUERY_BLOCK), full)] * 2 + [((count, WIDE), full)]
    scratch += [(piece, kind), ((2, 2) + piece, kind), (piece, kind), (piece, kind)]
    scratch += [((2,) + piece, kind)] + [(piece, kind)] * 3
    scratch += [((LINE, 4, mid_width), full), ((PLANE, 4, mid_width), full)]
    scratch += [((LINE, 2, width), full), ((PLANE, 2, width), full)]
    scratch += [((2, 64, mid_width), kind), ((2, 96, mid_width), kind)] + [((2, 16, mid_width), kind)] * 2
    dma = pltpu.SemaphoreType.DMA
    return pl.pallas_call(
        back_kernel,
        out_shape=[
            jax.ShapeDtypeStruct((ROWS, width), kind),
            jax.ShapeDtypeStruct((ROWS, width), kind),
            jax.ShapeDtypeStruct((4, mid_width), full),
            jax.ShapeDtypeStruct((2, width), full),
        ],
        in_specs=[vmem] * 11 + [anywhere] * 6,
        out_specs=[vmem] * 4,
        scratch_shapes=[pltpu.VMEM(shape, held) for shape, held in scratch]
        + [dma((128,)), dma((128,)), dma((sems,)), dma((sems,)), dma((1, 2)), dma((1, 2)), dma((6,))],
        compiler_params=pltpu.CompilerParams(
            collective_id=2, has_side_effects=True, vmem_limit_bytes=62 * 1024 * 1024
        ),
        name="back",
    )(
        rows_in, hidden, stats_one, stats_two, gain_two, bias_two, norm_gain, gain_one, bias_one,
        grad_out, cot, *weights
    )


def finish_kernel(
    encoded_from, grad_from, two_ref, one_ref,
    encoded_to, grad_to, gain_one, bias_one, gain_two, bias_two, gain_norm, own_sem
):
    copies = [
        pltpu.make_async_copy(encoded_from, encoded_to, own_sem.at[0]),
        pltpu.make_async_copy(grad_from, grad_to, own_sem.at[1]),
    ]
    for copy in copies:
        copy.start()
    mid_width = two_ref.shape[1]
    bias_one[...] = one_ref[0, :]
    gain_one[...] = one_ref[1, :]
    bias_two[...] = two_ref[0, :]
    gain_two[...] = two_ref[1, :]
    gain_norm[0:mid_width] = two_ref[2, :]
    gain_norm[mid_width : 2 * mid_width] = two_ref[3, :]
    for copy in copies:
        copy.wait()


def finish(encoded, grad_inputs, sums_two, sums_one):
    vmem = pl.BlockSpec(memory_space=pltpu.VMEM)
    anywhere = pl.BlockSpec(memory_space=pl.ANY)
    width, mid_width = sums_one.shape[1], sums_two.shape[1]
    full = jnp.float32
    return pl.pallas_call(
        finish_kernel,
        out_shape=[
            jax.ShapeDtypeStruct(encoded.shape, encoded.dtype),
            jax.ShapeDtypeStruct(grad_inputs.shape, grad_inputs.dtype),
            jax.ShapeDtypeStruct((width,), full),
            jax.ShapeDtypeStruct((width,), full),
            jax.ShapeDtypeStruct((mid_width,), full),
            jax.ShapeDtypeStruct((mid_width,), full),
            jax.ShapeDtypeStruct((2 * mid_width,), full),
        ],
        in_specs=[anywhere] * 2 + [vmem] * 2,
        out_specs=[anywhere] * 2 + [vmem] * 5,
        scratch_shapes=[pltpu.SemaphoreType.DMA((2,))],
        compiler_params=pltpu.CompilerParams(vmem_limit_bytes=62 * 1024 * 1024),
        name="finish",
    )(encoded, grad_inputs, sums_two, sums_one)


def on_device(
    inputs,
    conv_weight,
    mix_weight,
    first_gain,
    first_bias,
    second_gain,
    second_bias,
    norm_gain,
    query_weight,
    key_weight,
    value_weight,
    out_weight,
    cotangent,
):
    windows_here, local_bins, model_width = inputs.shape
    local_count = windows_here * local_bins
    rows_in = inputs.reshape(local_count, model_width)
    cot_flat = cotangent.reshape(local_count, model_width)
    conv_full, mix_full, hidden, stats_one, stats_two, grad_out = front(
        rows_in, conv_weight, mix_weight, first_gain, first_bias, cot_flat, out_weight
    )
    encoded_rows, grad_rows, sums_two, sums_one = back(
        rows_in,
        hidden,
        stats_one,
        stats_two,
        second_gain,
        second_bias,
        norm_gain,
        first_gain,
        first_bias,
        grad_out,
        cot_flat,
        mix_full,
        query_weight,
        key_weight,
        value_weight,
        out_weight,
        conv_full,
    )
    whole = (windows_here, local_bins, model_width)
    return finish(encoded_rows.reshape(whole), grad_rows.reshape(whole), sums_two, sums_one)


def solution(mesh):
    in_specs = (
        P("batch", "seq", None),
        P("seq", None),
        P("seq", None),
        P(),
        P(),
        P(),
        P(),
        P(),
        P(),
        P(),
        P(),
        P(),
        P("batch", "seq", None),
    )
    out_specs = (P("batch", "seq", None), P("batch", "seq", None), P(), P(), P(), P(), P())
    return jax.shard_map(
        on_device, mesh=mesh, in_specs=in_specs, out_specs=out_specs, check_vma=False
    )
```

```python
import jax
import jax.numpy as jnp
from jax import lax
from jax.experimental import pallas as pl
from jax.experimental.pallas import tpu as pltpu
from jax.sharding import PartitionSpec as P

H = 8
KD = 64
VD = 192
DILATION_STEP = 16


EPS = 1e-05
GELU_C = 0.7978845608028654


MESH = pl.DeviceIdType.MESH
ROWS = 128
LINE = 8
PLANE = 16
TAP_PARTS = ((0, 0, 0, 768), (1, 0, 768, 384), (1, 1, 0, 384), (2, 1, 384, 768))


def seq_of(z, y, x, core):
    return ((z * 4 + y) * 2 + x) * 2 + core


def remote(source, target, peer, sems, slot):
    copy = pltpu.make_async_remote_copy(
        src_ref=source,
        dst_ref=target,
        send_sem=sems[0].at[slot],
        recv_sem=sems[1].at[slot],
        device_id=peer,
        device_id_type=MESH,
    )
    copy.start()
    return copy


def line_place():
    return lax.axis_index("batch") * 4 + lax.rem(lax.axis_index("seq"), 4)


def line_peer(step):
    other = lax.rem(line_place() + step, LINE)
    spot = lax.axis_index("seq") // 4
    return {"seq": spot * 4 + lax.rem(other, 4), "batch": other // 4}


def plane_peer(step):
    seq = lax.axis_index("seq")
    return {"seq": lax.rem(seq // 4 + step, PLANE) * 4 + lax.rem(seq, 4)}


def ring_peer(step):
    count = 4 * PLANE
    return {"seq": lax.rem(lax.axis_index("seq") + step + count, count)}


def greet_all():
    barrier = pltpu.get_barrier_semaphore()
    peers = [line_peer(step) for step in range(1, LINE)]
    peers += [plane_peer(step) for step in range(1, PLANE)]
    peers += [ring_peer(1), ring_peer(-1)]
    for peer in peers:
        pl.semaphore_signal(barrier, inc=1, device_id=peer, device_id_type=MESH)
    return barrier, len(peers)


def line_send(line, sems, base):
    place = line.at[line_place()]
    return [remote(place, place, line_peer(step), sems, base + step) for step in range(1, LINE)]


def plane_send(line, plane, arrivals, sems, base):
    for copy in arrivals:
        copy.wait_recv()
    total = line[0]
    for i in range(1, LINE):
        total = total + line[i]
    spot = lax.axis_index("seq") // 4
    plane[spot] = total
    place = plane.at[spot]
    return [
        remote(place, place, plane_peer(step), sems, base + LINE + step) for step in range(1, PLANE)
    ]


def plane_sum(plane, arrivals):
    for copy in arrivals:
        copy.wait_recv()
    total = plane[0]
    for i in range(1, PLANE):
        total = total + plane[i]
    return total


def halo_send(middle, low, high, sems, base):
    return [
        remote(middle.at[:, 48:64, :], low, ring_peer(1), sems, (base, 0)),
        remote(middle.at[:, 0:16, :], high, ring_peer(-1), sems, (base, 1)),
    ]


def halo_fill(padded, low, high, copies):
    seq = lax.axis_index("seq")
    last = lax.axis_size("seq") - 1
    for copy in copies:
        copy.wait_recv()
    low_rows = low[...].astype(jnp.float32)
    high_rows = high[...].astype(jnp.float32)
    padded[:, 0:16, :] = jnp.where(seq == 0, 0.0, low_rows).astype(padded.dtype)
    padded[:, 80:96, :] = jnp.where(seq == last, 0.0, high_rows).astype(padded.dtype)


def tap_rows(padded, start):
    return jnp.concatenate([padded[0, start : start + 64, :], padded[1, start : start + 64, :]], axis=0)


def stacked(rows):
    return jnp.concatenate([jnp.sum(part, axis=0, keepdims=True) for part in rows], axis=0)


def gelu_value(values):
    cubic = GELU_C * (values + 0.044715 * values * values * values)
    return 0.5 * values * (1.0 + jnp.tanh(cubic))


def gelu_slope(values):
    tangent = jnp.tanh(GELU_C * (values + 0.044715 * values * values * values))
    return 0.5 * (1.0 + tangent) + 0.5 * values * (1.0 - tangent * tangent) * GELU_C * (
        1.0 + 3.0 * 0.044715 * values * values
    )


def rounded(values):
    return lax.optimization_barrier(values.astype(jnp.bfloat16)).astype(jnp.float32)


CHUNK = 256
QUERY_BLOCK = 256
SIDE = (((1,), (1,)), ((), ()))
def front_kernel(
    x_from, conv_from, mix_from, gain_ref, bias_ref, cot_from, out_weight_ref,
    conv_to, mix_to, hidden_out, stats_one_out, stats_two_out, grad_out,
    conv_out, mix_out, line_one, plane_one, line_two, plane_two, conv_other, mix_other, mix_land, middle, padded,
    low, high, weight, x_ref, conv_ref, mix_ref, cot_ref, sum_send, sum_recv, move_send, move_recv, own_sem
):
    seq = lax.axis_index("seq")
    core = lax.rem(seq, 2)
    x = lax.rem(seq // 2, 2)
    y = lax.rem(seq // 4, 4)
    z = seq // 16
    sums = (sum_send, sum_recv)
    moves = (move_send, move_recv)
    total_rows = ROWS * lax.axis_size("seq") * lax.axis_size("batch")
    barrier, count = greet_all()
    loads = [
        pltpu.make_async_copy(source, target, own_sem.at[i])
        for i, (source, target) in enumerate(
            (
                (x_from, x_ref),
                (conv_from, conv_ref),
                (mix_from, mix_ref),
                (cot_from, cot_ref),
                (out_weight_ref, weight),
            )
        )
    ]
    for load in loads:
        load.start()
    loads[0].wait()
    values = x_ref[...].astype(jnp.float32)
    line_one[line_place()] = stacked([values, values * values])
    pl.semaphore_wait(barrier, count)

    def first_peer(step):
        return {"seq": seq_of(lax.rem(z + step * x, 4), lax.rem(y + step * (1 - x), 4), x, core)}

    def second_peer(step):
        return {"seq": seq_of(lax.rem(z + step * (1 - x), 4), lax.rem(y + step * x, 4), x, core)}

    def y_peer(step):
        return {"seq": seq_of(z, lax.rem(y + step, 4), x, core)}

    def z_peer(step):
        return {"seq": seq_of(lax.rem(z + step, 4), y, x, core)}

    x_peer = {"seq": seq_of(z, y, 1 - x, core)}
    sibling = {"seq": seq_of(z, y, x, 1 - core)}
    outs = (conv_out, mix_land)
    widths = (conv_ref.shape[1] // 2, mix_ref.shape[1] // 2)
    halves = [pl.ds(pl.multiple_of(core * w, w), w) for w in widths]
    far_halves = [pl.ds(pl.multiple_of((1 - core) * w, w), w) for w in widths]

    def move(kind, where, peer, slot):
        place = outs[kind].at[(core, *where)]
        return remote(place, place, peer, moves, (slot, kind))

    started = line_send(line_one, sums, 0)
    line_started = started
    pair_up = [
        remote(conv_from.at[:, far_halves[0]], conv_other, sibling, moves, (0, 0)),
        remote(mix_from.at[:, far_halves[1]], mix_other, sibling, moves, (0, 1)),
    ]
    started = started + pair_up
    for kind, mine, other in ((0, conv_ref, conv_other), (1, mix_ref, mix_other)):
        loads[1 + kind].wait()
        pair_up[kind].wait_recv()
        out = outs[kind]
        here = mine[:, halves[kind]].astype(jnp.float32)
        there = other[...].astype(jnp.float32)
        upper = jnp.where(core == 0, here, there)
        lower = jnp.where(core == 0, there, here)
        out[core, z, y, x] = jnp.concatenate([upper, lower], axis=0).astype(out.dtype)
    to_x = [move(kind, (z, y, x), x_peer, 1) for kind in range(2)]
    spread_out = []
    for kind in range(2):
        for step in (1, 3):
            spread_out.append(move(kind, (z, y, x), first_peer(step), 1 + step))
    plane_started = plane_send(line_one, plane_one, line_started, sums, 0)
    for copy in to_x:
        copy.wait_recv()
    for kind in range(2):
        for step in (1, 3):
            spread_out.append(move(kind, (z, y, 1 - x), second_peer(step), 4 + step))
    first_block, second_block = spread_out[:4], spread_out[4:]
    for kind, step, back in ((0, 1, 3), (1, 3, 1)):
        first_block[2 * kind + step // 2].wait_recv()
        place = (lax.rem(z + back * x, 4), lax.rem(y + back * (1 - x), 4), x)
        spread_out.append(move(kind, place, first_peer(step), 3))
    total = plane_sum(plane_one, plane_started)
    mean = total[0:1, :] / total_rows
    scale = lax.rsqrt(total[1:2, :] / total_rows - mean * mean + EPS)
    stats_one_out[...] = jnp.concatenate([mean, scale], axis=0)
    pre = (values - mean) * scale * gain_ref[...][None, :] + bias_ref[...][None, :]
    active = gelu_value(pre).astype(middle.dtype)
    for window in range(2):
        middle[window] = active[window * 64 : window * 64 + 64, :]
        padded[window, 16:80, :] = active[window * 64 : window * 64 + 64, :]
    halos = halo_send(middle, low, high, moves, 19)
    for kind, step, back in ((0, 1, 3), (1, 3, 1)):
        second_block[2 * kind + step // 2].wait_recv()
        place = (lax.rem(z + back * (1 - x), 4), lax.rem(y + back * x, 4), 1 - x)
        spread_out.append(move(kind, place, second_peer(step), 6))
    waited = (first_block[0], first_block[3], second_block[0], second_block[3])
    for copy in spread_out:
        if all(copy is not other for other in waited):
            copy.wait_recv()
    whole = slice(None)
    blocks = [[], []]
    across = [[], []]

    def launch(kind):
        for step in (1, 3):
            blocks[kind].append(move(kind, (z, whole, 0), z_peer(step), 7 + step))
            blocks[kind].append(move(kind, (whole, y, 1), y_peer(step), 10 + step))
        across[kind].append(move(kind, (z, whole, 0), sibling, 14))
        across[kind].append(move(kind, (whole, y, 1), sibling, 15))

    def relay(kind):
        for i, (step, part) in enumerate(((1, slice(0, 2)), (3, slice(2, 4)))):
            from_z, from_y = lax.rem(z + 4 - step, 4), lax.rem(y + 4 - step, 4)
            blocks[kind][2 * i].wait_recv()
            blocks[kind].append(move(kind, (from_z, part, 0), z_peer(step), 9 if i == 0 else 24))
            blocks[kind][2 * i + 1].wait_recv()
            blocks[kind].append(move(kind, (part, from_y, 1), y_peer(step), 12 if i == 0 else 25))
            across[kind].append(move(kind, (from_z, whole, 0), sibling, 15 + step))
            across[kind].append(move(kind, (whole, from_y, 1), sibling, 20 + step))

    def finish(kind):
        blocks[kind][4].wait_recv()
        blocks[kind][6].wait_recv()
        across[kind].append(move(kind, (lax.rem(z + 2, 4), whole, 0), sibling, 17))
        blocks[kind][5].wait_recv()
        blocks[kind][7].wait_recv()
        across[kind].append(move(kind, (whole, lax.rem(y + 2, 4), 1), sibling, 22))

    launch(0)
    loads[3].wait()
    loads[4].wait()
    grad_out[...] = lax.dot_general(
        cot_ref[...], weight[...], SIDE, preferred_element_type=jnp.float32
    ).astype(grad_out.dtype)
    halo_fill(padded, low, high, halos)

    relay(0)
    launch(1)
    finish(0)
    for copy in across[0]:
        copy.wait_recv()
    stores = [pltpu.make_async_copy(conv_out, conv_to, own_sem.at[5])]
    stores[0].start()
    terms = {}
    for tap, half, start, size in TAP_PARTS:
        part = conv_out[half, :, :, :, :, start : start + size].reshape(-1, size)
        terms[tap, half] = jnp.dot(tap_rows(padded, 16 * tap), part, preferred_element_type=jnp.float32)
    middle_tap = jnp.concatenate([terms[1, 0], terms[1, 1]], axis=1)
    hidden = terms[0, 0] + middle_tap + terms[2, 1]
    hidden_out[...] = hidden
    line_two[line_place()] = stacked([hidden, hidden * hidden])
    line_again = line_send(line_two, sums, LINE + PLANE)
    relay(1)
    plane_again = plane_send(line_two, plane_two, line_again, sums, LINE + PLANE)
    finish(1)
    for copy in across[1]:
        copy.wait_recv()
    for i in range(4):
        for j in range(4):
            start = (i * 4 + j) * 48
            for half in range(2):
                pair = [mix_land[half, i, j, k].astype(jnp.float32) for k in range(2)]
                columns = slice(half * widths[1], half * widths[1] + widths[1])
                mix_out[start : start + 48, columns] = jnp.concatenate(pair, axis=0).astype(mix_out.dtype)
    stores.append(pltpu.make_async_copy(mix_out, mix_to, own_sem.at[6]))
    stores[1].start()
    stats_two_out[...] = plane_sum(plane_two, plane_again)
    ended = started + to_x + spread_out + halos + plane_started + line_again + plane_again
    for kind in range(2):
        ended += blocks[kind] + across[kind]
    for copy in ended:
        copy.wait_send()
    for copy in stores:
        copy.wait()


def front(inputs, conv_weight, mix_weight, gain, bias, cot, out_weight):
    vmem = pl.BlockSpec(memory_space=pltpu.VMEM)
    anywhere = pl.BlockSpec(memory_space=pl.ANY)
    width = inputs.shape[1]
    mid_width = conv_weight.shape[1] // 3
    kind = inputs.dtype
    conv_rows, mix_rows = conv_weight.shape[0], mix_weight.shape[0]
    full, wide = jnp.float32, conv_weight.shape[1]
    sems = 2 * (LINE + PLANE)
    conv_full, *rest = pl.pallas_call(
        front_kernel,
        out_shape=[
            jax.ShapeDtypeStruct((2, 4, 4, 2, 2 * conv_rows, wide // 2), kind),
            jax.ShapeDtypeStruct((64 * mix_rows, width), kind),
            jax.ShapeDtypeStruct((ROWS, mid_width), full),
            jax.ShapeDtypeStruct((2, width), full),
            jax.ShapeDtypeStruct((2, mid_width), full),
            jax.ShapeDtypeStruct((ROWS, out_weight.shape[0]), kind),
        ],
        in_specs=[anywhere] * 3 + [vmem] * 2 + [anywhere] * 2,
        out_specs=[anywhere] * 2 + [vmem] * 4,
        scratch_shapes=[
            pltpu.VMEM((2, 4, 4, 2, 2 * conv_rows, wide // 2), kind),
            pltpu.VMEM((64 * mix_rows, width), kind),
            pltpu.VMEM((LINE, 2, width), full),
            pltpu.VMEM((PLANE, 2, width), full),
            pltpu.VMEM((LINE, 2, mid_width), full),
            pltpu.VMEM((PLANE, 2, mid_width), full),
            pltpu.VMEM((conv_rows, wide // 2), kind),
            pltpu.VMEM((mix_rows, width // 2), kind),
            pltpu.VMEM((2, 4, 4, 2, 2 * mix_rows, width // 2), kind),
            pltpu.VMEM((2, 64, width), kind),
            pltpu.VMEM((2, 96, width), kind),
            pltpu.VMEM((2, 16, width), kind),
            pltpu.VMEM((2, 16, width), kind),
            pltpu.VMEM(out_weight.shape, kind),
            pltpu.VMEM(inputs.shape, kind),
            pltpu.VMEM(conv_weight.shape, kind),
            pltpu.VMEM(mix_weight.shape, kind),
            pltpu.VMEM(cot.shape, kind),
            pltpu.SemaphoreType.DMA((sems,)),
            pltpu.SemaphoreType.DMA((sems,)),
            pltpu.SemaphoreType.DMA((26, 2)),
            pltpu.SemaphoreType.DMA((26, 2)),
            pltpu.SemaphoreType.DMA((7,)),
        ],
        compiler_params=pltpu.CompilerParams(
            collective_id=1, has_side_effects=True, vmem_limit_bytes=62 * 1024 * 1024
        ),
        name="front",
    )(inputs, conv_weight, mix_weight, gain, bias, cot, out_weight)
    return [conv_full.reshape(2, -1, wide // 2)] + rest


LOW = VD
WIDE = VD + KD


def spots():
    seq = lax.axis_index("seq")
    core = lax.rem(seq, 2)
    z = seq // 16
    mine = (z // 2) * 8 + lax.rem(seq // 2, 8)
    return seq, core, lax.rem(z + z // 2, 2), mine


def pair_ahead(mine, step):
    return lax.rem(mine // 4 + step // 4, 4) * 4 + lax.rem(lax.rem(mine, 4) + step % 4, 4)


def pair_behind(mine, step):
    return lax.rem(mine // 4 + 4 - step // 4, 4) * 4 + lax.rem(lax.rem(mine, 4) + 4 - step % 4, 4)


def holder(pair, z_low, core):
    upper = pair // 8
    z = upper * 2 + lax.rem(z_low + upper, 2)
    return {"seq": z * 16 + lax.rem(pair, 8) * 2 + core}


def attention_peers(seq, core, z_low, mine):
    z_peer = holder(mine, 1 - z_low, core)
    sibling = {"seq": seq + 1 - 2 * core}
    return z_peer, sibling


def greet_attention(barrier):
    seq, core, z_low, mine = spots()
    peers = [holder(pair_ahead(mine, step), z_low, core) for step in range(1, 16)]
    peers += attention_peers(seq, core, z_low, mine)
    for peer in peers:
        pl.semaphore_signal(barrier, inc=1, device_id=peer, device_id_type=MESH)
    return len(peers)


def spread_heads(q_ref, k_ref, v_ref, g_ref, x_out, y_out, x_part, y_part, sems, meanwhile):
    seq, core, z_low, mine = spots()
    z_peer, sibling = attention_peers(seq, core, z_low, mine)
    for window in range(2):
        rows = slice(window * 64, window * 64 + 64)
        for head in range(H):
            pair = window * H + head
            y_part[pair, :, 0:LOW] = v_ref[rows, head * VD : head * VD + VD]
            y_part[pair, :, LOW:WIDE] = k_ref[rows, head * KD : head * KD + KD]

    def send(source, target, peer, slot):
        return remote(source, target, peer, sems, slot)

    y_sends = []
    for step in range(1, 16):
        pair = pair_ahead(mine, step)
        peer = holder(pair, z_low, core)
        y_sends.append(send(y_part.at[pair], y_out.at[z_low, core, mine], peer, step))
    for window in range(2):
        rows = slice(window * 64, window * 64 + 64)
        for head in range(H):
            pair = window * H + head
            x_part[pair, :, 0:LOW] = g_ref[rows, head * VD : head * VD + VD]
            x_part[pair, :, LOW:WIDE] = q_ref[rows, head * KD : head * KD + KD]
    x_sends = []
    for step in range(1, 16):
        pair = pair_ahead(mine, step)
        peer = holder(pair, z_low, core)
        x_sends.append(send(x_part.at[pair], x_out.at[mine], peer, 16 + step))
    y_out[z_low, core, mine] = y_part[mine]
    x_out[mine] = x_part[mine]
    along = []
    across = []
    for step in range(16):
        if step > 0:
            y_sends[step - 1].wait_recv()
        place = y_out.at[z_low, core, pair_behind(mine, step)]
        along.append(send(place, place, z_peer, 32 + step))
        across.append(send(place, place, sibling, 48 + step))
    meanwhile()
    for step in range(16):
        along[step].wait_recv()
        place = y_out.at[1 - z_low, core, pair_behind(mine, step)]
        across.append(send(place, place, sibling, 64 + step))
    for copy in x_sends + across:
        copy.wait_recv()
    for copy in y_sends + x_sends + along + across:
        copy.wait_send()


def collect_heads(
    oq_ref, vk_ref, a_ref, gq_ref, gv_ref, gk_ref, oq_got, vk_got, from_core, to_z, from_z, total, sems,
    meanwhile
):
    seq, core, z_low, mine = spots()
    z_peer, sibling = attention_peers(seq, core, z_low, mine)

    def send(source, target, peer, slot):
        return remote(source, target, peer, sems, 80 + slot)

    groups = [pl.ds(lax.rem(mine // 4 + k, 4) * 4, 4) for k in range(4)]
    across = []
    for far in range(2):
        z_part = 1 - z_low if far == 0 else z_low
        for k in range(4):
            across.append(
                send(
                    vk_ref.at[z_part, 1 - core, groups[k]],
                    from_core.at[far, groups[k]],
                    sibling,
                    4 * far + k,
                )
            )
    oq_sends = []
    for step in range(1, 16):
        pair = pair_ahead(mine, step)
        oq_sends.append(
            send(oq_ref.at[pair], oq_got.at[mine], holder(pair, z_low, core), 16 + step)
        )
    oq_got[mine] = oq_ref[mine]
    along = []
    for k in range(4):
        across[k].wait_recv()
        summed = vk_ref[1 - z_low, core, groups[k]].astype(jnp.float32) + from_core[
            0, groups[k]
        ].astype(jnp.float32)
        to_z[groups[k]] = summed.astype(to_z.dtype)
        along.append(send(to_z.at[groups[k]], from_z.at[groups[k]], z_peer, 8 + k))
    vk_sends = []
    for k in range(4):
        across[4 + k].wait_recv()
        along[k].wait_recv()
        summed = vk_ref[z_low, core, groups[k]].astype(jnp.float32) + from_core[
            1, groups[k]
        ].astype(jnp.float32)
        summed = summed + from_z[groups[k]].astype(jnp.float32)
        total[groups[k]] = summed.astype(total.dtype)
        for step in range(4 * k, 4 * k + 4):
            if step > 0:
                pair = pair_ahead(mine, step)
                vk_sends.append(
                    send(total.at[pair], vk_got.at[mine], holder(pair, z_low, core), 32 + step)
                )
    vk_got[mine] = total[mine]
    for copy in oq_sends:
        copy.wait_recv()
    for window in range(2):
        rows = slice(window * 64, window * 64 + 64)
        for head in range(H):
            pair = window * H + head
            a_ref[rows, head * VD : head * VD + VD] = oq_got[pair, :, 0:LOW]
            gq_ref[rows, head * KD : head * KD + KD] = oq_got[pair, :, LOW:WIDE]
    meanwhile()
    for copy in vk_sends:
        copy.wait_recv()
    for window in range(2):
        rows = slice(window * 64, window * 64 + 64)
        for head in range(H):
            pair = window * H + head
            gv_ref[rows, head * VD : head * VD + VD] = vk_got[pair, :, 0:LOW]
            gk_ref[rows, head * KD : head * KD + KD] = vk_got[pair, :, LOW:WIDE]
    for copy in across + oq_sends + along + vk_sends:
        copy.wait_send()


def attend_rows(x_ref, y_ref, oq_ref, vk_ref, y_turned, score, slope, total):
    keys = y_turned.shape[1]
    chunks = [slice(start, start + CHUNK) for start in range(0, keys, CHUNK)]

    def key_rows(part):
        quarter, first = part.start // 1024, part.start % 1024 // 64
        return y_ref[quarter // 2, quarter % 2, first : first + CHUNK // 64].reshape(CHUNK, WIDE)

    key_scale = KD ** (-0.5)
    for part in chunks:
        y_turned[:, part] = key_rows(part).T
    total[...] = jnp.zeros_like(total)

    def block(index, carry):
        rows = pl.ds(index * 4, 4)
        x_block = x_ref[rows].reshape(QUERY_BLOCK, WIDE)
        wide = x_block.astype(jnp.float32)
        low = lax.broadcasted_iota(jnp.int32, wide.shape, 1) < LOW
        query = jnp.where(low, 0.0, wide).astype(x_block.dtype)
        grad = jnp.where(low, wide, 0.0).astype(x_block.dtype)
        peak = None
        for part in chunks:
            scores = lax.dot_general(key_rows(part), query, SIDE, preferred_element_type=jnp.float32)
            score[part, :] = scores
            top = jnp.max(scores, axis=0, keepdims=True)
            peak = top if peak is None else jnp.maximum(peak, top)
        weight = jnp.zeros((1, QUERY_BLOCK), jnp.float32)
        center = jnp.zeros((1, QUERY_BLOCK), jnp.float32)
        for part in chunks:
            grads = lax.dot_general(key_rows(part), grad, SIDE, preferred_element_type=jnp.float32)
            slope[part, :] = grads
            terms = jnp.exp2((score[part, :] - peak) * (key_scale * 1.4426950408889634))
            score[part, :] = terms
            weight = weight + jnp.sum(terms, axis=0, keepdims=True)
            center = center + jnp.sum(terms * grads, axis=0, keepdims=True)
        share = 1.0 / weight
        center = center * share
        out = jnp.zeros((WIDE, QUERY_BLOCK), jnp.float32)
        back = jnp.zeros((WIDE, QUERY_BLOCK), jnp.float32)
        low_keys = lax.broadcasted_iota(jnp.int32, (CHUNK, WIDE), 1) < LOW
        for part in chunks:
            probs = score[part, :] * share
            prob_low = probs.astype(jnp.bfloat16)
            grads = (probs * (slope[part, :] - center)).astype(jnp.bfloat16)
            out = out + jnp.dot(y_turned[:, part], prob_low, preferred_element_type=jnp.float32)
            back = back + jnp.dot(y_turned[:, part], grads, preferred_element_type=jnp.float32)
            for_values = jnp.dot(prob_low, x_block, preferred_element_type=jnp.float32)
            for_keys = jnp.dot(grads, x_block, preferred_element_type=jnp.float32)
            total[part, :] += jnp.where(low_keys, for_values, for_keys)
        low_rows = lax.broadcasted_iota(jnp.int32, out.shape, 0) < LOW
        turned = jnp.where(low_rows, out, back * key_scale).T
        oq_ref[rows] = turned.reshape(4, 64, WIDE).astype(oq_ref.dtype)
        return carry

    lax.fori_loop(0, x_ref.shape[0] // 4, block, 0)
    low_keys = lax.broadcasted_iota(jnp.int32, (CHUNK, WIDE), 1) < LOW
    for part in chunks:
        quarter, first = part.start // 1024, part.start % 1024 // 64
        grads = total[part, :]
        grads = jnp.where(low_keys, grads, grads * key_scale).astype(vk_ref.dtype)
        pieces = slice(first, first + CHUNK // 64)
        vk_ref[quarter // 2, quarter % 2, pieces] = grads.reshape(CHUNK // 64, 64, WIDE)


def back_kernel(
    x_ref, hidden_ref, stats_one_ref, stats_two_ref, gain_two_ref, bias_two_ref, norm_ref,
    gain_ref, bias_ref, g_ref, cot_ref, mix_from, q_from, k_from, v_from, o_from, conv_from,
    encoded_out, out_ref, sums_two_out, sums_one_out,
    mix, q_weight, k_weight, v_weight, o_weight, weight,
    hat_two, slope_two, trunk, row_hat, mixed, hat_one, slope_one, q_rows, k_rows, v_rows,
    a_rows, gq_rows, gv_rows, gk_rows,
    x_part, y_part, x_got, y_got, y_turned, score, slope, total_vk, oq, vk,
    oq_got, vk_got, from_core, to_z, from_z, summed,
    line_two, plane_two, line_one, plane_one, middle, padded, low, high,
    head_send, head_recv, sum_send, sum_recv, move_send, move_recv, own_sem
):
    heads = (head_send, head_recv)
    sums = (sum_send, sum_recv)
    moves = (move_send, move_recv)
    total_rows = ROWS * lax.axis_size("seq") * lax.axis_size("batch")
    kind = x_ref.dtype
    full = jnp.float32
    barrier, count = greet_all()
    count += greet_attention(barrier)
    loads = [
        pltpu.make_async_copy(source, target, own_sem.at[i])
        for i, (source, target) in enumerate(
            (
                (mix_from, mix),
                (q_from, q_weight),
                (k_from, k_weight),
                (v_from, v_weight),
                (o_from, o_weight),
                (conv_from, weight),
            )
        )
    ]
    for load in loads[:4]:
        load.start()
    mean_two = stats_two_ref[0:1, :] / total_rows
    scale_two = lax.rsqrt(stats_two_ref[1:2, :] / total_rows - mean_two * mean_two + EPS)
    hat = (hidden_ref[...] - mean_two) * scale_two
    pre = hat * gain_two_ref[...][None, :] + bias_two_ref[...][None, :]
    hat_two[...] = hat
    loads[0].wait()
    trunk[...] = (
        x_ref[...].astype(full)
        + jnp.dot(gelu_value(pre).astype(kind), mix[...], preferred_element_type=full)
    ).astype(kind)
    rows = trunk[...].astype(full)
    centered = rows - jnp.mean(rows, axis=-1, keepdims=True)
    row_scale = lax.rsqrt(jnp.mean(centered * centered, axis=-1, keepdims=True) + EPS)
    row_hat[...] = centered * row_scale
    norm_gain = norm_ref[...][None, :]
    normed = (row_hat[...] * norm_gain).astype(kind)
    for load, table, place in (
        (loads[3], v_weight, v_rows),
        (loads[2], k_weight, k_rows),
        (loads[1], q_weight, q_rows),
    ):
        load.wait()
        place[...] = jnp.dot(normed, table[...], preferred_element_type=full).astype(kind)
    pl.semaphore_wait(barrier, count)

    mean, scale = stats_one_ref[0:1, :], stats_one_ref[1:2, :]
    gain_one = gain_ref[...][None, :]

    def recall():
        for load in loads[4:]:
            load.start()
        slope_two[...] = gelu_slope(hat_two[...] * gain_two_ref[...][None, :] + bias_two_ref[...][None, :])
        hat_one[...] = (x_ref[...].astype(full) - mean) * scale
        slope_one[...] = gelu_slope(hat_one[...] * gain_one + bias_ref[...][None, :])

    def encode():
        loads[4].wait()
        encoded_out[...] = (
            trunk[...].astype(full) + jnp.dot(a_rows[...], o_weight[...], preferred_element_type=full)
        ).astype(kind)
        mixed[...] = lax.dot_general(gq_rows[...], q_weight[...], SIDE, preferred_element_type=full)

    spread_heads(q_rows, k_rows, v_rows, g_ref, x_got, y_got, x_part, y_part, heads, recall)
    attend_rows(x_got, y_got, oq, vk, y_turned, score, slope, total_vk)
    collect_heads(
        oq, vk, a_rows, gq_rows, gv_rows, gk_rows, oq_got, vk_got, from_core, to_z, from_z, summed,
        heads, encode
    )
    grad_normed = (
        mixed[...]
        + lax.dot_general(gk_rows[...], k_weight[...], SIDE, preferred_element_type=full)
        + lax.dot_general(gv_rows[...], v_weight[...], SIDE, preferred_element_type=full)
    )
    hats = row_hat[...]
    norm_part = jnp.sum(grad_normed * hats, axis=0, keepdims=True)
    grad_hat = grad_normed * norm_gain
    mixed[...] = cot_ref[...].astype(full) + row_scale * (
        grad_hat
        - jnp.mean(grad_hat, axis=-1, keepdims=True)
        - hats * jnp.mean(grad_hat * hats, axis=-1, keepdims=True)
    )
    grad_two = (
        lax.dot_general(mixed[...].astype(kind), mix[...], SIDE, preferred_element_type=full)
        * slope_two[...]
    )
    mid_width = grad_two.shape[1]
    place = line_place()
    line_two[place] = jnp.concatenate(
        [
            jnp.sum(grad_two, axis=0, keepdims=True),
            jnp.sum(grad_two * hat_two[...], axis=0, keepdims=True),
            norm_part[:, :mid_width],
            norm_part[:, mid_width:],
        ],
        axis=0,
    )
    started = line_send(line_two, sums, 0)
    plane_started = plane_send(line_two, plane_two, started, sums, 0)
    total = plane_sum(plane_two, plane_started)
    sums_two_out[...] = total
    hidden_grad = (
        gain_two_ref[...][None, :]
        * scale_two
        * (grad_two - total[0:1, :] / total_rows - hat_two[...] * total[1:2, :] / total_rows)
    ).astype(kind)
    for window in range(2):
        middle[window] = hidden_grad[window * 64 : window * 64 + 64, :]
        padded[window, 16:80, :] = hidden_grad[window * 64 : window * 64 + 64, :]
    halos = halo_send(middle, low, high, moves, 0)
    loads[5].wait()
    grad_act = None
    for tap, half, start, size in (TAP_PARTS[1], TAP_PARTS[2], TAP_PARTS[0], TAP_PARTS[3]):
        if tap == 0:
            halo_fill(padded, low, high, halos)
        first = 0 if half == 0 or tap == 2 else 384
        term = lax.dot_general(
            tap_rows(padded, 16 * (2 - tap))[:, first : first + size],
            weight[half, :, start : start + size],
            SIDE,
            preferred_element_type=jnp.float32,
        )
        grad_act = term if grad_act is None else grad_act + term
    grad_pre = grad_act * slope_one[...]
    line_one[place] = stacked([grad_pre, grad_pre * hat_one[...]])
    line_again = line_send(line_one, sums, LINE + PLANE)
    plane_again = plane_send(line_one, plane_one, line_again, sums, LINE + PLANE)
    total = plane_sum(plane_one, plane_again)
    sums_one_out[...] = total
    grad_rows = (
        gain_one
        * scale
        * (grad_pre - total[0:1, :] / total_rows - hat_one[...] * total[1:2, :] / total_rows)
    )
    out_ref[...] = (mixed[...] + grad_rows).astype(out_ref.dtype)
    for copy in started + plane_started + halos + line_again + plane_again:
        copy.wait_send()


def back(
    rows_in, hidden, stats_one, stats_two, gain_two, bias_two, norm_gain, gain_one, bias_one,
    grad_out, cot, mix_full, query_weight, key_weight, value_weight, out_weight, conv_full
):
    vmem = pl.BlockSpec(memory_space=pltpu.VMEM)
    anywhere = pl.BlockSpec(memory_space=pl.ANY)
    kind, full = rows_in.dtype, jnp.float32
    width, mid_width = rows_in.shape[1], hidden.shape[1]
    piece = (16, 64, WIDE)
    count = 4 * 16 * 64
    sems = 2 * (LINE + PLANE)
    weights = (mix_full, query_weight, key_weight, value_weight, out_weight, conv_full)
    scratch = [(table.shape, kind) for table in weights]
    scratch += [((ROWS, mid_width), full)] * 2 + [((ROWS, width), kind)] + [((ROWS, width), full)] * 4
    scratch += [((ROWS, H * KD), kind)] * 2 + [((ROWS, H * VD), kind)] * 2
    scratch += [((ROWS, H * KD), kind), ((ROWS, H * VD), kind), ((ROWS, H * KD), kind)]
    scratch += [(piece, kind)] * 3 + [((2, 2) + piece, kind), ((WIDE, count), kind)]
    scratch += [((count, QUERY_BLOCK), full)] * 2 + [((count, WIDE), full)]
    scratch += [(piece, kind), ((2, 2) + piece, kind), (piece, kind), (piece, kind)]
    scratch += [((2,) + piece, kind)] + [(piece, kind)] * 3
    scratch += [((LINE, 4, mid_width), full), ((PLANE, 4, mid_width), full)]
    scratch += [((LINE, 2, width), full), ((PLANE, 2, width), full)]
    scratch += [((2, 64, mid_width), kind), ((2, 96, mid_width), kind)] + [((2, 16, mid_width), kind)] * 2
    dma = pltpu.SemaphoreType.DMA
    return pl.pallas_call(
        back_kernel,
        out_shape=[
            jax.ShapeDtypeStruct((ROWS, width), kind),
            jax.ShapeDtypeStruct((ROWS, width), kind),
            jax.ShapeDtypeStruct((4, mid_width), full),
            jax.ShapeDtypeStruct((2, width), full),
        ],
        in_specs=[vmem] * 11 + [anywhere] * 6,
        out_specs=[vmem] * 4,
        scratch_shapes=[pltpu.VMEM(shape, held) for shape, held in scratch]
        + [dma((128,)), dma((128,)), dma((sems,)), dma((sems,)), dma((1, 2)), dma((1, 2)), dma((6,))],
        compiler_params=pltpu.CompilerParams(
            collective_id=2, has_side_effects=True, vmem_limit_bytes=62 * 1024 * 1024
        ),
        name="back",
    )(
        rows_in, hidden, stats_one, stats_two, gain_two, bias_two, norm_gain, gain_one, bias_one,
        grad_out, cot, *weights
    )


def finish_kernel(
    encoded_from, grad_from, two_ref, one_ref,
    encoded_to, grad_to, gain_one, bias_one, gain_two, bias_two, gain_norm
):
    encoded_to[...] = encoded_from[...]
    grad_to[...] = grad_from[...]
    mid_width = two_ref.shape[1]
    bias_one[...] = one_ref[0, :]
    gain_one[...] = one_ref[1, :]
    bias_two[...] = two_ref[0, :]
    gain_two[...] = two_ref[1, :]
    gain_norm[0:mid_width] = two_ref[2, :]
    gain_norm[mid_width : 2 * mid_width] = two_ref[3, :]


def finish(encoded, grad_inputs, sums_two, sums_one):
    vmem = pl.BlockSpec(memory_space=pltpu.VMEM)
    width, mid_width = sums_one.shape[1], sums_two.shape[1]
    full = jnp.float32
    return pl.pallas_call(
        finish_kernel,
        out_shape=[
            jax.ShapeDtypeStruct(encoded.shape, encoded.dtype),
            jax.ShapeDtypeStruct(grad_inputs.shape, grad_inputs.dtype),
            jax.ShapeDtypeStruct((width,), full),
            jax.ShapeDtypeStruct((width,), full),
            jax.ShapeDtypeStruct((mid_width,), full),
            jax.ShapeDtypeStruct((mid_width,), full),
            jax.ShapeDtypeStruct((2 * mid_width,), full),
        ],
        in_specs=[vmem] * 4,
        out_specs=[vmem] * 7,
        compiler_params=pltpu.CompilerParams(vmem_limit_bytes=62 * 1024 * 1024),
        name="finish",
    )(encoded, grad_inputs, sums_two, sums_one)


def on_device(
    inputs,
    conv_weight,
    mix_weight,
    first_gain,
    first_bias,
    second_gain,
    second_bias,
    norm_gain,
    query_weight,
    key_weight,
    value_weight,
    out_weight,
    cotangent,
):
    windows_here, local_bins, model_width = inputs.shape
    local_count = windows_here * local_bins
    rows_in = inputs.reshape(local_count, model_width)
    cot_flat = cotangent.reshape(local_count, model_width)
    conv_full, mix_full, hidden, stats_one, stats_two, grad_out = front(
        rows_in, conv_weight, mix_weight, first_gain, first_bias, cot_flat, out_weight
    )
    encoded_rows, grad_rows, sums_two, sums_one = back(
        rows_in,
        hidden,
        stats_one,
        stats_two,
        second_gain,
        second_bias,
        norm_gain,
        first_gain,
        first_bias,
        grad_out,
        cot_flat,
        mix_full,
        query_weight,
        key_weight,
        value_weight,
        out_weight,
        conv_full,
    )
    whole = (windows_here, local_bins, model_width)
    return finish(encoded_rows.reshape(whole), grad_rows.reshape(whole), sums_two, sums_one)


def solution(mesh):
    in_specs = (
        P("batch", "seq", None),
        P("seq", None),
        P("seq", None),
        P(),
        P(),
        P(),
        P(),
        P(),
        P(),
        P(),
        P(),
        P(),
        P("batch", "seq", None),
    )
    out_specs = (P("batch", "seq", None), P("batch", "seq", None), P(), P(), P(), P(), P())
    return jax.shard_map(
        on_device, mesh=mesh, in_specs=in_specs, out_specs=out_specs, check_vma=False
    )
```

```python
import jax
import jax.numpy as jnp
from jax import lax
from jax.experimental import pallas as pl
from jax.experimental.pallas import tpu as pltpu
from jax.sharding import PartitionSpec as P

H = 8
KD = 64
VD = 192
DILATION_STEP = 16


EPS = 1e-05
GELU_C = 0.7978845608028654


MESH = pl.DeviceIdType.MESH
ROWS = 128
LINE = 8
PLANE = 16
TAP_PARTS = ((0, 0, 0, 768), (1, 0, 768, 384), (1, 1, 0, 384), (2, 1, 384, 768))


def seq_of(z, y, x, core):
    return ((z * 4 + y) * 2 + x) * 2 + core


def remote(source, target, peer, sems, slot):
    copy = pltpu.make_async_remote_copy(
        src_ref=source,
        dst_ref=target,
        send_sem=sems[0].at[slot],
        recv_sem=sems[1].at[slot],
        device_id=peer,
        device_id_type=MESH,
    )
    copy.start()
    return copy


def line_place():
    return lax.axis_index("batch") * 4 + lax.rem(lax.axis_index("seq"), 4)


def line_peer(step):
    other = lax.rem(line_place() + step, LINE)
    spot = lax.axis_index("seq") // 4
    return {"seq": spot * 4 + lax.rem(other, 4), "batch": other // 4}


def plane_peer(step):
    seq = lax.axis_index("seq")
    return {"seq": lax.rem(seq // 4 + step, PLANE) * 4 + lax.rem(seq, 4)}


def ring_peer(step):
    count = 4 * PLANE
    return {"seq": lax.rem(lax.axis_index("seq") + step + count, count)}


def greet_all():
    barrier = pltpu.get_barrier_semaphore()
    peers = [line_peer(step) for step in range(1, LINE)]
    peers += [plane_peer(step) for step in range(1, PLANE)]
    peers += [ring_peer(1), ring_peer(-1)]
    for peer in peers:
        pl.semaphore_signal(barrier, inc=1, device_id=peer, device_id_type=MESH)
    return barrier, len(peers)


def line_send(line, sems, base):
    place = line.at[line_place()]
    return [remote(place, place, line_peer(step), sems, base + step) for step in range(1, LINE)]


def plane_send(line, plane, arrivals, sems, base):
    for copy in arrivals:
        copy.wait_recv()
    total = line[0]
    for i in range(1, LINE):
        total = total + line[i]
    spot = lax.axis_index("seq") // 4
    plane[spot] = total
    place = plane.at[spot]
    return [
        remote(place, place, plane_peer(step), sems, base + LINE + step) for step in range(1, PLANE)
    ]


def plane_sum(plane, arrivals):
    for copy in arrivals:
        copy.wait_recv()
    total = plane[0]
    for i in range(1, PLANE):
        total = total + plane[i]
    return total


def halo_send(middle, low, high, sems, base):
    return [
        remote(middle.at[:, 48:64, :], low, ring_peer(1), sems, (base, 0)),
        remote(middle.at[:, 0:16, :], high, ring_peer(-1), sems, (base, 1)),
    ]


def halo_fill(padded, low, high, copies):
    seq = lax.axis_index("seq")
    last = lax.axis_size("seq") - 1
    for copy in copies:
        copy.wait_recv()
    low_rows = low[...].astype(jnp.float32)
    high_rows = high[...].astype(jnp.float32)
    padded[:, 0:16, :] = jnp.where(seq == 0, 0.0, low_rows).astype(padded.dtype)
    padded[:, 80:96, :] = jnp.where(seq == last, 0.0, high_rows).astype(padded.dtype)


def tap_rows(padded, start):
    return jnp.concatenate([padded[0, start : start + 64, :], padded[1, start : start + 64, :]], axis=0)


def stacked(rows):
    return jnp.concatenate([jnp.sum(part, axis=0, keepdims=True) for part in rows], axis=0)


def gelu_value(values):
    cubic = GELU_C * (values + 0.044715 * values * values * values)
    return 0.5 * values * (1.0 + jnp.tanh(cubic))


def gelu_slope(values):
    tangent = jnp.tanh(GELU_C * (values + 0.044715 * values * values * values))
    return 0.5 * (1.0 + tangent) + 0.5 * values * (1.0 - tangent * tangent) * GELU_C * (
        1.0 + 3.0 * 0.044715 * values * values
    )


def rounded(values):
    return lax.optimization_barrier(values.astype(jnp.bfloat16)).astype(jnp.float32)


CHUNK = 256
QUERY_BLOCK = 256
SIDE = (((1,), (1,)), ((), ()))
def front_kernel(
    x_from, conv_from, mix_from, gain_ref, bias_ref, cot_from, out_weight_ref,
    conv_to, mix_to, hidden_out, stats_one_out, stats_two_out, grad_out,
    conv_out, mix_out, line_one, plane_one, line_two, plane_two, conv_other, mix_other, mix_land, middle, padded,
    low, high, weight, x_ref, conv_ref, mix_ref, cot_ref, sum_send, sum_recv, move_send, move_recv, own_sem
):
    seq = lax.axis_index("seq")
    core = lax.rem(seq, 2)
    x = lax.rem(seq // 2, 2)
    y = lax.rem(seq // 4, 4)
    z = seq // 16
    sums = (sum_send, sum_recv)
    moves = (move_send, move_recv)
    total_rows = ROWS * lax.axis_size("seq") * lax.axis_size("batch")
    barrier, count = greet_all()
    loads = [
        pltpu.make_async_copy(source, target, own_sem.at[i])
        for i, (source, target) in enumerate(
            (
                (x_from, x_ref),
                (conv_from, conv_ref),
                (mix_from, mix_ref),
                (cot_from, cot_ref),
                (out_weight_ref, weight),
            )
        )
    ]
    for load in loads:
        load.start()
    loads[0].wait()
    values = x_ref[...].astype(jnp.float32)
    line_one[line_place()] = stacked([values, values * values])
    pl.semaphore_wait(barrier, count)

    def first_peer(step):
        return {"seq": seq_of(lax.rem(z + step * x, 4), lax.rem(y + step * (1 - x), 4), x, core)}

    def second_peer(step):
        return {"seq": seq_of(lax.rem(z + step * (1 - x), 4), lax.rem(y + step * x, 4), x, core)}

    def y_peer(step):
        return {"seq": seq_of(z, lax.rem(y + step, 4), x, core)}

    def z_peer(step):
        return {"seq": seq_of(lax.rem(z + step, 4), y, x, core)}

    x_peer = {"seq": seq_of(z, y, 1 - x, core)}
    sibling = {"seq": seq_of(z, y, x, 1 - core)}
    outs = (conv_out, mix_land)
    widths = (conv_ref.shape[1] // 2, mix_ref.shape[1] // 2)
    halves = [pl.ds(pl.multiple_of(core * w, w), w) for w in widths]
    far_halves = [pl.ds(pl.multiple_of((1 - core) * w, w), w) for w in widths]

    def move(kind, where, peer, slot):
        place = outs[kind].at[(core, *where)]
        return remote(place, place, peer, moves, (slot, kind))

    started = line_send(line_one, sums, 0)
    line_started = started
    pair_up = [
        remote(conv_from.at[:, far_halves[0]], conv_other, sibling, moves, (0, 0)),
        remote(mix_from.at[:, far_halves[1]], mix_other, sibling, moves, (0, 1)),
    ]
    started = started + pair_up
    for kind, mine, other in ((0, conv_ref, conv_other), (1, mix_ref, mix_other)):
        loads[1 + kind].wait()
        pair_up[kind].wait_recv()
        out = outs[kind]
        here = mine[:, halves[kind]].astype(jnp.float32)
        there = other[...].astype(jnp.float32)
        upper = jnp.where(core == 0, here, there)
        lower = jnp.where(core == 0, there, here)
        out[core, z, y, x] = jnp.concatenate([upper, lower], axis=0).astype(out.dtype)
    to_x = [move(kind, (z, y, x), x_peer, 1) for kind in range(2)]
    spread_out = []
    for kind in range(2):
        for step in (1, 3):
            spread_out.append(move(kind, (z, y, x), first_peer(step), 1 + step))
    plane_started = plane_send(line_one, plane_one, line_started, sums, 0)
    for copy in to_x:
        copy.wait_recv()
    for kind in range(2):
        for step in (1, 3):
            spread_out.append(move(kind, (z, y, 1 - x), second_peer(step), 4 + step))
    first_block, second_block = spread_out[:4], spread_out[4:]
    for kind, step, back in ((0, 1, 3), (1, 3, 1)):
        first_block[2 * kind + step // 2].wait_recv()
        place = (lax.rem(z + back * x, 4), lax.rem(y + back * (1 - x), 4), x)
        spread_out.append(move(kind, place, first_peer(step), 3))
    total = plane_sum(plane_one, plane_started)
    mean = total[0:1, :] / total_rows
    scale = lax.rsqrt(total[1:2, :] / total_rows - mean * mean + EPS)
    stats_one_out[...] = jnp.concatenate([mean, scale], axis=0)
    pre = (values - mean) * scale * gain_ref[...][None, :] + bias_ref[...][None, :]
    active = gelu_value(pre).astype(middle.dtype)
    for window in range(2):
        middle[window] = active[window * 64 : window * 64 + 64, :]
        padded[window, 16:80, :] = active[window * 64 : window * 64 + 64, :]
    halos = halo_send(middle, low, high, moves, 19)
    for kind, step, back in ((0, 1, 3), (1, 3, 1)):
        second_block[2 * kind + step // 2].wait_recv()
        place = (lax.rem(z + back * (1 - x), 4), lax.rem(y + back * x, 4), 1 - x)
        spread_out.append(move(kind, place, second_peer(step), 6))
    waited = (first_block[0], first_block[3], second_block[0], second_block[3])
    for copy in spread_out:
        if all(copy is not other for other in waited):
            copy.wait_recv()
    whole = slice(None)
    blocks = [[], []]
    across = [[], []]

    def launch(kind):
        for step in (1, 3):
            blocks[kind].append(move(kind, (z, whole, 0), z_peer(step), 7 + step))
            blocks[kind].append(move(kind, (whole, y, 1), y_peer(step), 10 + step))
        across[kind].append(move(kind, (z, whole, 0), sibling, 14))
        across[kind].append(move(kind, (whole, y, 1), sibling, 15))

    def relay(kind):
        for i, (step, part) in enumerate(((1, slice(0, 2)), (3, slice(2, 4)))):
            from_z, from_y = lax.rem(z + 4 - step, 4), lax.rem(y + 4 - step, 4)
            blocks[kind][2 * i].wait_recv()
            blocks[kind].append(move(kind, (from_z, part, 0), z_peer(step), 9 if i == 0 else 24))
            blocks[kind][2 * i + 1].wait_recv()
            blocks[kind].append(move(kind, (part, from_y, 1), y_peer(step), 12 if i == 0 else 25))
            across[kind].append(move(kind, (from_z, whole, 0), sibling, 15 + step))
            across[kind].append(move(kind, (whole, from_y, 1), sibling, 20 + step))

    def finish(kind):
        blocks[kind][4].wait_recv()
        blocks[kind][6].wait_recv()
        across[kind].append(move(kind, (lax.rem(z + 2, 4), whole, 0), sibling, 17))
        blocks[kind][5].wait_recv()
        blocks[kind][7].wait_recv()
        across[kind].append(move(kind, (whole, lax.rem(y + 2, 4), 1), sibling, 22))

    launch(0)
    loads[3].wait()
    loads[4].wait()
    grad_out[...] = lax.dot_general(
        cot_ref[...], weight[...], SIDE, preferred_element_type=jnp.float32
    ).astype(grad_out.dtype)
    halo_fill(padded, low, high, halos)

    relay(0)
    finish(0)
    launch(1)
    for copy in across[0]:
        copy.wait_recv()
    stores = [pltpu.make_async_copy(conv_out, conv_to, own_sem.at[5])]
    stores[0].start()
    terms = {}
    for tap, half, start, size in TAP_PARTS:
        part = conv_out[half, :, :, :, :, start : start + size].reshape(-1, size)
        terms[tap, half] = jnp.dot(tap_rows(padded, 16 * tap), part, preferred_element_type=jnp.float32)
    middle_tap = jnp.concatenate([terms[1, 0], terms[1, 1]], axis=1)
    hidden = terms[0, 0] + middle_tap + terms[2, 1]
    hidden_out[...] = hidden
    line_two[line_place()] = stacked([hidden, hidden * hidden])
    line_again = line_send(line_two, sums, LINE + PLANE)
    relay(1)
    plane_again = plane_send(line_two, plane_two, line_again, sums, LINE + PLANE)
    finish(1)
    for copy in across[1]:
        copy.wait_recv()
    for i in range(4):
        for j in range(4):
            start = (i * 4 + j) * 48
            for half in range(2):
                pair = [mix_land[half, i, j, k].astype(jnp.float32) for k in range(2)]
                columns = slice(half * widths[1], half * widths[1] + widths[1])
                mix_out[start : start + 48, columns] = jnp.concatenate(pair, axis=0).astype(mix_out.dtype)
    stores.append(pltpu.make_async_copy(mix_out, mix_to, own_sem.at[6]))
    stores[1].start()
    stats_two_out[...] = plane_sum(plane_two, plane_again)
    ended = started + to_x + spread_out + halos + plane_started + line_again + plane_again
    for kind in range(2):
        ended += blocks[kind] + across[kind]
    for copy in ended:
        copy.wait_send()
    for copy in stores:
        copy.wait()


def front(inputs, conv_weight, mix_weight, gain, bias, cot, out_weight):
    vmem = pl.BlockSpec(memory_space=pltpu.VMEM)
    anywhere = pl.BlockSpec(memory_space=pl.ANY)
    width = inputs.shape[1]
    mid_width = conv_weight.shape[1] // 3
    kind = inputs.dtype
    conv_rows, mix_rows = conv_weight.shape[0], mix_weight.shape[0]
    full, wide = jnp.float32, conv_weight.shape[1]
    sems = 2 * (LINE + PLANE)
    conv_full, *rest = pl.pallas_call(
        front_kernel,
        out_shape=[
            jax.ShapeDtypeStruct((2, 4, 4, 2, 2 * conv_rows, wide // 2), kind),
            jax.ShapeDtypeStruct((64 * mix_rows, width), kind),
            jax.ShapeDtypeStruct((ROWS, mid_width), full),
            jax.ShapeDtypeStruct((2, width), full),
            jax.ShapeDtypeStruct((2, mid_width), full),
            jax.ShapeDtypeStruct((ROWS, out_weight.shape[0]), kind),
        ],
        in_specs=[anywhere] * 3 + [vmem] * 2 + [anywhere] * 2,
        out_specs=[anywhere] * 2 + [vmem] * 4,
        scratch_shapes=[
            pltpu.VMEM((2, 4, 4, 2, 2 * conv_rows, wide // 2), kind),
            pltpu.VMEM((64 * mix_rows, width), kind),
            pltpu.VMEM((LINE, 2, width), full),
            pltpu.VMEM((PLANE, 2, width), full),
            pltpu.VMEM((LINE, 2, mid_width), full),
            pltpu.VMEM((PLANE, 2, mid_width), full),
            pltpu.VMEM((conv_rows, wide // 2), kind),
            pltpu.VMEM((mix_rows, width // 2), kind),
            pltpu.VMEM((2, 4, 4, 2, 2 * mix_rows, width // 2), kind),
            pltpu.VMEM((2, 64, width), kind),
            pltpu.VMEM((2, 96, width), kind),
            pltpu.VMEM((2, 16, width), kind),
            pltpu.VMEM((2, 16, width), kind),
            pltpu.VMEM(out_weight.shape, kind),
            pltpu.VMEM(inputs.shape, kind),
            pltpu.VMEM(conv_weight.shape, kind),
            pltpu.VMEM(mix_weight.shape, kind),
            pltpu.VMEM(cot.shape, kind),
            pltpu.SemaphoreType.DMA((sems,)),
            pltpu.SemaphoreType.DMA((sems,)),
            pltpu.SemaphoreType.DMA((26, 2)),
            pltpu.SemaphoreType.DMA((26, 2)),
            pltpu.SemaphoreType.DMA((7,)),
        ],
        compiler_params=pltpu.CompilerParams(
            collective_id=1, has_side_effects=True, vmem_limit_bytes=62 * 1024 * 1024
        ),
        name="front",
    )(inputs, conv_weight, mix_weight, gain, bias, cot, out_weight)
    return [conv_full.reshape(2, -1, wide // 2)] + rest


LOW = VD
WIDE = VD + KD


def spots():
    seq = lax.axis_index("seq")
    core = lax.rem(seq, 2)
    z = seq // 16
    mine = (z // 2) * 8 + lax.rem(seq // 2, 8)
    return seq, core, lax.rem(z + z // 2, 2), mine


def pair_ahead(mine, step):
    return lax.rem(mine // 4 + step // 4, 4) * 4 + lax.rem(lax.rem(mine, 4) + step % 4, 4)


def pair_behind(mine, step):
    return lax.rem(mine // 4 + 4 - step // 4, 4) * 4 + lax.rem(lax.rem(mine, 4) + 4 - step % 4, 4)


def holder(pair, z_low, core):
    upper = pair // 8
    z = upper * 2 + lax.rem(z_low + upper, 2)
    return {"seq": z * 16 + lax.rem(pair, 8) * 2 + core}


def attention_peers(seq, core, z_low, mine):
    z_peer = holder(mine, 1 - z_low, core)
    sibling = {"seq": seq + 1 - 2 * core}
    return z_peer, sibling


def greet_attention(barrier):
    seq, core, z_low, mine = spots()
    peers = [holder(pair_ahead(mine, step), z_low, core) for step in range(1, 16)]
    peers += attention_peers(seq, core, z_low, mine)
    for peer in peers:
        pl.semaphore_signal(barrier, inc=1, device_id=peer, device_id_type=MESH)
    return len(peers)


def spread_heads(q_ref, k_ref, v_ref, g_ref, x_out, y_out, x_part, y_part, sems, meanwhile):
    seq, core, z_low, mine = spots()
    z_peer, sibling = attention_peers(seq, core, z_low, mine)
    for window in range(2):
        rows = slice(window * 64, window * 64 + 64)
        for head in range(H):
            pair = window * H + head
            y_part[pair, :, 0:LOW] = v_ref[rows, head * VD : head * VD + VD]
            y_part[pair, :, LOW:WIDE] = k_ref[rows, head * KD : head * KD + KD]

    def send(source, target, peer, slot):
        return remote(source, target, peer, sems, slot)

    y_sends = []
    for step in range(1, 16):
        pair = pair_ahead(mine, step)
        peer = holder(pair, z_low, core)
        y_sends.append(send(y_part.at[pair], y_out.at[z_low, core, mine], peer, step))
    for window in range(2):
        rows = slice(window * 64, window * 64 + 64)
        for head in range(H):
            pair = window * H + head
            x_part[pair, :, 0:LOW] = g_ref[rows, head * VD : head * VD + VD]
            x_part[pair, :, LOW:WIDE] = q_ref[rows, head * KD : head * KD + KD]
    x_sends = []
    for step in range(1, 16):
        pair = pair_ahead(mine, step)
        peer = holder(pair, z_low, core)
        x_sends.append(send(x_part.at[pair], x_out.at[mine], peer, 16 + step))
    y_out[z_low, core, mine] = y_part[mine]
    x_out[mine] = x_part[mine]
    along = []
    across = []
    for step in range(16):
        if step > 0:
            y_sends[step - 1].wait_recv()
        place = y_out.at[z_low, core, pair_behind(mine, step)]
        along.append(send(place, place, z_peer, 32 + step))
        across.append(send(place, place, sibling, 48 + step))
    meanwhile()
    for step in range(16):
        along[step].wait_recv()
        place = y_out.at[1 - z_low, core, pair_behind(mine, step)]
        across.append(send(place, place, sibling, 64 + step))
    for copy in x_sends + across:
        copy.wait_recv()
    for copy in y_sends + x_sends + along + across:
        copy.wait_send()


def collect_heads(
    oq_ref, vk_ref, a_ref, gq_ref, gv_ref, gk_ref, oq_got, vk_got, from_core, to_z, from_z, total, sems,
    meanwhile
):
    seq, core, z_low, mine = spots()
    z_peer, sibling = attention_peers(seq, core, z_low, mine)

    def send(source, target, peer, slot):
        return remote(source, target, peer, sems, 80 + slot)

    groups = [pl.ds(lax.rem(mine // 4 + k, 4) * 4, 4) for k in range(4)]
    across = []
    for far in range(2):
        z_part = 1 - z_low if far == 0 else z_low
        for k in range(4):
            across.append(
                send(
                    vk_ref.at[z_part, 1 - core, groups[k]],
                    from_core.at[far, groups[k]],
                    sibling,
                    4 * far + k,
                )
            )
    oq_sends = []
    for step in range(1, 16):
        pair = pair_ahead(mine, step)
        oq_sends.append(
            send(oq_ref.at[pair], oq_got.at[mine], holder(pair, z_low, core), 16 + step)
        )
    oq_got[mine] = oq_ref[mine]
    along = []
    for k in range(4):
        across[k].wait_recv()
        summed = vk_ref[1 - z_low, core, groups[k]].astype(jnp.float32) + from_core[
            0, groups[k]
        ].astype(jnp.float32)
        to_z[groups[k]] = summed.astype(to_z.dtype)
        along.append(send(to_z.at[groups[k]], from_z.at[groups[k]], z_peer, 8 + k))
    vk_sends = []
    for k in range(4):
        across[4 + k].wait_recv()
        along[k].wait_recv()
        summed = vk_ref[z_low, core, groups[k]].astype(jnp.float32) + from_core[
            1, groups[k]
        ].astype(jnp.float32)
        summed = summed + from_z[groups[k]].astype(jnp.float32)
        total[groups[k]] = summed.astype(total.dtype)
        for step in range(4 * k, 4 * k + 4):
            if step > 0:
                pair = pair_ahead(mine, step)
                vk_sends.append(
                    send(total.at[pair], vk_got.at[mine], holder(pair, z_low, core), 32 + step)
                )
    vk_got[mine] = total[mine]
    for copy in oq_sends:
        copy.wait_recv()
    for window in range(2):
        rows = slice(window * 64, window * 64 + 64)
        for head in range(H):
            pair = window * H + head
            a_ref[rows, head * VD : head * VD + VD] = oq_got[pair, :, 0:LOW]
            gq_ref[rows, head * KD : head * KD + KD] = oq_got[pair, :, LOW:WIDE]
    meanwhile()
    for copy in vk_sends:
        copy.wait_recv()
    for window in range(2):
        rows = slice(window * 64, window * 64 + 64)
        for head in range(H):
            pair = window * H + head
            gv_ref[rows, head * VD : head * VD + VD] = vk_got[pair, :, 0:LOW]
            gk_ref[rows, head * KD : head * KD + KD] = vk_got[pair, :, LOW:WIDE]
    for copy in across + oq_sends + along + vk_sends:
        copy.wait_send()


def attend_rows(x_ref, y_ref, oq_ref, vk_ref, y_turned, score, slope, total):
    keys = y_turned.shape[1]
    chunks = [slice(start, start + CHUNK) for start in range(0, keys, CHUNK)]

    def key_rows(part):
        quarter, first = part.start // 1024, part.start % 1024 // 64
        return y_ref[quarter // 2, quarter % 2, first : first + CHUNK // 64].reshape(CHUNK, WIDE)

    key_scale = KD ** (-0.5)
    for part in chunks:
        y_turned[:, part] = key_rows(part).T
    total[...] = jnp.zeros_like(total)

    def block(index, carry):
        rows = pl.ds(index * 4, 4)
        x_block = x_ref[rows].reshape(QUERY_BLOCK, WIDE)
        wide = x_block.astype(jnp.float32)
        low = lax.broadcasted_iota(jnp.int32, wide.shape, 1) < LOW
        query = jnp.where(low, 0.0, wide).astype(x_block.dtype)
        grad = jnp.where(low, wide, 0.0).astype(x_block.dtype)
        peak = None
        for part in chunks:
            scores = lax.dot_general(key_rows(part), query, SIDE, preferred_element_type=jnp.float32)
            score[part, :] = scores
            top = jnp.max(scores, axis=0, keepdims=True)
            peak = top if peak is None else jnp.maximum(peak, top)
        weight = jnp.zeros((1, QUERY_BLOCK), jnp.float32)
        center = jnp.zeros((1, QUERY_BLOCK), jnp.float32)
        for part in chunks:
            grads = lax.dot_general(key_rows(part), grad, SIDE, preferred_element_type=jnp.float32)
            slope[part, :] = grads
            terms = jnp.exp2((score[part, :] - peak) * (key_scale * 1.4426950408889634))
            score[part, :] = terms
            weight = weight + jnp.sum(terms, axis=0, keepdims=True)
            center = center + jnp.sum(terms * grads, axis=0, keepdims=True)
        share = 1.0 / weight
        center = center * share
        out = jnp.zeros((WIDE, QUERY_BLOCK), jnp.float32)
        back = jnp.zeros((WIDE, QUERY_BLOCK), jnp.float32)
        low_keys = lax.broadcasted_iota(jnp.int32, (CHUNK, WIDE), 1) < LOW
        for part in chunks:
            probs = score[part, :] * share
            prob_low = probs.astype(jnp.bfloat16)
            grads = (probs * (slope[part, :] - center)).astype(jnp.bfloat16)
            out = out + jnp.dot(y_turned[:, part], prob_low, preferred_element_type=jnp.float32)
            back = back + jnp.dot(y_turned[:, part], grads, preferred_element_type=jnp.float32)
            for_values = jnp.dot(prob_low, x_block, preferred_element_type=jnp.float32)
            for_keys = jnp.dot(grads, x_block, preferred_element_type=jnp.float32)
            total[part, :] += jnp.where(low_keys, for_values, for_keys)
        low_rows = lax.broadcasted_iota(jnp.int32, out.shape, 0) < LOW
        turned = jnp.where(low_rows, out, back * key_scale).T
        oq_ref[rows] = turned.reshape(4, 64, WIDE).astype(oq_ref.dtype)
        return carry

    lax.fori_loop(0, x_ref.shape[0] // 4, block, 0)
    low_keys = lax.broadcasted_iota(jnp.int32, (CHUNK, WIDE), 1) < LOW
    for part in chunks:
        quarter, first = part.start // 1024, part.start % 1024 // 64
        grads = total[part, :]
        grads = jnp.where(low_keys, grads, grads * key_scale).astype(vk_ref.dtype)
        pieces = slice(first, first + CHUNK // 64)
        vk_ref[quarter // 2, quarter % 2, pieces] = grads.reshape(CHUNK // 64, 64, WIDE)


def back_kernel(
    x_ref, hidden_ref, stats_one_ref, stats_two_ref, gain_two_ref, bias_two_ref, norm_ref,
    gain_ref, bias_ref, g_ref, cot_ref, mix_from, q_from, k_from, v_from, o_from, conv_from,
    encoded_out, out_ref, sums_two_out, sums_one_out,
    mix, q_weight, k_weight, v_weight, o_weight, weight,
    hat_two, slope_two, trunk, row_hat, mixed, hat_one, slope_one, q_rows, k_rows, v_rows,
    a_rows, gq_rows, gv_rows, gk_rows,
    x_part, y_part, x_got, y_got, y_turned, score, slope, total_vk, oq, vk,
    oq_got, vk_got, from_core, to_z, from_z, summed,
    line_two, plane_two, line_one, plane_one, middle, padded, low, high,
    head_send, head_recv, sum_send, sum_recv, move_send, move_recv, own_sem
):
    heads = (head_send, head_recv)
    sums = (sum_send, sum_recv)
    moves = (move_send, move_recv)
    total_rows = ROWS * lax.axis_size("seq") * lax.axis_size("batch")
    kind = x_ref.dtype
    full = jnp.float32
    barrier, count = greet_all()
    count += greet_attention(barrier)
    loads = [
        pltpu.make_async_copy(source, target, own_sem.at[i])
        for i, (source, target) in enumerate(
            (
                (mix_from, mix),
                (q_from, q_weight),
                (k_from, k_weight),
                (v_from, v_weight),
                (o_from, o_weight),
                (conv_from, weight),
            )
        )
    ]
    for load in loads[:4]:
        load.start()
    mean_two = stats_two_ref[0:1, :] / total_rows
    scale_two = lax.rsqrt(stats_two_ref[1:2, :] / total_rows - mean_two * mean_two + EPS)
    hat = (hidden_ref[...] - mean_two) * scale_two
    pre = hat * gain_two_ref[...][None, :] + bias_two_ref[...][None, :]
    hat_two[...] = hat
    loads[0].wait()
    trunk[...] = (
        x_ref[...].astype(full)
        + jnp.dot(gelu_value(pre).astype(kind), mix[...], preferred_element_type=full)
    ).astype(kind)
    rows = trunk[...].astype(full)
    centered = rows - jnp.mean(rows, axis=-1, keepdims=True)
    row_scale = lax.rsqrt(jnp.mean(centered * centered, axis=-1, keepdims=True) + EPS)
    row_hat[...] = centered * row_scale
    norm_gain = norm_ref[...][None, :]
    normed = (row_hat[...] * norm_gain).astype(kind)
    for load, table, place in (
        (loads[3], v_weight, v_rows),
        (loads[2], k_weight, k_rows),
        (loads[1], q_weight, q_rows),
    ):
        load.wait()
        place[...] = jnp.dot(normed, table[...], preferred_element_type=full).astype(kind)
    pl.semaphore_wait(barrier, count)

    mean, scale = stats_one_ref[0:1, :], stats_one_ref[1:2, :]
    gain_one = gain_ref[...][None, :]

    def recall():
        for load in loads[4:]:
            load.start()
        slope_two[...] = gelu_slope(hat_two[...] * gain_two_ref[...][None, :] + bias_two_ref[...][None, :])
        hat_one[...] = (x_ref[...].astype(full) - mean) * scale
        slope_one[...] = gelu_slope(hat_one[...] * gain_one + bias_ref[...][None, :])

    def encode():
        loads[4].wait()
        encoded_out[...] = (
            trunk[...].astype(full) + jnp.dot(a_rows[...], o_weight[...], preferred_element_type=full)
        ).astype(kind)
        mixed[...] = lax.dot_general(gq_rows[...], q_weight[...], SIDE, preferred_element_type=full)

    spread_heads(q_rows, k_rows, v_rows, g_ref, x_got, y_got, x_part, y_part, heads, recall)
    attend_rows(x_got, y_got, oq, vk, y_turned, score, slope, total_vk)
    collect_heads(
        oq, vk, a_rows, gq_rows, gv_rows, gk_rows, oq_got, vk_got, from_core, to_z, from_z, summed,
        heads, encode
    )
    grad_normed = (
        mixed[...]
        + lax.dot_general(gk_rows[...], k_weight[...], SIDE, preferred_element_type=full)
        + lax.dot_general(gv_rows[...], v_weight[...], SIDE, preferred_element_type=full)
    )
    hats = row_hat[...]
    norm_part = jnp.sum(grad_normed * hats, axis=0, keepdims=True)
    grad_hat = grad_normed * norm_gain
    mixed[...] = cot_ref[...].astype(full) + row_scale * (
        grad_hat
        - jnp.mean(grad_hat, axis=-1, keepdims=True)
        - hats * jnp.mean(grad_hat * hats, axis=-1, keepdims=True)
    )
    grad_two = (
        lax.dot_general(mixed[...].astype(kind), mix[...], SIDE, preferred_element_type=full)
        * slope_two[...]
    )
    mid_width = grad_two.shape[1]
    place = line_place()
    line_two[place] = jnp.concatenate(
        [
            jnp.sum(grad_two, axis=0, keepdims=True),
            jnp.sum(grad_two * hat_two[...], axis=0, keepdims=True),
            norm_part[:, :mid_width],
            norm_part[:, mid_width:],
        ],
        axis=0,
    )
    started = line_send(line_two, sums, 0)
    plane_started = plane_send(line_two, plane_two, started, sums, 0)
    total = plane_sum(plane_two, plane_started)
    sums_two_out[...] = total
    hidden_grad = (
        gain_two_ref[...][None, :]
        * scale_two
        * (grad_two - total[0:1, :] / total_rows - hat_two[...] * total[1:2, :] / total_rows)
    ).astype(kind)
    for window in range(2):
        middle[window] = hidden_grad[window * 64 : window * 64 + 64, :]
        padded[window, 16:80, :] = hidden_grad[window * 64 : window * 64 + 64, :]
    halos = halo_send(middle, low, high, moves, 0)
    loads[5].wait()
    grad_act = None
    for tap, half, start, size in (TAP_PARTS[1], TAP_PARTS[2], TAP_PARTS[0], TAP_PARTS[3]):
        if tap == 0:
            halo_fill(padded, low, high, halos)
        first = 0 if half == 0 or tap == 2 else 384
        term = lax.dot_general(
            tap_rows(padded, 16 * (2 - tap))[:, first : first + size],
            weight[half, :, start : start + size],
            SIDE,
            preferred_element_type=jnp.float32,
        )
        grad_act = term if grad_act is None else grad_act + term
    grad_pre = grad_act * slope_one[...]
    line_one[place] = stacked([grad_pre, grad_pre * hat_one[...]])
    line_again = line_send(line_one, sums, LINE + PLANE)
    plane_again = plane_send(line_one, plane_one, line_again, sums, LINE + PLANE)
    total = plane_sum(plane_one, plane_again)
    sums_one_out[...] = total
    grad_rows = (
        gain_one
        * scale
        * (grad_pre - total[0:1, :] / total_rows - hat_one[...] * total[1:2, :] / total_rows)
    )
    out_ref[...] = (mixed[...] + grad_rows).astype(out_ref.dtype)
    for copy in started + plane_started + halos + line_again + plane_again:
        copy.wait_send()


def back(
    rows_in, hidden, stats_one, stats_two, gain_two, bias_two, norm_gain, gain_one, bias_one,
    grad_out, cot, mix_full, query_weight, key_weight, value_weight, out_weight, conv_full
):
    vmem = pl.BlockSpec(memory_space=pltpu.VMEM)
    anywhere = pl.BlockSpec(memory_space=pl.ANY)
    kind, full = rows_in.dtype, jnp.float32
    width, mid_width = rows_in.shape[1], hidden.shape[1]
    piece = (16, 64, WIDE)
    count = 4 * 16 * 64
    sems = 2 * (LINE + PLANE)
    weights = (mix_full, query_weight, key_weight, value_weight, out_weight, conv_full)
    scratch = [(table.shape, kind) for table in weights]
    scratch += [((ROWS, mid_width), full)] * 2 + [((ROWS, width), kind)] + [((ROWS, width), full)] * 4
    scratch += [((ROWS, H * KD), kind)] * 2 + [((ROWS, H * VD), kind)] * 2
    scratch += [((ROWS, H * KD), kind), ((ROWS, H * VD), kind), ((ROWS, H * KD), kind)]
    scratch += [(piece, kind)] * 3 + [((2, 2) + piece, kind), ((WIDE, count), kind)]
    scratch += [((count, QUERY_BLOCK), full)] * 2 + [((count, WIDE), full)]
    scratch += [(piece, kind), ((2, 2) + piece, kind), (piece, kind), (piece, kind)]
    scratch += [((2,) + piece, kind)] + [(piece, kind)] * 3
    scratch += [((LINE, 4, mid_width), full), ((PLANE, 4, mid_width), full)]
    scratch += [((LINE, 2, width), full), ((PLANE, 2, width), full)]
    scratch += [((2, 64, mid_width), kind), ((2, 96, mid_width), kind)] + [((2, 16, mid_width), kind)] * 2
    dma = pltpu.SemaphoreType.DMA
    return pl.pallas_call(
        back_kernel,
        out_shape=[
            jax.ShapeDtypeStruct((ROWS, width), kind),
            jax.ShapeDtypeStruct((ROWS, width), kind),
            jax.ShapeDtypeStruct((4, mid_width), full),
            jax.ShapeDtypeStruct((2, width), full),
        ],
        in_specs=[vmem] * 11 + [anywhere] * 6,
        out_specs=[vmem] * 4,
        scratch_shapes=[pltpu.VMEM(shape, held) for shape, held in scratch]
        + [dma((128,)), dma((128,)), dma((sems,)), dma((sems,)), dma((1, 2)), dma((1, 2)), dma((6,))],
        compiler_params=pltpu.CompilerParams(
            collective_id=2, has_side_effects=True, vmem_limit_bytes=62 * 1024 * 1024
        ),
        name="back",
    )(
        rows_in, hidden, stats_one, stats_two, gain_two, bias_two, norm_gain, gain_one, bias_one,
        grad_out, cot, *weights
    )


def finish_kernel(
    encoded_from, grad_from, two_ref, one_ref,
    encoded_to, grad_to, gain_one, bias_one, gain_two, bias_two, gain_norm
):
    encoded_to[...] = encoded_from[...]
    grad_to[...] = grad_from[...]
    mid_width = two_ref.shape[1]
    bias_one[...] = one_ref[0, :]
    gain_one[...] = one_ref[1, :]
    bias_two[...] = two_ref[0, :]
    gain_two[...] = two_ref[1, :]
    gain_norm[0:mid_width] = two_ref[2, :]
    gain_norm[mid_width : 2 * mid_width] = two_ref[3, :]


def finish(encoded, grad_inputs, sums_two, sums_one):
    vmem = pl.BlockSpec(memory_space=pltpu.VMEM)
    width, mid_width = sums_one.shape[1], sums_two.shape[1]
    full = jnp.float32
    return pl.pallas_call(
        finish_kernel,
        out_shape=[
            jax.ShapeDtypeStruct(encoded.shape, encoded.dtype),
            jax.ShapeDtypeStruct(grad_inputs.shape, grad_inputs.dtype),
            jax.ShapeDtypeStruct((width,), full),
            jax.ShapeDtypeStruct((width,), full),
            jax.ShapeDtypeStruct((mid_width,), full),
            jax.ShapeDtypeStruct((mid_width,), full),
            jax.ShapeDtypeStruct((2 * mid_width,), full),
        ],
        in_specs=[vmem] * 4,
        out_specs=[vmem] * 7,
        compiler_params=pltpu.CompilerParams(vmem_limit_bytes=62 * 1024 * 1024),
        name="finish",
    )(encoded, grad_inputs, sums_two, sums_one)


def on_device(
    inputs,
    conv_weight,
    mix_weight,
    first_gain,
    first_bias,
    second_gain,
    second_bias,
    norm_gain,
    query_weight,
    key_weight,
    value_weight,
    out_weight,
    cotangent,
):
    windows_here, local_bins, model_width = inputs.shape
    local_count = windows_here * local_bins
    rows_in = inputs.reshape(local_count, model_width)
    cot_flat = cotangent.reshape(local_count, model_width)
    conv_full, mix_full, hidden, stats_one, stats_two, grad_out = front(
        rows_in, conv_weight, mix_weight, first_gain, first_bias, cot_flat, out_weight
    )
    encoded_rows, grad_rows, sums_two, sums_one = back(
        rows_in,
        hidden,
        stats_one,
        stats_two,
        second_gain,
        second_bias,
        norm_gain,
        first_gain,
        first_bias,
        grad_out,
        cot_flat,
        mix_full,
        query_weight,
        key_weight,
        value_weight,
        out_weight,
        conv_full,
    )
    whole = (windows_here, local_bins, model_width)
    return finish(encoded_rows.reshape(whole), grad_rows.reshape(whole), sums_two, sums_one)


def solution(mesh):
    in_specs = (
        P("batch", "seq", None),
        P("seq", None),
        P("seq", None),
        P(),
        P(),
        P(),
        P(),
        P(),
        P(),
        P(),
        P(),
        P(),
        P("batch", "seq", None),
    )
    out_specs = (P("batch", "seq", None), P("batch", "seq", None), P(), P(), P(), P(), P())
    return jax.shard_map(
        on_device, mesh=mesh, in_specs=in_specs, out_specs=out_specs, check_vma=False
    )
```

```python
import jax
import jax.numpy as jnp
from jax import lax
from jax.experimental import pallas as pl
from jax.experimental.pallas import tpu as pltpu
from jax.sharding import PartitionSpec as P

H = 8
KD = 64
VD = 192
DILATION_STEP = 16


EPS = 1e-05
GELU_C = 0.7978845608028654


MESH = pl.DeviceIdType.MESH
ROWS = 128
LINE = 8
PLANE = 16
TAP_PARTS = ((0, 0, 0, 768), (1, 0, 768, 384), (1, 1, 0, 384), (2, 1, 384, 768))


def seq_of(z, y, x, core):
    return ((z * 4 + y) * 2 + x) * 2 + core


def remote(source, target, peer, sems, slot):
    copy = pltpu.make_async_remote_copy(
        src_ref=source,
        dst_ref=target,
        send_sem=sems[0].at[slot],
        recv_sem=sems[1].at[slot],
        device_id=peer,
        device_id_type=MESH,
    )
    copy.start()
    return copy


def line_place():
    return lax.axis_index("batch") * 4 + lax.rem(lax.axis_index("seq"), 4)


def line_peer(step):
    other = lax.rem(line_place() + step, LINE)
    spot = lax.axis_index("seq") // 4
    return {"seq": spot * 4 + lax.rem(other, 4), "batch": other // 4}


def plane_peer(step):
    seq = lax.axis_index("seq")
    return {"seq": lax.rem(seq // 4 + step, PLANE) * 4 + lax.rem(seq, 4)}


def ring_peer(step):
    count = 4 * PLANE
    return {"seq": lax.rem(lax.axis_index("seq") + step + count, count)}


def greet_all():
    barrier = pltpu.get_barrier_semaphore()
    peers = [line_peer(step) for step in range(1, LINE)]
    peers += [plane_peer(step) for step in range(1, PLANE)]
    peers += [ring_peer(1), ring_peer(-1)]
    for peer in peers:
        pl.semaphore_signal(barrier, inc=1, device_id=peer, device_id_type=MESH)
    return barrier, len(peers)


def line_send(line, sems, base):
    place = line.at[line_place()]
    return [remote(place, place, line_peer(step), sems, base + step) for step in range(1, LINE)]


def plane_send(line, plane, arrivals, sems, base):
    for copy in arrivals:
        copy.wait_recv()
    total = line[0]
    for i in range(1, LINE):
        total = total + line[i]
    spot = lax.axis_index("seq") // 4
    plane[spot] = total
    place = plane.at[spot]
    return [
        remote(place, place, plane_peer(step), sems, base + LINE + step) for step in range(1, PLANE)
    ]


def plane_sum(plane, arrivals):
    for copy in arrivals:
        copy.wait_recv()
    total = plane[0]
    for i in range(1, PLANE):
        total = total + plane[i]
    return total


def halo_send(middle, low, high, sems, base):
    return [
        remote(middle.at[:, 48:64, :], low, ring_peer(1), sems, (base, 0)),
        remote(middle.at[:, 0:16, :], high, ring_peer(-1), sems, (base, 1)),
    ]


def halo_fill(padded, low, high, copies):
    seq = lax.axis_index("seq")
    last = lax.axis_size("seq") - 1
    for copy in copies:
        copy.wait_recv()
    low_rows = low[...].astype(jnp.float32)
    high_rows = high[...].astype(jnp.float32)
    padded[:, 0:16, :] = jnp.where(seq == 0, 0.0, low_rows).astype(padded.dtype)
    padded[:, 80:96, :] = jnp.where(seq == last, 0.0, high_rows).astype(padded.dtype)


def tap_rows(padded, start):
    return jnp.concatenate([padded[0, start : start + 64, :], padded[1, start : start + 64, :]], axis=0)


def stacked(rows):
    return jnp.concatenate([jnp.sum(part, axis=0, keepdims=True) for part in rows], axis=0)


def gelu_value(values):
    cubic = GELU_C * (values + 0.044715 * values * values * values)
    return 0.5 * values * (1.0 + jnp.tanh(cubic))


def gelu_slope(values):
    tangent = jnp.tanh(GELU_C * (values + 0.044715 * values * values * values))
    return 0.5 * (1.0 + tangent) + 0.5 * values * (1.0 - tangent * tangent) * GELU_C * (
        1.0 + 3.0 * 0.044715 * values * values
    )


def rounded(values):
    return lax.optimization_barrier(values.astype(jnp.bfloat16)).astype(jnp.float32)


CHUNK = 256
QUERY_BLOCK = 256
SIDE = (((1,), (1,)), ((), ()))
def front_kernel(
    x_from, conv_from, mix_from, gain_ref, bias_ref, cot_from, out_weight_ref,
    conv_to, mix_to, hidden_out, stats_one_out, stats_two_out, grad_out,
    conv_out, mix_out, line_one, plane_one, line_two, plane_two, conv_other, mix_other, mix_land, middle, padded,
    low, high, weight, x_ref, conv_ref, mix_ref, cot_ref, sum_send, sum_recv, move_send, move_recv, own_sem
):
    seq = lax.axis_index("seq")
    core = lax.rem(seq, 2)
    x = lax.rem(seq // 2, 2)
    y = lax.rem(seq // 4, 4)
    z = seq // 16
    sums = (sum_send, sum_recv)
    moves = (move_send, move_recv)
    total_rows = ROWS * lax.axis_size("seq") * lax.axis_size("batch")
    barrier, count = greet_all()
    loads = [
        pltpu.make_async_copy(source, target, own_sem.at[i])
        for i, (source, target) in enumerate(
            (
                (x_from, x_ref),
                (conv_from, conv_ref),
                (mix_from, mix_ref),
                (cot_from, cot_ref),
                (out_weight_ref, weight),
            )
        )
    ]
    for load in loads:
        load.start()
    loads[0].wait()
    values = x_ref[...].astype(jnp.float32)
    line_one[line_place()] = stacked([values, values * values])
    pl.semaphore_wait(barrier, count)

    def first_peer(step):
        return {"seq": seq_of(lax.rem(z + step * x, 4), lax.rem(y + step * (1 - x), 4), x, core)}

    def second_peer(step):
        return {"seq": seq_of(lax.rem(z + step * (1 - x), 4), lax.rem(y + step * x, 4), x, core)}

    def y_peer(step):
        return {"seq": seq_of(z, lax.rem(y + step, 4), x, core)}

    def z_peer(step):
        return {"seq": seq_of(lax.rem(z + step, 4), y, x, core)}

    x_peer = {"seq": seq_of(z, y, 1 - x, core)}
    sibling = {"seq": seq_of(z, y, x, 1 - core)}
    outs = (conv_out, mix_land)
    widths = (conv_ref.shape[1] // 2, mix_ref.shape[1] // 2)
    halves = [pl.ds(pl.multiple_of(core * w, w), w) for w in widths]
    far_halves = [pl.ds(pl.multiple_of((1 - core) * w, w), w) for w in widths]

    def move(kind, where, peer, slot):
        place = outs[kind].at[(core, *where)]
        return remote(place, place, peer, moves, (slot, kind))

    started = line_send(line_one, sums, 0)
    line_started = started
    pair_up = [
        remote(conv_from.at[:, far_halves[0]], conv_other, sibling, moves, (0, 0)),
        remote(mix_from.at[:, far_halves[1]], mix_other, sibling, moves, (0, 1)),
    ]
    started = started + pair_up
    for kind, mine, other in ((0, conv_ref, conv_other), (1, mix_ref, mix_other)):
        loads[1 + kind].wait()
        pair_up[kind].wait_recv()
        out = outs[kind]
        here = mine[:, halves[kind]].astype(jnp.float32)
        there = other[...].astype(jnp.float32)
        upper = jnp.where(core == 0, here, there)
        lower = jnp.where(core == 0, there, here)
        out[core, z, y, x] = jnp.concatenate([upper, lower], axis=0).astype(out.dtype)
    to_x = [move(kind, (z, y, x), x_peer, 1) for kind in range(2)]
    spread_out = []
    for kind in range(2):
        for step in (1, 3):
            spread_out.append(move(kind, (z, y, x), first_peer(step), 1 + step))
    plane_started = plane_send(line_one, plane_one, line_started, sums, 0)
    for copy in to_x:
        copy.wait_recv()
    for kind in range(2):
        for step in (1, 3):
            spread_out.append(move(kind, (z, y, 1 - x), second_peer(step), 4 + step))
    first_block, second_block = spread_out[:4], spread_out[4:]
    for kind, step, back in ((0, 1, 3), (1, 3, 1)):
        first_block[2 * kind + step // 2].wait_recv()
        place = (lax.rem(z + back * x, 4), lax.rem(y + back * (1 - x), 4), x)
        spread_out.append(move(kind, place, first_peer(step), 3))
    total = plane_sum(plane_one, plane_started)
    mean = total[0:1, :] / total_rows
    scale = lax.rsqrt(total[1:2, :] / total_rows - mean * mean + EPS)
    stats_one_out[...] = jnp.concatenate([mean, scale], axis=0)
    pre = (values - mean) * scale * gain_ref[...][None, :] + bias_ref[...][None, :]
    active = gelu_value(pre).astype(middle.dtype)
    for window in range(2):
        middle[window] = active[window * 64 : window * 64 + 64, :]
        padded[window, 16:80, :] = active[window * 64 : window * 64 + 64, :]
    halos = halo_send(middle, low, high, moves, 19)
    for kind, step, back in ((0, 1, 3), (1, 3, 1)):
        second_block[2 * kind + step // 2].wait_recv()
        place = (lax.rem(z + back * (1 - x), 4), lax.rem(y + back * x, 4), 1 - x)
        spread_out.append(move(kind, place, second_peer(step), 6))
    waited = (first_block[0], first_block[3], second_block[0], second_block[3])
    for copy in spread_out:
        if all(copy is not other for other in waited):
            copy.wait_recv()
    whole = slice(None)
    blocks = [[], []]
    across = [[], []]

    def launch(kind):
        for step in (1, 3):
            blocks[kind].append(move(kind, (z, whole, 0), z_peer(step), 7 + step))
            blocks[kind].append(move(kind, (whole, y, 1), y_peer(step), 10 + step))
        across[kind].append(move(kind, (z, whole, 0), sibling, 14))
        across[kind].append(move(kind, (whole, y, 1), sibling, 15))

    def relay(kind):
        for i, (step, part) in enumerate(((1, slice(0, 2)), (3, slice(2, 4)))):
            from_z, from_y = lax.rem(z + 4 - step, 4), lax.rem(y + 4 - step, 4)
            blocks[kind][2 * i].wait_recv()
            blocks[kind].append(move(kind, (from_z, part, 0), z_peer(step), 9 if i == 0 else 24))
            blocks[kind][2 * i + 1].wait_recv()
            blocks[kind].append(move(kind, (part, from_y, 1), y_peer(step), 12 if i == 0 else 25))
            across[kind].append(move(kind, (from_z, whole, 0), sibling, 15 + step))
            across[kind].append(move(kind, (whole, from_y, 1), sibling, 20 + step))

    def finish(kind):
        blocks[kind][4].wait_recv()
        blocks[kind][6].wait_recv()
        across[kind].append(move(kind, (lax.rem(z + 2, 4), whole, 0), sibling, 17))
        blocks[kind][5].wait_recv()
        blocks[kind][7].wait_recv()
        across[kind].append(move(kind, (whole, lax.rem(y + 2, 4), 1), sibling, 22))

    launch(0)
    loads[3].wait()
    loads[4].wait()
    grad_out[...] = lax.dot_general(
        cot_ref[...], weight[...], SIDE, preferred_element_type=jnp.float32
    ).astype(grad_out.dtype)
    halo_fill(padded, low, high, halos)

    relay(0)
    launch(1)
    finish(0)
    for copy in across[0]:
        copy.wait_recv()
    stores = [pltpu.make_async_copy(conv_out, conv_to, own_sem.at[5])]
    stores[0].start()
    terms = {}
    for tap, half, start, size in TAP_PARTS:
        part = conv_out[half, :, :, :, :, start : start + size].reshape(-1, size)
        terms[tap, half] = jnp.dot(tap_rows(padded, 16 * tap), part, preferred_element_type=jnp.float32)
    middle_tap = jnp.concatenate([terms[1, 0], terms[1, 1]], axis=1)
    hidden = terms[0, 0] + middle_tap + terms[2, 1]
    hidden_out[...] = hidden
    line_two[line_place()] = stacked([hidden, hidden * hidden])
    line_again = line_send(line_two, sums, LINE + PLANE)
    relay(1)
    plane_again = plane_send(line_two, plane_two, line_again, sums, LINE + PLANE)
    finish(1)
    for copy in across[1]:
        copy.wait_recv()
    for i in range(4):
        for j in range(4):
            start = (i * 4 + j) * 48
            for half in range(2):
                pair = [mix_land[half, i, j, k].astype(jnp.float32) for k in range(2)]
                columns = slice(half * widths[1], half * widths[1] + widths[1])
                mix_out[start : start + 48, columns] = jnp.concatenate(pair, axis=0).astype(mix_out.dtype)
    stores.append(pltpu.make_async_copy(mix_out, mix_to, own_sem.at[6]))
    stores[1].start()
    stats_two_out[...] = plane_sum(plane_two, plane_again)
    ended = started + to_x + spread_out + halos + plane_started + line_again + plane_again
    for kind in range(2):
        ended += blocks[kind] + across[kind]
    for copy in ended:
        copy.wait_send()
    for copy in stores:
        copy.wait()


def front(inputs, conv_weight, mix_weight, gain, bias, cot, out_weight):
    vmem = pl.BlockSpec(memory_space=pltpu.VMEM)
    anywhere = pl.BlockSpec(memory_space=pl.ANY)
    width = inputs.shape[1]
    mid_width = conv_weight.shape[1] // 3
    kind = inputs.dtype
    conv_rows, mix_rows = conv_weight.shape[0], mix_weight.shape[0]
    full, wide = jnp.float32, conv_weight.shape[1]
    sems = 2 * (LINE + PLANE)
    conv_full, *rest = pl.pallas_call(
        front_kernel,
        out_shape=[
            jax.ShapeDtypeStruct((2, 4, 4, 2, 2 * conv_rows, wide // 2), kind),
            jax.ShapeDtypeStruct((64 * mix_rows, width), kind),
            jax.ShapeDtypeStruct((ROWS, mid_width), full),
            jax.ShapeDtypeStruct((2, width), full),
            jax.ShapeDtypeStruct((2, mid_width), full),
            jax.ShapeDtypeStruct((ROWS, out_weight.shape[0]), kind),
        ],
        in_specs=[anywhere] * 3 + [vmem] * 2 + [anywhere] * 2,
        out_specs=[anywhere] * 2 + [vmem] * 4,
        scratch_shapes=[
            pltpu.VMEM((2, 4, 4, 2, 2 * conv_rows, wide // 2), kind),
            pltpu.VMEM((64 * mix_rows, width), kind),
            pltpu.VMEM((LINE, 2, width), full),
            pltpu.VMEM((PLANE, 2, width), full),
            pltpu.VMEM((LINE, 2, mid_width), full),
            pltpu.VMEM((PLANE, 2, mid_width), full),
            pltpu.VMEM((conv_rows, wide // 2), kind),
            pltpu.VMEM((mix_rows, width // 2), kind),
            pltpu.VMEM((2, 4, 4, 2, 2 * mix_rows, width // 2), kind),
            pltpu.VMEM((2, 64, width), kind),
            pltpu.VMEM((2, 96, width), kind),
            pltpu.VMEM((2, 16, width), kind),
            pltpu.VMEM((2, 16, width), kind),
            pltpu.VMEM(out_weight.shape, kind),
            pltpu.VMEM(inputs.shape, kind),
            pltpu.VMEM(conv_weight.shape, kind),
            pltpu.VMEM(mix_weight.shape, kind),
            pltpu.VMEM(cot.shape, kind),
            pltpu.SemaphoreType.DMA((sems,)),
            pltpu.SemaphoreType.DMA((sems,)),
            pltpu.SemaphoreType.DMA((26, 2)),
            pltpu.SemaphoreType.DMA((26, 2)),
            pltpu.SemaphoreType.DMA((7,)),
        ],
        compiler_params=pltpu.CompilerParams(
            collective_id=1, has_side_effects=True, vmem_limit_bytes=62 * 1024 * 1024
        ),
        name="front",
    )(inputs, conv_weight, mix_weight, gain, bias, cot, out_weight)
    return [conv_full.reshape(2, -1, wide // 2)] + rest


LOW = VD
WIDE = VD + KD


def spots():
    seq = lax.axis_index("seq")
    core = lax.rem(seq, 2)
    z = seq // 16
    mine = (z // 2) * 8 + lax.rem(seq // 2, 8)
    return seq, core, lax.rem(z + z // 2, 2), mine


def pair_ahead(mine, step):
    return lax.rem(mine // 4 + step // 4, 4) * 4 + lax.rem(lax.rem(mine, 4) + step % 4, 4)


def pair_behind(mine, step):
    return lax.rem(mine // 4 + 4 - step // 4, 4) * 4 + lax.rem(lax.rem(mine, 4) + 4 - step % 4, 4)


def holder(pair, z_low, core):
    upper = pair // 8
    z = upper * 2 + lax.rem(z_low + upper, 2)
    return {"seq": z * 16 + lax.rem(pair, 8) * 2 + core}


def attention_peers(seq, core, z_low, mine):
    z_peer = holder(mine, 1 - z_low, core)
    sibling = {"seq": seq + 1 - 2 * core}
    return z_peer, sibling


def greet_attention(barrier):
    seq, core, z_low, mine = spots()
    peers = [holder(pair_ahead(mine, step), z_low, core) for step in range(1, 16)]
    peers += attention_peers(seq, core, z_low, mine)
    for peer in peers:
        pl.semaphore_signal(barrier, inc=1, device_id=peer, device_id_type=MESH)
    return len(peers)


def spread_heads(q_ref, k_ref, v_ref, g_ref, x_out, y_out, x_part, y_part, sems, meanwhile):
    seq, core, z_low, mine = spots()
    z_peer, sibling = attention_peers(seq, core, z_low, mine)
    for window in range(2):
        rows = slice(window * 64, window * 64 + 64)
        for head in range(H):
            pair = window * H + head
            y_part[pair, :, 0:LOW] = v_ref[rows, head * VD : head * VD + VD]
            y_part[pair, :, LOW:WIDE] = k_ref[rows, head * KD : head * KD + KD]

    def send(source, target, peer, slot):
        return remote(source, target, peer, sems, slot)

    y_sends = []
    for step in range(1, 16):
        pair = pair_ahead(mine, step)
        peer = holder(pair, z_low, core)
        y_sends.append(send(y_part.at[pair], y_out.at[z_low, core, mine], peer, step))
    for window in range(2):
        rows = slice(window * 64, window * 64 + 64)
        for head in range(H):
            pair = window * H + head
            x_part[pair, :, 0:LOW] = g_ref[rows, head * VD : head * VD + VD]
            x_part[pair, :, LOW:WIDE] = q_ref[rows, head * KD : head * KD + KD]
    x_sends = []
    for step in range(1, 16):
        pair = pair_ahead(mine, step)
        peer = holder(pair, z_low, core)
        x_sends.append(send(x_part.at[pair], x_out.at[mine], peer, 16 + step))
    y_out[z_low, core, mine] = y_part[mine]
    x_out[mine] = x_part[mine]
    along = []
    across = []
    for step in range(16):
        if step > 0:
            y_sends[step - 1].wait_recv()
        place = y_out.at[z_low, core, pair_behind(mine, step)]
        along.append(send(place, place, z_peer, 32 + step))
        across.append(send(place, place, sibling, 48 + step))
    meanwhile()
    for step in range(16):
        along[step].wait_recv()
        place = y_out.at[1 - z_low, core, pair_behind(mine, step)]
        across.append(send(place, place, sibling, 64 + step))
    for copy in x_sends + across:
        copy.wait_recv()
    for copy in y_sends + x_sends + along + across:
        copy.wait_send()


def collect_heads(
    oq_ref, vk_ref, a_ref, gq_ref, gv_ref, gk_ref, oq_got, vk_got, from_core, to_z, from_z, total, sems,
    meanwhile
):
    seq, core, z_low, mine = spots()
    z_peer, sibling = attention_peers(seq, core, z_low, mine)

    def send(source, target, peer, slot):
        return remote(source, target, peer, sems, 80 + slot)

    groups = [pl.ds(lax.rem(mine // 4 + k, 4) * 4, 4) for k in range(4)]
    across = []
    for far in range(2):
        z_part = 1 - z_low if far == 0 else z_low
        for k in range(4):
            across.append(
                send(
                    vk_ref.at[z_part, 1 - core, groups[k]],
                    from_core.at[far, groups[k]],
                    sibling,
                    4 * far + k,
                )
            )
    oq_sends = []
    for step in range(1, 16):
        pair = pair_ahead(mine, step)
        oq_sends.append(
            send(oq_ref.at[pair], oq_got.at[mine], holder(pair, z_low, core), 16 + step)
        )
    oq_got[mine] = oq_ref[mine]
    along = []
    for k in range(4):
        across[k].wait_recv()
        summed = vk_ref[1 - z_low, core, groups[k]].astype(jnp.float32) + from_core[
            0, groups[k]
        ].astype(jnp.float32)
        to_z[groups[k]] = summed.astype(to_z.dtype)
        along.append(send(to_z.at[groups[k]], from_z.at[groups[k]], z_peer, 8 + k))
    vk_sends = []
    for k in range(4):
        across[4 + k].wait_recv()
        along[k].wait_recv()
        summed = vk_ref[z_low, core, groups[k]].astype(jnp.float32) + from_core[
            1, groups[k]
        ].astype(jnp.float32)
        summed = summed + from_z[groups[k]].astype(jnp.float32)
        total[groups[k]] = summed.astype(total.dtype)
        for step in range(4 * k, 4 * k + 4):
            if step > 0:
                pair = pair_ahead(mine, step)
                vk_sends.append(
                    send(total.at[pair], vk_got.at[mine], holder(pair, z_low, core), 32 + step)
                )
    vk_got[mine] = total[mine]
    for copy in oq_sends:
        copy.wait_recv()
    for window in range(2):
        rows = slice(window * 64, window * 64 + 64)
        for head in range(H):
            pair = window * H + head
            a_ref[rows, head * VD : head * VD + VD] = oq_got[pair, :, 0:LOW]
            gq_ref[rows, head * KD : head * KD + KD] = oq_got[pair, :, LOW:WIDE]
    meanwhile()
    for copy in vk_sends:
        copy.wait_recv()
    for window in range(2):
        rows = slice(window * 64, window * 64 + 64)
        for head in range(H):
            pair = window * H + head
            gv_ref[rows, head * VD : head * VD + VD] = vk_got[pair, :, 0:LOW]
            gk_ref[rows, head * KD : head * KD + KD] = vk_got[pair, :, LOW:WIDE]
    for copy in across + oq_sends + along + vk_sends:
        copy.wait_send()


def attend_rows(x_ref, y_ref, oq_ref, vk_ref, y_turned, score, slope, total):
    keys = y_turned.shape[1]
    chunks = [slice(start, start + CHUNK) for start in range(0, keys, CHUNK)]

    def key_rows(part):
        quarter, first = part.start // 1024, part.start % 1024 // 64
        return y_ref[quarter // 2, quarter % 2, first : first + CHUNK // 64].reshape(CHUNK, WIDE)

    key_scale = KD ** (-0.5)
    for part in chunks:
        y_turned[:, part] = key_rows(part).T
    total[...] = jnp.zeros_like(total)

    def block(index, carry):
        rows = pl.ds(index * 4, 4)
        x_block = x_ref[rows].reshape(QUERY_BLOCK, WIDE)
        wide = x_block.astype(jnp.float32)
        low = lax.broadcasted_iota(jnp.int32, wide.shape, 1) < LOW
        query = jnp.where(low, 0.0, wide).astype(x_block.dtype)
        grad = jnp.where(low, wide, 0.0).astype(x_block.dtype)
        peak = None
        for part in chunks:
            scores = lax.dot_general(key_rows(part), query, SIDE, preferred_element_type=jnp.float32)
            score[part, :] = scores
            top = jnp.max(scores, axis=0, keepdims=True)
            peak = top if peak is None else jnp.maximum(peak, top)
        weight = jnp.zeros((1, QUERY_BLOCK), jnp.float32)
        center = jnp.zeros((1, QUERY_BLOCK), jnp.float32)
        for part in chunks:
            grads = lax.dot_general(key_rows(part), grad, SIDE, preferred_element_type=jnp.float32)
            slope[part, :] = grads
            terms = jnp.exp2((score[part, :] - peak) * (key_scale * 1.4426950408889634))
            score[part, :] = terms
            weight = weight + jnp.sum(terms, axis=0, keepdims=True)
            center = center + jnp.sum(terms * grads, axis=0, keepdims=True)
        share = 1.0 / weight
        center = center * share
        out = jnp.zeros((WIDE, QUERY_BLOCK), jnp.float32)
        back = jnp.zeros((WIDE, QUERY_BLOCK), jnp.float32)
        low_keys = lax.broadcasted_iota(jnp.int32, (CHUNK, WIDE), 1) < LOW
        for part in chunks:
            probs = score[part, :] * share
            prob_low = probs.astype(jnp.bfloat16)
            grads = (probs * (slope[part, :] - center)).astype(jnp.bfloat16)
            out = out + jnp.dot(y_turned[:, part], prob_low, preferred_element_type=jnp.float32)
            back = back + jnp.dot(y_turned[:, part], grads, preferred_element_type=jnp.float32)
            for_values = jnp.dot(prob_low, x_block, preferred_element_type=jnp.float32)
            for_keys = jnp.dot(grads, x_block, preferred_element_type=jnp.float32)
            total[part, :] += jnp.where(low_keys, for_values, for_keys)
        low_rows = lax.broadcasted_iota(jnp.int32, out.shape, 0) < LOW
        turned = jnp.where(low_rows, out, back * key_scale).T
        oq_ref[rows] = turned.reshape(4, 64, WIDE).astype(oq_ref.dtype)
        return carry

    lax.fori_loop(0, x_ref.shape[0] // 4, block, 0)
    low_keys = lax.broadcasted_iota(jnp.int32, (CHUNK, WIDE), 1) < LOW
    for part in chunks:
        quarter, first = part.start // 1024, part.start % 1024 // 64
        grads = total[part, :]
        grads = jnp.where(low_keys, grads, grads * key_scale).astype(vk_ref.dtype)
        pieces = slice(first, first + CHUNK // 64)
        vk_ref[quarter // 2, quarter % 2, pieces] = grads.reshape(CHUNK // 64, 64, WIDE)


def back_kernel(
    x_ref, hidden_ref, stats_one_ref, stats_two_ref, gain_two_ref, bias_two_ref, norm_ref,
    gain_ref, bias_ref, g_ref, cot_ref, mix_from, q_from, k_from, v_from, o_from, conv_from,
    encoded_out, out_ref, sums_two_out, sums_one_out,
    mix, q_weight, k_weight, v_weight, o_weight, weight,
    hat_two, slope_two, trunk, row_hat, mixed, hat_one, slope_one, q_rows, k_rows, v_rows,
    a_rows, gq_rows, gv_rows, gk_rows,
    x_part, y_part, x_got, y_got, y_turned, score, slope, total_vk, oq, vk,
    oq_got, vk_got, from_core, to_z, from_z, summed,
    line_two, plane_two, line_one, plane_one, middle, padded, low, high,
    head_send, head_recv, sum_send, sum_recv, move_send, move_recv, own_sem
):
    heads = (head_send, head_recv)
    sums = (sum_send, sum_recv)
    moves = (move_send, move_recv)
    total_rows = ROWS * lax.axis_size("seq") * lax.axis_size("batch")
    kind = x_ref.dtype
    full = jnp.float32
    barrier, count = greet_all()
    count += greet_attention(barrier)
    loads = [
        pltpu.make_async_copy(source, target, own_sem.at[i])
        for i, (source, target) in enumerate(
            (
                (mix_from, mix),
                (q_from, q_weight),
                (k_from, k_weight),
                (v_from, v_weight),
                (o_from, o_weight),
                (conv_from, weight),
            )
        )
    ]
    for load in loads[:4]:
        load.start()
    mean_two = stats_two_ref[0:1, :] / total_rows
    scale_two = lax.rsqrt(stats_two_ref[1:2, :] / total_rows - mean_two * mean_two + EPS)
    hat = (hidden_ref[...] - mean_two) * scale_two
    pre = hat * gain_two_ref[...][None, :] + bias_two_ref[...][None, :]
    hat_two[...] = hat
    loads[0].wait()
    trunk[...] = (
        x_ref[...].astype(full)
        + jnp.dot(gelu_value(pre).astype(kind), mix[...], preferred_element_type=full)
    ).astype(kind)
    rows = trunk[...].astype(full)
    centered = rows - jnp.mean(rows, axis=-1, keepdims=True)
    row_scale = lax.rsqrt(jnp.mean(centered * centered, axis=-1, keepdims=True) + EPS)
    row_hat[...] = centered * row_scale
    norm_gain = norm_ref[...][None, :]
    normed = (row_hat[...] * norm_gain).astype(kind)
    for load, table, place in (
        (loads[3], v_weight, v_rows),
        (loads[2], k_weight, k_rows),
        (loads[1], q_weight, q_rows),
    ):
        load.wait()
        place[...] = jnp.dot(normed, table[...], preferred_element_type=full).astype(kind)
    pl.semaphore_wait(barrier, count)

    mean, scale = stats_one_ref[0:1, :], stats_one_ref[1:2, :]
    gain_one = gain_ref[...][None, :]

    def recall():
        for load in loads[4:]:
            load.start()

    def encode():
        loads[4].wait()
        encoded_out[...] = (
            trunk[...].astype(full) + jnp.dot(a_rows[...], o_weight[...], preferred_element_type=full)
        ).astype(kind)
        mixed[...] = lax.dot_general(gq_rows[...], q_weight[...], SIDE, preferred_element_type=full)
        slope_two[...] = gelu_slope(hat_two[...] * gain_two_ref[...][None, :] + bias_two_ref[...][None, :])

    spread_heads(q_rows, k_rows, v_rows, g_ref, x_got, y_got, x_part, y_part, heads, recall)
    attend_rows(x_got, y_got, oq, vk, y_turned, score, slope, total_vk)
    collect_heads(
        oq, vk, a_rows, gq_rows, gv_rows, gk_rows, oq_got, vk_got, from_core, to_z, from_z, summed,
        heads, encode
    )
    grad_normed = (
        mixed[...]
        + lax.dot_general(gk_rows[...], k_weight[...], SIDE, preferred_element_type=full)
        + lax.dot_general(gv_rows[...], v_weight[...], SIDE, preferred_element_type=full)
    )
    hats = row_hat[...]
    norm_part = jnp.sum(grad_normed * hats, axis=0, keepdims=True)
    grad_hat = grad_normed * norm_gain
    mixed[...] = cot_ref[...].astype(full) + row_scale * (
        grad_hat
        - jnp.mean(grad_hat, axis=-1, keepdims=True)
        - hats * jnp.mean(grad_hat * hats, axis=-1, keepdims=True)
    )
    grad_two = (
        lax.dot_general(mixed[...].astype(kind), mix[...], SIDE, preferred_element_type=full)
        * slope_two[...]
    )
    mid_width = grad_two.shape[1]
    place = line_place()
    line_two[place] = jnp.concatenate(
        [
            jnp.sum(grad_two, axis=0, keepdims=True),
            jnp.sum(grad_two * hat_two[...], axis=0, keepdims=True),
            norm_part[:, :mid_width],
            norm_part[:, mid_width:],
        ],
        axis=0,
    )
    started = line_send(line_two, sums, 0)
    hat_one[...] = (x_ref[...].astype(full) - mean) * scale
    plane_started = plane_send(line_two, plane_two, started, sums, 0)
    slope_one[...] = gelu_slope(hat_one[...] * gain_one + bias_ref[...][None, :])
    total = plane_sum(plane_two, plane_started)
    sums_two_out[...] = total
    hidden_grad = (
        gain_two_ref[...][None, :]
        * scale_two
        * (grad_two - total[0:1, :] / total_rows - hat_two[...] * total[1:2, :] / total_rows)
    ).astype(kind)
    for window in range(2):
        middle[window] = hidden_grad[window * 64 : window * 64 + 64, :]
        padded[window, 16:80, :] = hidden_grad[window * 64 : window * 64 + 64, :]
    halos = halo_send(middle, low, high, moves, 0)
    loads[5].wait()
    grad_act = None
    for tap, half, start, size in (TAP_PARTS[1], TAP_PARTS[2], TAP_PARTS[0], TAP_PARTS[3]):
        if tap == 0:
            halo_fill(padded, low, high, halos)
        first = 0 if half == 0 or tap == 2 else 384
        term = lax.dot_general(
            tap_rows(padded, 16 * (2 - tap))[:, first : first + size],
            weight[half, :, start : start + size],
            SIDE,
            preferred_element_type=jnp.float32,
        )
        grad_act = term if grad_act is None else grad_act + term
    grad_pre = grad_act * slope_one[...]
    line_one[place] = stacked([grad_pre, grad_pre * hat_one[...]])
    line_again = line_send(line_one, sums, LINE + PLANE)
    plane_again = plane_send(line_one, plane_one, line_again, sums, LINE + PLANE)
    total = plane_sum(plane_one, plane_again)
    sums_one_out[...] = total
    grad_rows = (
        gain_one
        * scale
        * (grad_pre - total[0:1, :] / total_rows - hat_one[...] * total[1:2, :] / total_rows)
    )
    out_ref[...] = (mixed[...] + grad_rows).astype(out_ref.dtype)
    for copy in started + plane_started + halos + line_again + plane_again:
        copy.wait_send()


def back(
    rows_in, hidden, stats_one, stats_two, gain_two, bias_two, norm_gain, gain_one, bias_one,
    grad_out, cot, mix_full, query_weight, key_weight, value_weight, out_weight, conv_full
):
    vmem = pl.BlockSpec(memory_space=pltpu.VMEM)
    anywhere = pl.BlockSpec(memory_space=pl.ANY)
    kind, full = rows_in.dtype, jnp.float32
    width, mid_width = rows_in.shape[1], hidden.shape[1]
    piece = (16, 64, WIDE)
    count = 4 * 16 * 64
    sems = 2 * (LINE + PLANE)
    weights = (mix_full, query_weight, key_weight, value_weight, out_weight, conv_full)
    scratch = [(table.shape, kind) for table in weights]
    scratch += [((ROWS, mid_width), full)] * 2 + [((ROWS, width), kind)] + [((ROWS, width), full)] * 4
    scratch += [((ROWS, H * KD), kind)] * 2 + [((ROWS, H * VD), kind)] * 2
    scratch += [((ROWS, H * KD), kind), ((ROWS, H * VD), kind), ((ROWS, H * KD), kind)]
    scratch += [(piece, kind)] * 3 + [((2, 2) + piece, kind), ((WIDE, count), kind)]
    scratch += [((count, QUERY_BLOCK), full)] * 2 + [((count, WIDE), full)]
    scratch += [(piece, kind), ((2, 2) + piece, kind), (piece, kind), (piece, kind)]
    scratch += [((2,) + piece, kind)] + [(piece, kind)] * 3
    scratch += [((LINE, 4, mid_width), full), ((PLANE, 4, mid_width), full)]
    scratch += [((LINE, 2, width), full), ((PLANE, 2, width), full)]
    scratch += [((2, 64, mid_width), kind), ((2, 96, mid_width), kind)] + [((2, 16, mid_width), kind)] * 2
    dma = pltpu.SemaphoreType.DMA
    return pl.pallas_call(
        back_kernel,
        out_shape=[
            jax.ShapeDtypeStruct((ROWS, width), kind),
            jax.ShapeDtypeStruct((ROWS, width), kind),
            jax.ShapeDtypeStruct((4, mid_width), full),
            jax.ShapeDtypeStruct((2, width), full),
        ],
        in_specs=[vmem] * 11 + [anywhere] * 6,
        out_specs=[vmem] * 4,
        scratch_shapes=[pltpu.VMEM(shape, held) for shape, held in scratch]
        + [dma((128,)), dma((128,)), dma((sems,)), dma((sems,)), dma((1, 2)), dma((1, 2)), dma((6,))],
        compiler_params=pltpu.CompilerParams(
            collective_id=2, has_side_effects=True, vmem_limit_bytes=62 * 1024 * 1024
        ),
        name="back",
    )(
        rows_in, hidden, stats_one, stats_two, gain_two, bias_two, norm_gain, gain_one, bias_one,
        grad_out, cot, *weights
    )


def finish_kernel(
    encoded_from, grad_from, two_ref, one_ref,
    encoded_to, grad_to, gain_one, bias_one, gain_two, bias_two, gain_norm
):
    encoded_to[...] = encoded_from[...]
    grad_to[...] = grad_from[...]
    mid_width = two_ref.shape[1]
    bias_one[...] = one_ref[0, :]
    gain_one[...] = one_ref[1, :]
    bias_two[...] = two_ref[0, :]
    gain_two[...] = two_ref[1, :]
    gain_norm[0:mid_width] = two_ref[2, :]
    gain_norm[mid_width : 2 * mid_width] = two_ref[3, :]


def finish(encoded, grad_inputs, sums_two, sums_one):
    vmem = pl.BlockSpec(memory_space=pltpu.VMEM)
    width, mid_width = sums_one.shape[1], sums_two.shape[1]
    full = jnp.float32
    return pl.pallas_call(
        finish_kernel,
        out_shape=[
            jax.ShapeDtypeStruct(encoded.shape, encoded.dtype),
            jax.ShapeDtypeStruct(grad_inputs.shape, grad_inputs.dtype),
            jax.ShapeDtypeStruct((width,), full),
            jax.ShapeDtypeStruct((width,), full),
            jax.ShapeDtypeStruct((mid_width,), full),
            jax.ShapeDtypeStruct((mid_width,), full),
            jax.ShapeDtypeStruct((2 * mid_width,), full),
        ],
        in_specs=[vmem] * 4,
        out_specs=[vmem] * 7,
        compiler_params=pltpu.CompilerParams(vmem_limit_bytes=62 * 1024 * 1024),
        name="finish",
    )(encoded, grad_inputs, sums_two, sums_one)


def on_device(
    inputs,
    conv_weight,
    mix_weight,
    first_gain,
    first_bias,
    second_gain,
    second_bias,
    norm_gain,
    query_weight,
    key_weight,
    value_weight,
    out_weight,
    cotangent,
):
    windows_here, local_bins, model_width = inputs.shape
    local_count = windows_here * local_bins
    rows_in = inputs.reshape(local_count, model_width)
    cot_flat = cotangent.reshape(local_count, model_width)
    conv_full, mix_full, hidden, stats_one, stats_two, grad_out = front(
        rows_in, conv_weight, mix_weight, first_gain, first_bias, cot_flat, out_weight
    )
    encoded_rows, grad_rows, sums_two, sums_one = back(
        rows_in,
        hidden,
        stats_one,
        stats_two,
        second_gain,
        second_bias,
        norm_gain,
        first_gain,
        first_bias,
        grad_out,
        cot_flat,
        mix_full,
        query_weight,
        key_weight,
        value_weight,
        out_weight,
        conv_full,
    )
    whole = (windows_here, local_bins, model_width)
    return finish(encoded_rows.reshape(whole), grad_rows.reshape(whole), sums_two, sums_one)


def solution(mesh):
    in_specs = (
        P("batch", "seq", None),
        P("seq", None),
        P("seq", None),
        P(),
        P(),
        P(),
        P(),
        P(),
        P(),
        P(),
        P(),
        P(),
        P("batch", "seq", None),
    )
    out_specs = (P("batch", "seq", None), P("batch", "seq", None), P(), P(), P(), P(), P())
    return jax.shard_map(
        on_device, mesh=mesh, in_specs=in_specs, out_specs=out_specs, check_vma=False
    )
```
